512 devices in a mesh: group: 64 (over x, y_lo, z), tensor: 8 (over y_hi, core).
Axes of the slice: x: 4, y: 8 (y_hi: 4, y_lo: 2; y = y_hi * 2 + y_lo), z: 8, core: 2. Of those that a mesh axis runs over, the one named last changes fastest.
Arguments:
- inputs: bfloat16 [4, 128, 8192], P(None, None, 'group'), may hold values from -160 to 160
- gain: float32 [8192], P('group'), may hold values from 0.1 to 1.9
- w_query: bfloat16 [8192, 8192], P('group', 'tensor'), may hold values from -0.0625 to 0.0625
- key_projection_weight: bfloat16 [8192, 1024], P('group', 'tensor'), may hold values from -0.0625 to 0.0625
- value_projection_weight: bfloat16 [8192, 1024], P('group', 'tensor'), may hold values from -0.0625 to 0.0625
- w_output: bfloat16 [8192, 8192], P('tensor', 'group'), may hold values from -0.0625 to 0.0625
- adapter_in: bfloat16 [8, 8192, 192], P(None, 'group'), may hold values from -0.0625 to 0.0625
- adapter_attn: bfloat16 [8, 8192, 64], P(None, 'tensor'), may hold values from -0.0625 to 0.0625
- adapter_out: bfloat16 [8, 64, 8192], P(None, None, 'group'), may hold values from -0.75 to 0.75
- pool_query: bfloat16 [64, 64, 8192], P('group', None, 'tensor'), may hold values from -0.75 to 0.75
- slot_keyvalue_matrices: bfloat16 [64, 64, 2, 1024], P('group', None, None, 'tensor'), may hold values from -0.75 to 0.75
- cache_keys: bfloat16 [128, 8, 1024, 128], P('group', 'tensor'), may hold values from -600 to 600
- value_cache: bfloat16 [128, 8, 1024, 128], P('group', 'tensor'), may hold values from -6 to 6
- tasks: int32 [128], replicated, may hold values from 0 to 7
- homes: int32 [8], replicated, may hold values from 0 to 63, as said below
- moves: int32 [16, 2], replicated, may hold values from 0 to 63, as said below
- lengths: int32 [128], P('group'), may hold values from 1 to 1024
Outputs:
- outputs: bfloat16 [4, 128, 8192], P(None, None, 'group')
The draws below stay inside these ranges and needn't reach their ends.
Inputs may be any that keep to these rules, and one draw needn't show every extreme that they name: `homes`: 8 different groups, one a home for each adapter. `moves`: column 0 an adapter (0 to 7), column 1 a destination group; no group is named twice.
All inputs are finite; a program needn't handle non-finite values.
Results may differ from the reference program's by a relative error of at most 0.0071.
Values may be sent and summed in bfloat16 or wider, within the bound.
No kernel may reach another device: no remote copies, remote signals or barrier semaphores. Data moves between devices by JAX's collectives and lax.ppermute only.
A program may use at most 64 MiB of HBM per device.

```python
import math
import jax
import jax.numpy as jnp
from jax import lax

MODEL_WIDTH = 8192
QUERY_HEADS = 64
KEY_VALUE_HEADS = 8
HEAD_SIZE = 128
ADAPTER_RANK = 64
TASKS = 8
CONTEXT_TOKENS = 1024
DECODE_STEPS = 4
ROW_GRP = 2
DECODE_ROWS = 128
NMOVE = 16
N_GROUP = 64


def draw_inputs(key, part):
    key = jax.random.fold_in(key, 11)
    drawn_key_projection, key_rows = jax.random.split(key, 2)
    column = jnp.arange(MODEL_WIDTH, dtype=jnp.float32) / (MODEL_WIDTH - 1)
    value_rows = jnp.clip(jax.random.normal(drawn_key_projection, (DECODE_STEPS, DECODE_ROWS, MODEL_WIDTH), jnp.float32), -5.0, 5.0)
    column_scale = 3.0 ** column
    row_scale = 10.0 ** (jax.random.uniform(key_rows, (DECODE_STEPS, DECODE_ROWS, 1), jnp.float32) - 0.5)
    return jnp.clip(value_rows * row_scale * column_scale[None, None, :], -160.0, 160.0).astype(jnp.bfloat16)


def draw_cache_keys(key, part):
    key = jax.random.fold_in(key, 23)
    drawn_key_projection = jax.random.fold_in(key, 0)
    value_rows = jax.random.normal(drawn_key_projection, (DECODE_ROWS, KEY_VALUE_HEADS, CONTEXT_TOKENS, HEAD_SIZE), jnp.float32)
    return jnp.clip(value_rows, -600.0, 600.0).astype(jnp.bfloat16)


def draw_lengths(key, part):
    key = jax.random.fold_in(key, 31)
    drawn_key_projection, key_spot, key_other = jax.random.split(key, 3)
    value_rows = jax.random.randint(drawn_key_projection, (DECODE_ROWS,), 1, CONTEXT_TOKENS + 1)
    spot_index = jax.random.randint(key_spot, (), 0, DECODE_ROWS)
    other_index = (spot_index + 1 + jax.random.randint(key_other, (), 0, DECODE_ROWS - 1)) % DECODE_ROWS
    token_positions = jnp.arange(DECODE_ROWS)
    value_rows = jnp.where(token_positions == spot_index, CONTEXT_TOKENS, value_rows)
    value_rows = jnp.where(token_positions == other_index, 1, value_rows)
    return value_rows.astype(jnp.int32)


def draw_homes(key, part):
    key = jax.random.fold_in(key, 41)
    key_middle, key_order = jax.random.split(key, 2)
    group_count = DECODE_ROWS // ROW_GRP
    middle = 1 + jax.random.permutation(key_middle, group_count - 2)[:TASKS - 2]
    value_rows = jnp.concatenate([jnp.array([0, group_count - 1], dtype=jnp.int32), middle.astype(jnp.int32)])
    return jax.random.permutation(key_order, value_rows).astype(jnp.int32)


def draw_moves(key, part):
    key = jax.random.fold_in(key, 53)
    key_middle, key_order, key_adapters = jax.random.split(key, 3)
    group_count = DECODE_ROWS // ROW_GRP
    middle = 1 + jax.random.permutation(key_middle, group_count - 2)[:NMOVE - 2]
    groups = jnp.concatenate([jnp.array([0, group_count - 1], dtype=jnp.int32), middle.astype(jnp.int32)])
    groups = jax.random.permutation(key_order, groups)
    adapters = jax.random.randint(key_adapters, (NMOVE,), 0, TASKS)
    adapters = adapters.at[0].set(0).at[1].set(TASKS - 1)
    return jnp.stack([adapters, groups], axis=1).astype(jnp.int32)


def plant(drawn, stream_key, least, largest):
    spot = [jax.random.randint(jax.random.fold_in(stream_key, axis), (), 0, length) for axis, length in enumerate(drawn.shape)]
    main_axis = drawn.shape.index(max(drawn.shape))
    beside = spot[:main_axis] + [(spot[main_axis] + 1) % drawn.shape[main_axis]] + spot[main_axis + 1:]
    return drawn.at[tuple(spot)].set(least).at[tuple(beside)].set(largest)


def block_scale(own_key, extent, shards, least, top_value):
    def one(dim, blocks):
        draws = jax.random.uniform(jax.random.fold_in(jax.random.fold_in(own_key, 6), dim), (blocks,), jnp.float32, least / len(shards), top_value / len(shards))
        return jnp.repeat(jnp.exp(draws), extent[dim] // blocks).reshape((-1,) + (1,) * (len(extent) - dim - 1))

    factor_of = one(*shards[0])
    for cut in shards[1:]:
        factor_of = factor_of * one(*cut)
    return factor_of


def gaussian(own_key, extent, spread, reach, shards=(), held_as=jnp.bfloat16):
    entries = spread * jax.random.normal(own_key, extent, jnp.float32)
    if shards:
        entries = entries * block_scale(own_key, extent, shards, -0.22, 0.18)
    return jnp.clip(entries, -reach, reach).astype(held_as)


def setup_inputs(seed: int = 0) -> dict:
    arg_keys = jax.random.split(jax.random.key(seed), 18)
    return {
        "inputs": draw_inputs(jax.random.fold_in(arg_keys[17], 71), 0),
        "gain": jnp.clip(1.0 + 0.18 * jax.random.normal(arg_keys[1], (MODEL_WIDTH,), jnp.float32), 0.1, 1.9),
        "w_query": gaussian(arg_keys[2], (MODEL_WIDTH, QUERY_HEADS * HEAD_SIZE), MODEL_WIDTH ** -0.5, 0.0625, ((0, 64), (1, 8))),
        "key_projection_weight": gaussian(arg_keys[3], (MODEL_WIDTH, KEY_VALUE_HEADS * HEAD_SIZE), MODEL_WIDTH ** -0.5, 0.0625, ((0, 64), (1, 8))),
        "value_projection_weight": gaussian(arg_keys[4], (MODEL_WIDTH, KEY_VALUE_HEADS * HEAD_SIZE), MODEL_WIDTH ** -0.5, 0.0625, ((0, 64), (1, 8))),
        "w_output": gaussian(arg_keys[5], (QUERY_HEADS * HEAD_SIZE, MODEL_WIDTH), (QUERY_HEADS * HEAD_SIZE) ** -0.5, 0.0625, ((0, 8), (1, 64))),
        "adapter_in": gaussian(arg_keys[6], (TASKS, MODEL_WIDTH, 3 * ADAPTER_RANK), MODEL_WIDTH ** -0.5, 0.0625, ((1, 64),)),
        "adapter_attn": gaussian(arg_keys[7], (TASKS, QUERY_HEADS * HEAD_SIZE, ADAPTER_RANK), (QUERY_HEADS * HEAD_SIZE) ** -0.5, 0.0625, ((1, 8),)),
        "adapter_out": gaussian(arg_keys[8], (TASKS, ADAPTER_RANK, MODEL_WIDTH), ADAPTER_RANK ** -0.5, 0.75, ((2, 64),)),
        "pool_query": gaussian(arg_keys[9], (N_GROUP, ADAPTER_RANK, QUERY_HEADS * HEAD_SIZE), ADAPTER_RANK ** -0.5, 0.75, ((0, 64), (2, 8))),
        "slot_keyvalue_matrices": gaussian(arg_keys[10], (N_GROUP, ADAPTER_RANK, 2, KEY_VALUE_HEADS * HEAD_SIZE), ADAPTER_RANK ** -0.5, 0.75, ((0, 64), (3, 8))),
        "cache_keys": draw_cache_keys(jax.random.fold_in(arg_keys[17], 71), 0),
        "value_cache": gaussian(arg_keys[12], (DECODE_ROWS, KEY_VALUE_HEADS, CONTEXT_TOKENS, HEAD_SIZE), 1.0, 6.0, ((0, 64), (1, 8))),
        "tasks": plant(jax.random.randint(arg_keys[13], (DECODE_ROWS,), 0, TASKS), jax.random.fold_in(arg_keys[13], 1), 0, TASKS - 1).astype(jnp.int32),
        "homes": draw_homes(jax.random.fold_in(arg_keys[17], 71), 0),
        "moves": draw_moves(jax.random.fold_in(arg_keys[17], 71), 0),
        "lengths": draw_lengths(jax.random.fold_in(arg_keys[17], 71), 0),
    }


epsilon = 1e-05

def apply_rotary(vectors, token_positions):
    half_width = vectors.shape[-1] // 2
    frequency = jnp.exp(-jnp.log(500000.0) * jnp.arange(half_width, dtype=jnp.float32) * (2.0 / vectors.shape[-1]))
    angles = token_positions.astype(jnp.float32)[:, None] * frequency[None, :]
    cosine = jnp.cos(angles)[:, None, :]
    sine_part = jnp.sin(angles)[:, None, :]
    leading = vectors[..., :half_width]
    trailing = vectors[..., half_width:]
    return jnp.concatenate([leading * cosine - trailing * sine_part, leading * sine_part + trailing * cosine], axis=-1)

def pick_tasks(tasks, moves, decode_step, per_group, step_total):
    if decode_step < step_total // 2:
        return tasks
    owners = jnp.arange(tasks.shape[0], dtype=jnp.int32) // per_group
    matched = moves[:, 1][None, :] == owners[:, None]
    moved = jnp.any(matched, axis=1)
    chosen = lax.optimization_barrier(jnp.sum(jnp.where(matched, moves[:, 0][None, :], 0), axis=1)).astype(jnp.int32)
    return jnp.where(moved, chosen, tasks)

def expand(marks, rows):
    return (marks[:, :, None] * rows[:, None, :]).reshape(rows.shape[0], marks.shape[1] * rows.shape[1])

def attend_row(operands, decode_step, scaling):
    grouped_queries, keys_row, values_row, fresh_keys, fresh_values, length = operands
    query_vectors = grouped_queries.astype(jnp.float32)
    old_scores = jnp.einsum('kgd,kjd->kgj', query_vectors, keys_row.astype(jnp.float32)) * scaling
    new_scores = jnp.einsum('kgd,kjd->kgj', query_vectors, fresh_keys.astype(jnp.float32)) * scaling
    old_scores = jnp.where(jnp.arange(keys_row.shape[1])[None, None, :] < length, old_scores, -1e+30)
    new_scores = jnp.where(jnp.arange(fresh_keys.shape[1])[None, None, :] <= decode_step, new_scores, -1e+30)
    highest = jnp.maximum(lax.optimization_barrier(jnp.max(old_scores, axis=-1)), lax.optimization_barrier(jnp.max(new_scores, axis=-1)))[..., None]
    old_exp = jnp.exp(old_scores - highest)
    new_exp = jnp.exp(new_scores - highest)
    denominator = lax.optimization_barrier(jnp.sum(old_exp, axis=-1, keepdims=True)) + lax.optimization_barrier(jnp.sum(new_exp, axis=-1, keepdims=True))
    old_weights = (old_exp / denominator).astype(jnp.bfloat16)
    new_weights = (new_exp / denominator).astype(jnp.bfloat16)
    mixed = jnp.einsum('kgj,kjd->kgd', old_weights.astype(jnp.float32), values_row.astype(jnp.float32))
    mixed = mixed + jnp.einsum('kgj,kjd->kgd', new_weights.astype(jnp.float32), fresh_values.astype(jnp.float32))
    return mixed.astype(jnp.bfloat16).reshape(-1)

def reference(inputs, gain, w_query, key_projection_weight, value_projection_weight, w_output, adapter_in, adapter_attn, adapter_out, pool_query, slot_keyvalue_matrices, cache_keys, value_cache, tasks, homes, moves, lengths):
    query_width = QUERY_HEADS * HEAD_SIZE
    key_total_width = KEY_VALUE_HEADS * HEAD_SIZE
    b_query = jnp.take(pool_query, homes, axis=0).reshape(TASKS * ADAPTER_RANK, query_width)
    b_keyval = jnp.take(slot_keyvalue_matrices, homes, axis=0)
    b_key = b_keyval[:, :, 0, :].reshape(TASKS * ADAPTER_RANK, key_total_width)
    b_value = b_keyval[:, :, 1, :].reshape(TASKS * ADAPTER_RANK, key_total_width)
    out_flat = adapter_out.reshape(TASKS * ADAPTER_RANK, MODEL_WIDTH)
    labels = jnp.arange(TASKS, dtype=jnp.int32)
    appended_keys = jnp.zeros((DECODE_ROWS, KEY_VALUE_HEADS, DECODE_STEPS, HEAD_SIZE), jnp.bfloat16)
    appended_values = jnp.zeros((DECODE_ROWS, KEY_VALUE_HEADS, DECODE_STEPS, HEAD_SIZE), jnp.bfloat16)
    scaling = 1.0 / math.sqrt(HEAD_SIZE)
    results = []
    for decode_step in range(DECODE_STEPS):
        active = pick_tasks(tasks, moves, decode_step, ROW_GRP, DECODE_STEPS)
        marks = (active[:, None] == labels[None, :]).astype(jnp.float32)
        marks_low = marks.astype(jnp.bfloat16)
        states = inputs[decode_step].astype(jnp.float32)
        inverse = lax.rsqrt(lax.optimization_barrier(jnp.mean(states * states, axis=1)) + epsilon)
        gained = (states * gain[None, :]).astype(jnp.bfloat16)
        basic_query = jnp.dot(gained, w_query, preferred_element_type=jnp.float32)
        basic_key = jnp.dot(gained, key_projection_weight, preferred_element_type=jnp.float32)
        basic_value = jnp.dot(gained, value_projection_weight, preferred_element_type=jnp.float32)
        every_low = jnp.einsum('rd,tdc->rtc', gained.astype(jnp.float32), adapter_in.astype(jnp.float32))
        lowrank = (inverse[:, None] * jnp.einsum('rt,rtc->rc', marks, every_low)).astype(jnp.bfloat16)
        raw_query = inverse[:, None] * basic_query + jnp.dot(expand(marks_low, lowrank[:, :ADAPTER_RANK]), b_query, preferred_element_type=jnp.float32)
        unrotated_key = inverse[:, None] * basic_key + jnp.dot(expand(marks_low, lowrank[:, ADAPTER_RANK:2 * ADAPTER_RANK]), b_key, preferred_element_type=jnp.float32)
        projected_value = inverse[:, None] * basic_value + jnp.dot(expand(marks_low, lowrank[:, 2 * ADAPTER_RANK:]), b_value, preferred_element_type=jnp.float32)
        token_positions = lengths + decode_step
        query_vectors = apply_rotary(raw_query.reshape(DECODE_ROWS, QUERY_HEADS, HEAD_SIZE), token_positions).astype(jnp.bfloat16)
        current_keys = apply_rotary(unrotated_key.reshape(DECODE_ROWS, KEY_VALUE_HEADS, HEAD_SIZE), token_positions).astype(jnp.bfloat16)
        current_values = projected_value.reshape(DECODE_ROWS, KEY_VALUE_HEADS, HEAD_SIZE).astype(jnp.bfloat16)
        appended_keys = appended_keys.at[:, :, decode_step, :].set(current_keys)
        appended_values = appended_values.at[:, :, decode_step, :].set(current_values)
        grouped_queries = query_vectors.reshape(DECODE_ROWS, KEY_VALUE_HEADS, QUERY_HEADS // KEY_VALUE_HEADS, HEAD_SIZE)
        attended = lax.map(lambda operands: attend_row(operands, decode_step, scaling), (grouped_queries, cache_keys, value_cache, appended_keys, appended_values, lengths))
        every_reduced = jnp.einsum('rq,tqc->rtc', attended.astype(jnp.float32), adapter_attn.astype(jnp.float32))
        reduced = jnp.einsum('rt,rtc->rc', marks, every_reduced).astype(jnp.bfloat16)
        projected = jnp.dot(attended, w_output, preferred_element_type=jnp.float32)
        adapted = jnp.dot(expand(marks_low, reduced), out_flat, preferred_element_type=jnp.float32)
        results.append((states + projected + adapted).astype(jnp.bfloat16))
    return jnp.stack(results, axis=0)
```

```python
import math

import jax
import jax.numpy as jnp
from jax import lax
from jax.sharding import Mesh
from jax.sharding import PartitionSpec as P

epsilon = 1e-05
GROUP = ("x", "y_lo", "z")
PLANE = ("x", "y_lo")
TENSOR = ("y_hi", "core")
PADDED_WIDTH = 256


def exchange(blocks, axes):
    return lax.all_to_all(blocks, axes, 0, 0, tiled=True)


def apply_rotary(vectors, token_positions):
    half_width = vectors.shape[-1] // 2
    frequency = jnp.exp(
        -jnp.log(500000.0) * jnp.arange(half_width, dtype=jnp.float32) * (2.0 / vectors.shape[-1])
    )
    angles = token_positions.astype(jnp.float32)[:, None] * frequency[None, :]
    cosine = jnp.cos(angles)[:, None, :]
    sine_part = jnp.sin(angles)[:, None, :]
    leading = vectors[..., :half_width]
    trailing = vectors[..., half_width:]
    return jnp.concatenate(
        [leading * cosine - trailing * sine_part, leading * sine_part + trailing * cosine], axis=-1
    )


def dot(left, right):
    return jnp.dot(left, right, preferred_element_type=jnp.float32)


def attend(queries, cache_keys, value_cache, fresh_keys, fresh_values, lengths, query_steps):
    scaling = 1.0 / math.sqrt(queries.shape[-1])
    old_scores = (
        jnp.einsum("rnd,rjd->rnj", queries, cache_keys, preferred_element_type=jnp.float32)
        * scaling
    )
    new_scores = (
        jnp.einsum("rnd,rjd->rnj", queries, fresh_keys, preferred_element_type=jnp.float32)
        * scaling
    )
    visible = jnp.arange(cache_keys.shape[1])[None, None, :] < lengths[:, None, None]
    old_scores = jnp.where(visible, old_scores, -1e30)
    fresh = jnp.arange(fresh_keys.shape[1])[None, None, :] <= query_steps[None, :, None]
    new_scores = jnp.where(fresh, new_scores, -1e30)
    highest = jnp.maximum(jnp.max(old_scores, axis=-1), jnp.max(new_scores, axis=-1))[..., None]
    old_exp = jnp.exp(old_scores - highest)
    new_exp = jnp.exp(new_scores - highest)
    denominator = jnp.sum(old_exp, axis=-1, keepdims=True) + jnp.sum(
        new_exp, axis=-1, keepdims=True
    )
    old_weights = (old_exp / denominator).astype(jnp.bfloat16)
    new_weights = (new_exp / denominator).astype(jnp.bfloat16)
    mixed = jnp.einsum(
        "rnj,rjd->rnd", old_weights, value_cache, preferred_element_type=jnp.float32
    )
    mixed = mixed + jnp.einsum(
        "rnj,rjd->rnd", new_weights, fresh_values, preferred_element_type=jnp.float32
    )
    return mixed.astype(jnp.bfloat16)


def on_device(
    inputs,
    gain,
    w_query,
    key_projection_weight,
    value_projection_weight,
    w_output,
    adapter_in,
    adapter_attn,
    adapter_out,
    pool_query,
    slot_keyvalue_matrices,
    cache_keys,
    value_cache,
    tasks,
    homes,
    moves,
    lengths,
):
    steps, all_rows, width_part = inputs.shape
    own_rows = lengths.shape[0]
    groups = all_rows // own_rows
    planes = lax.axis_size(PLANE)
    depth = lax.axis_size("z")
    task_count = homes.shape[0]
    rank = adapter_out.shape[1]
    head_dim = cache_keys.shape[3]
    query_width = w_query.shape[1]
    heads = query_width // head_dim
    key_end = query_width + head_dim
    base_end = key_end + head_dim
    per_group = steps * own_rows
    every_row = groups * per_group
    model_width = width_part * groups
    me = lax.axis_index(GROUP)

    group_tasks = tasks.reshape(groups, own_rows)
    matched = moves[:, 1][None, :] == jnp.arange(groups, dtype=jnp.int32)[:, None]
    moved = jnp.any(matched, axis=1)
    chosen = jnp.sum(jnp.where(matched, moves[:, 0][None, :], 0), axis=1)
    needed = jnp.concatenate([group_tasks, chosen[:, None]], axis=1)
    slots = own_rows + 1
    late = jnp.where(moved[:, None], chosen[:, None], group_tasks)
    active = jnp.stack([group_tasks if s < steps // 2 else late for s in range(steps)], axis=1)
    active = active.reshape(every_row)
    marks = active[:, None] == jnp.arange(task_count, dtype=jnp.int32)[None, :]

    up = jnp.concatenate(
        [
            pool_query.reshape(rank, query_width),
            slot_keyvalue_matrices.reshape(rank, 2 * head_dim),
        ],
        axis=1,
    )
    with jax.named_scope("up_rows"):
        up_rows = exchange(up, GROUP)
    sources = jnp.sum(
        jnp.where(
            needed.reshape(-1)[:, None] == jnp.arange(task_count, dtype=jnp.int32)[None, :],
            homes[None, :],
            0,
        ),
        axis=1,
    )
    pick = (sources[:, None] == jnp.arange(groups, dtype=jnp.int32)[None, :]).astype(jnp.bfloat16)
    chosen_rows = dot(pick, up_rows).astype(jnp.bfloat16)
    with jax.named_scope("up_needed"):
        up_needed = exchange(chosen_rows.reshape(groups, slots * base_end), GROUP)

    residual = (
        inputs.reshape(steps, groups, own_rows, width_part)
        .transpose(1, 0, 2, 3)
        .reshape(every_row, width_part)
    )
    states = residual.astype(jnp.float32)
    gained = (states * gain[None, :]).astype(jnp.bfloat16)
    squares = jnp.sum(states * states, axis=1, keepdims=True)
    squares_high = lax.reduce_precision(squares, 8, 7)
    spread = jnp.where(marks[:, :, None], gained[:, None, :], 0).reshape(
        every_row, task_count * width_part
    )
    partial = jnp.concatenate(
        [
            dot(gained, w_query),
            dot(gained, key_projection_weight),
            dot(gained, value_projection_weight),
            dot(spread, adapter_in.reshape(task_count * width_part, 3 * rank)),
            squares_high,
            squares - squares_high,
            jnp.zeros((every_row, PADDED_WIDTH - 3 * rank - 2), jnp.float32),
        ],
        axis=1,
    ).astype(jnp.bfloat16)
    with jax.named_scope("sum_plane"):
        by_plane = exchange(partial.reshape(planes, depth * per_group, -1), PLANE)
    plane_sum = jnp.sum(by_plane.astype(jnp.float32), axis=0).astype(jnp.bfloat16)
    with jax.named_scope("sum_z"):
        by_depth = exchange(plane_sum.reshape(depth, per_group, -1), "z")
    own = jnp.sum(by_depth.astype(jnp.float32), axis=0)

    low_end = base_end + 3 * rank
    inverse = lax.rsqrt((own[:, low_end] + own[:, low_end + 1]) / model_width + epsilon)[:, None]
    lowrank = (inverse * own[:, base_end:low_end]).astype(jnp.bfloat16)
    own_moved = lax.dynamic_index_in_dim(moved, me, 0, keepdims=False)
    row_step = jnp.arange(per_group) // own_rows
    row_slot = jnp.where(
        jnp.logical_and(row_step >= steps // 2, own_moved),
        own_rows,
        jnp.arange(per_group) % own_rows,
    )[:, None]

    def lift(block, first, last):
        total = jnp.zeros((per_group, last - first), jnp.float32)
        for slot in range(slots):
            matrix = up_needed[:, slot * base_end + first : slot * base_end + last]
            lifted = dot(lowrank[:, block * rank : (block + 1) * rank], matrix)
            total = jnp.where(row_slot == slot, lifted, total)
        return total

    raw_query = inverse * own[:, :query_width] + lift(0, 0, query_width)
    raw_key = inverse * own[:, query_width:key_end] + lift(1, query_width, key_end)
    raw_value = inverse * own[:, key_end:base_end] + lift(2, key_end, base_end)
    positions = jnp.tile(lengths, steps) + row_step
    queries = apply_rotary(raw_query.reshape(per_group, heads, head_dim), positions)
    new_keys = apply_rotary(raw_key.reshape(per_group, 1, head_dim), positions)

    def by_row(array):
        return (
            array.astype(jnp.bfloat16)
            .reshape(steps, own_rows, -1, head_dim)
            .transpose(1, 0, 2, 3)
            .reshape(own_rows, -1, head_dim)
        )

    attended = attend(
        by_row(queries),
        cache_keys.reshape(own_rows, -1, head_dim),
        value_cache.reshape(own_rows, -1, head_dim),
        by_row(new_keys),
        by_row(raw_value),
        lengths,
        jnp.arange(steps * heads) // heads,
    )
    attended = (
        attended.reshape(own_rows, steps, query_width)
        .transpose(1, 0, 2)
        .reshape(per_group, query_width)
    )

    with jax.named_scope("gather_z"):
        line = exchange(
            jnp.broadcast_to(attended[None], (depth, per_group, query_width)), "z"
        ).reshape(depth * per_group, query_width)
    with jax.named_scope("gather_plane"):
        piece_rows = exchange(
            jnp.broadcast_to(line[None], (planes, depth * per_group, query_width)), PLANE
        ).reshape(every_row, query_width)

    every_reduced = jnp.einsum(
        "rq,tqc->rtc", piece_rows, adapter_attn, preferred_element_type=jnp.float32
    )
    reduced = jnp.where(marks[:, :, None], every_reduced, 0).astype(jnp.bfloat16)
    mixed = dot(piece_rows, w_output) + dot(
        reduced.reshape(every_row, task_count * rank),
        adapter_out.reshape(task_count * rank, width_part),
    )
    mixed = mixed.astype(jnp.bfloat16)
    half = every_row // 2
    core = lax.axis_index("core")
    with jax.named_scope("sum_core"):
        pair = lax.all_gather(mixed, "core", axis=0)
    mine = lax.dynamic_slice_in_dim(pair, core * half, half, 1).astype(jnp.float32)
    mine = mine[0] + mine[1]
    for hop in (1, 2):
        with jax.named_scope("sum_y_hi"):
            ways = [(i, i ^ hop) for i in range(lax.axis_size("y_hi"))]
            mine = lax.reduce_precision(mine, 8, 7)
            mine = mine + lax.ppermute(mine.astype(jnp.bfloat16), "y_hi", ways).astype(jnp.float32)
    finished = lax.dynamic_slice_in_dim(states, core * half, half, 0) + mine
    with jax.named_scope("gather_core"):
        finished = lax.all_gather(finished.astype(jnp.bfloat16), "core", axis=0, tiled=True)
    return (
        finished.reshape(groups, steps, own_rows, width_part)
        .transpose(1, 0, 2, 3)
        .reshape(steps, all_rows, width_part)
    )


def solution(mesh):
    parts = Mesh(mesh.devices.reshape(4, 2, 8, 4, 2), GROUP + TENSOR)
    return jax.shard_map(
        on_device,
        mesh=parts,
        in_specs=(
            P(None, None, GROUP),
            P(GROUP),
            P(GROUP, TENSOR),
            P(GROUP, TENSOR),
            P(GROUP, TENSOR),
            P(TENSOR, GROUP),
            P(None, GROUP, None),
            P(None, TENSOR, None),
            P(None, None, GROUP),
            P(GROUP, None, TENSOR),
            P(GROUP, None, None, TENSOR),
            P(GROUP, TENSOR, None, None),
            P(GROUP, TENSOR, None, None),
            P(),
            P(),
            P(),
            P(GROUP),
        ),
        out_specs=P(None, None, GROUP),
        check_vma=False,
    )
```

```python
import math

import jax
import jax.numpy as jnp
from jax import lax
from jax.sharding import Mesh
from jax.sharding import PartitionSpec as P

epsilon = 1e-05
GROUP = ("x", "y_lo", "z")
PLANE = ("x", "y_lo")
TENSOR = ("y_hi", "core")
PADDED_WIDTH = 256


def exchange(blocks, axes):
    return lax.all_to_all(blocks, axes, 0, 0, tiled=True)


def apply_rotary(vectors, token_positions):
    half_width = vectors.shape[-1] // 2
    frequency = jnp.exp(
        -jnp.log(500000.0) * jnp.arange(half_width, dtype=jnp.float32) * (2.0 / vectors.shape[-1])
    )
    angles = token_positions.astype(jnp.float32)[:, None] * frequency[None, :]
    cosine = jnp.cos(angles)[:, None, :]
    sine_part = jnp.sin(angles)[:, None, :]
    leading = vectors[..., :half_width]
    trailing = vectors[..., half_width:]
    return jnp.concatenate(
        [leading * cosine - trailing * sine_part, leading * sine_part + trailing * cosine], axis=-1
    )


def dot(left, right):
    return jnp.dot(left, right, preferred_element_type=jnp.float32)


def attend(queries, cache_keys, value_cache, fresh_keys, fresh_values, lengths, query_steps):
    scaling = 1.0 / math.sqrt(queries.shape[-1])
    old_scores = (
        jnp.einsum("rnd,rjd->rnj", queries, cache_keys, preferred_element_type=jnp.float32)
        * scaling
    )
    new_scores = (
        jnp.einsum("rnd,rjd->rnj", queries, fresh_keys, preferred_element_type=jnp.float32)
        * scaling
    )
    visible = jnp.arange(cache_keys.shape[1])[None, None, :] < lengths[:, None, None]
    old_scores = jnp.where(visible, old_scores, -1e30)
    fresh = jnp.arange(fresh_keys.shape[1])[None, None, :] <= query_steps[None, :, None]
    new_scores = jnp.where(fresh, new_scores, -1e30)
    highest = jnp.maximum(jnp.max(old_scores, axis=-1), jnp.max(new_scores, axis=-1))[..., None]
    old_exp = jnp.exp(old_scores - highest)
    new_exp = jnp.exp(new_scores - highest)
    denominator = jnp.sum(old_exp, axis=-1, keepdims=True) + jnp.sum(
        new_exp, axis=-1, keepdims=True
    )
    old_weights = (old_exp / denominator).astype(jnp.bfloat16)
    new_weights = (new_exp / denominator).astype(jnp.bfloat16)
    mixed = jnp.einsum(
        "rnj,rjd->rnd", old_weights, value_cache, preferred_element_type=jnp.float32
    )
    mixed = mixed + jnp.einsum(
        "rnj,rjd->rnd", new_weights, fresh_values, preferred_element_type=jnp.float32
    )
    return mixed.astype(jnp.bfloat16)


def on_device(
    inputs,
    gain,
    w_query,
    key_projection_weight,
    value_projection_weight,
    w_output,
    adapter_in,
    adapter_attn,
    adapter_out,
    pool_query,
    slot_keyvalue_matrices,
    cache_keys,
    value_cache,
    tasks,
    homes,
    moves,
    lengths,
):
    steps, all_rows, width_part = inputs.shape
    own_rows = lengths.shape[0]
    groups = all_rows // own_rows
    planes = lax.axis_size(PLANE)
    depth = lax.axis_size("z")
    task_count = homes.shape[0]
    rank = adapter_out.shape[1]
    head_dim = cache_keys.shape[3]
    query_width = w_query.shape[1]
    heads = query_width // head_dim
    key_end = query_width + head_dim
    base_end = key_end + head_dim
    per_group = steps * own_rows
    every_row = groups * per_group
    model_width = width_part * groups
    line = lax.axis_size("x")
    column_rows = depth * per_group

    group_tasks = tasks.reshape(groups, own_rows)
    matched = moves[:, 1][None, :] == jnp.arange(groups, dtype=jnp.int32)[:, None]
    moved = jnp.any(matched, axis=1)
    chosen = jnp.sum(jnp.where(matched, moves[:, 0][None, :], 0), axis=1)
    late = jnp.where(moved[:, None], chosen[:, None], group_tasks)
    active = jnp.stack([group_tasks if s < steps // 2 else late for s in range(steps)], axis=1)
    active = active.reshape(every_row)
    marks = active[:, None] == jnp.arange(task_count, dtype=jnp.int32)[None, :]
    row_home = jnp.sum(jnp.where(marks, homes[None, :], 0), axis=1)

    up = jnp.concatenate(
        [
            pool_query.reshape(rank, query_width),
            slot_keyvalue_matrices.reshape(rank, 2 * head_dim),
        ],
        axis=1,
    )
    with jax.named_scope("up_x"):
        up_line = exchange(jnp.broadcast_to(up[None], (line, rank, base_end)), "x")

    residual = (
        inputs.reshape(steps, groups, own_rows, width_part)
        .transpose(1, 0, 2, 3)
        .reshape(every_row, width_part)
    )
    states = residual.astype(jnp.float32)
    gained = (states * gain[None, :]).astype(jnp.bfloat16)
    squares = jnp.sum(states * states, axis=1, keepdims=True)
    squares_high = lax.reduce_precision(squares, 8, 7)
    spread = jnp.where(marks[:, :, None], gained[:, None, :], 0).reshape(
        every_row, task_count * width_part
    )
    partial = jnp.concatenate(
        [
            dot(gained, w_query),
            dot(gained, key_projection_weight),
            dot(gained, value_projection_weight),
            dot(spread, adapter_in.reshape(task_count * width_part, 3 * rank)),
            squares_high,
            squares - squares_high,
            jnp.zeros((every_row, PADDED_WIDTH - 3 * rank - 2), jnp.float32),
        ],
        axis=1,
    ).astype(jnp.bfloat16)
    with jax.named_scope("sum_plane"):
        by_plane = exchange(partial.reshape(planes, column_rows, -1), PLANE)

    up_line, by_plane = lax.optimization_barrier((up_line, by_plane))
    with jax.named_scope("up_y_lo"):
        up_other = lax.ppermute(up_line, "y_lo", [(0, 1), (1, 0)])
    plane_sum = jnp.sum(by_plane.astype(jnp.float32), axis=0)

    low_end = 3 * rank
    low_part = plane_sum[:, base_end:]
    squares = low_part[:, low_end : low_end + 1] + low_part[:, low_end + 1 : low_end + 2]
    squares_high = lax.reduce_precision(squares, 8, 7)
    low_part = jnp.concatenate(
        [
            low_part[:, :low_end],
            squares_high,
            squares - squares_high,
            low_part[:, low_end + 2 :],
        ],
        axis=1,
    ).astype(jnp.bfloat16)
    with jax.named_scope("sum_low"):
        low_sum = exchange(
            jnp.broadcast_to(low_part[None], (depth, column_rows, PADDED_WIDTH)), "z"
        )
    low_sum = jnp.sum(low_sum.astype(jnp.float32), axis=0)
    inverse = lax.rsqrt(
        (low_sum[:, low_end : low_end + 1] + low_sum[:, low_end + 1 : low_end + 2]) / model_width
        + epsilon
    )
    lowrank = (inverse * low_sum[:, :low_end]).astype(jnp.bfloat16)

    x, y_lo, z = (lax.axis_index(name) for name in GROUP)
    column_home = lax.dynamic_slice_in_dim(
        row_home, (x * 2 + y_lo) * column_rows, column_rows, 0
    )

    def lift(block, first, last):
        total = jnp.zeros((column_rows, last - first), jnp.float32)
        rows = lowrank[:, block * rank : (block + 1) * rank]
        for matrices, half in ((up_line, y_lo), (up_other, 1 - y_lo)):
            slots = (jnp.arange(line) * 2 + half) * depth + z
            use = column_home[:, None] == slots[None, :]
            spread = jnp.where(use[:, :, None], rows[:, None, :], 0).reshape(
                column_rows, line * rank
            )
            total = total + dot(
                spread, matrices[:, :, first:last].reshape(line * rank, last - first)
            )
        return total

    lifted = jnp.concatenate(
        [lift(0, 0, query_width), lift(1, query_width, key_end), lift(2, key_end, base_end)],
        axis=1,
    )
    raw_part = (inverse * plane_sum[:, :base_end] + lifted).astype(jnp.bfloat16)
    with jax.named_scope("sum_z"):
        by_depth = exchange(raw_part.reshape(depth, per_group, base_end), "z")
    raw = jnp.sum(by_depth.astype(jnp.float32), axis=0)

    row_step = jnp.arange(per_group) // own_rows
    positions = jnp.tile(lengths, steps) + row_step
    queries = apply_rotary(raw[:, :query_width].reshape(per_group, heads, head_dim), positions)
    new_keys = apply_rotary(
        raw[:, query_width:key_end].reshape(per_group, 1, head_dim), positions
    )
    raw_value = raw[:, key_end:]

    def by_row(array):
        return (
            array.astype(jnp.bfloat16)
            .reshape(steps, own_rows, -1, head_dim)
            .transpose(1, 0, 2, 3)
            .reshape(own_rows, -1, head_dim)
        )

    attended = attend(
        by_row(queries),
        cache_keys.reshape(own_rows, -1, head_dim),
        value_cache.reshape(own_rows, -1, head_dim),
        by_row(new_keys),
        by_row(raw_value),
        lengths,
        jnp.arange(steps * heads) // heads,
    )
    attended = (
        attended.reshape(own_rows, steps, query_width)
        .transpose(1, 0, 2)
        .reshape(per_group, query_width)
    )

    with jax.named_scope("gather_z"):
        line = exchange(
            jnp.broadcast_to(attended[None], (depth, per_group, query_width)), "z"
        ).reshape(depth * per_group, query_width)
    with jax.named_scope("gather_plane"):
        piece_rows = exchange(
            jnp.broadcast_to(line[None], (planes, depth * per_group, query_width)), PLANE
        ).reshape(every_row, query_width)

    every_reduced = jnp.einsum(
        "rq,tqc->rtc", piece_rows, adapter_attn, preferred_element_type=jnp.float32
    )
    reduced = jnp.where(marks[:, :, None], every_reduced, 0).astype(jnp.bfloat16)
    mixed = dot(piece_rows, w_output) + dot(
        reduced.reshape(every_row, task_count * rank),
        adapter_out.reshape(task_count * rank, width_part),
    )
    mixed = mixed.astype(jnp.bfloat16)
    half = every_row // 2
    core = lax.axis_index("core")
    with jax.named_scope("sum_core"):
        pair = lax.all_gather(mixed, "core", axis=0)
    mine = lax.dynamic_slice_in_dim(pair, core * half, half, 1).astype(jnp.float32)
    mine = (mine[0] + mine[1]).astype(jnp.bfloat16)
    with jax.named_scope("sum_y_hi"):
        mine = exchange(
            jnp.broadcast_to(mine[None], (lax.axis_size("y_hi"), half, width_part)), "y_hi"
        )
    mine = jnp.sum(mine.astype(jnp.float32), axis=0)
    finished = lax.dynamic_slice_in_dim(states, core * half, half, 0) + mine
    with jax.named_scope("gather_core"):
        finished = lax.all_gather(finished.astype(jnp.bfloat16), "core", axis=0, tiled=True)
    return (
        finished.reshape(groups, steps, own_rows, width_part)
        .transpose(1, 0, 2, 3)
        .reshape(steps, all_rows, width_part)
    )


def solution(mesh):
    parts = Mesh(mesh.devices.reshape(4, 2, 8, 4, 2), GROUP + TENSOR)
    return jax.shard_map(
        on_device,
        mesh=parts,
        in_specs=(
            P(None, None, GROUP),
            P(GROUP),
            P(GROUP, TENSOR),
            P(GROUP, TENSOR),
            P(GROUP, TENSOR),
            P(TENSOR, GROUP),
            P(None, GROUP, None),
            P(None, TENSOR, None),
            P(None, None, GROUP),
            P(GROUP, None, TENSOR),
            P(GROUP, None, None, TENSOR),
            P(GROUP, TENSOR, None, None),
            P(GROUP, TENSOR, None, None),
            P(),
            P(),
            P(),
            P(GROUP),
        ),
        out_specs=P(None, None, GROUP),
        check_vma=False,
    )
```

```python
import functools
import math

import jax
import jax.numpy as jnp
from jax import lax
from jax.experimental import pallas as pl
from jax.experimental.pallas import tpu as pltpu
from jax.sharding import Mesh
from jax.sharding import PartitionSpec as P

epsilon = 1e-05
GROUP = ("x", "y_lo", "z")
PLANE = ("x", "y_lo")
TENSOR = ("y_hi", "core")
PADDED_WIDTH = 256


def exchange(blocks, axes):
    return lax.all_to_all(blocks, axes, 0, 0, tiled=True)


def apply_rotary(vectors, token_positions):
    half_width = vectors.shape[-1] // 2
    frequency = jnp.exp(
        -jnp.log(500000.0) * jnp.arange(half_width, dtype=jnp.float32) * (2.0 / vectors.shape[-1])
    )
    angles = token_positions.astype(jnp.float32)[:, None] * frequency[None, :]
    cosine = jnp.cos(angles)[:, None, :]
    sine_part = jnp.sin(angles)[:, None, :]
    leading = vectors[..., :half_width]
    trailing = vectors[..., half_width:]
    return jnp.concatenate(
        [leading * cosine - trailing * sine_part, leading * sine_part + trailing * cosine], axis=-1
    )


def dot(left, right):
    return jnp.dot(left, right, preferred_element_type=jnp.float32)


def project_kernel(
    own_rows,
    inputs_ref,
    gain_ref,
    query_ref,
    key_ref,
    value_ref,
    adapter_ref,
    tasks_ref,
    moves_ref,
    out_ref,
):
    steps, all_rows, width = inputs_ref.shape
    every_row = steps * all_rows
    per_group = steps * own_rows
    query_width = query_ref.shape[1]
    head_dim = key_ref.shape[1]
    low = adapter_ref.shape[1]
    base_end = query_width + 2 * head_dim
    block = 128
    gathered = inputs_ref[...].reshape(every_row, width)

    @pl.loop(0, every_row // block)
    def _(index):
        first = pl.multiple_of(index * block, block)
        rows = pl.ds(first, block)

        def row_of(width):
            return first + lax.broadcasted_iota(jnp.int32, (block, width), 0)

        def lane(width):
            return lax.broadcasted_iota(jnp.int32, (block, width), 1)

        def source_of(row):
            return row // per_group * own_rows + row % own_rows

        row = row_of(every_row)
        place = row % per_group // own_rows * all_rows + source_of(row)
        order = jnp.where(lane(every_row) == place, 1.0, 0.0).astype(jnp.bfloat16)
        states = dot(order, gathered)
        gained = (states * gain_ref[...]).astype(jnp.bfloat16)
        squares = jnp.sum(states * states, axis=1, keepdims=True)
        squares_high = squares.astype(jnp.bfloat16).astype(jnp.float32)

        own = lane(all_rows) == source_of(row_of(all_rows))
        task = jnp.sum(jnp.where(own, tasks_ref[...], 0), axis=1, keepdims=True)
        moves = moves_ref.shape[1]
        here = moves_ref[1:2, :] == row_of(moves) // per_group
        moved = jnp.sum(jnp.where(here, 1, 0), axis=1, keepdims=True) > 0
        chosen = jnp.sum(jnp.where(here, moves_ref[0:1, :], 0), axis=1, keepdims=True)
        late = row_of(1) % per_group >= per_group // 2
        task = jnp.where(jnp.logical_and(late, moved), chosen, task)

        out_ref[rows, 0:query_width] = dot(gained, query_ref[...]).astype(jnp.bfloat16)
        out_ref[rows, query_width : query_width + head_dim] = dot(gained, key_ref[...]).astype(
            jnp.bfloat16
        )
        out_ref[rows, query_width + head_dim : base_end] = dot(gained, value_ref[...]).astype(
            jnp.bfloat16
        )
        total = jnp.zeros((block, low), jnp.float32)
        for adapter in range(adapter_ref.shape[0]):
            mine = jnp.where(task == adapter, gained, jnp.zeros_like(gained))
            total = total + lax.dot_general(
                mine,
                adapter_ref[adapter],
                (((1,), (1,)), ((), ())),
                preferred_element_type=jnp.float32,
            )
        rest = PADDED_WIDTH - low
        extra = jnp.where(
            lane(rest) == 0,
            squares_high,
            jnp.where(lane(rest) == 1, squares - squares_high, 0.0),
        )
        out_ref[rows, base_end : base_end + PADDED_WIDTH] = jnp.concatenate(
            [total, extra], axis=1
        ).astype(jnp.bfloat16)


def project(inputs, gain, w_query, w_key, w_value, adapter_in, tasks, moves, own_rows):
    steps, all_rows, width = inputs.shape
    columns = w_query.shape[1] + w_key.shape[1] + w_value.shape[1] + PADDED_WIDTH
    return pl.pallas_call(
        functools.partial(project_kernel, own_rows),
        out_shape=jax.ShapeDtypeStruct((steps * all_rows, columns), jnp.bfloat16),
        compiler_params=pltpu.CompilerParams(vmem_limit_bytes=32 * 1024 * 1024),
        cost_estimate=pl.CostEstimate(
            flops=2 * steps * all_rows * width * 3328, bytes_accessed=3_000_000, transcendentals=0
        ),
    )(
        inputs,
        gain[None, :],
        w_query,
        w_key,
        w_value,
        jnp.swapaxes(adapter_in, 1, 2),
        tasks[None, :],
        moves.T,
    )


def attend(queries, cache_keys, value_cache, fresh_keys, fresh_values, lengths, query_steps):
    scaling = 1.0 / math.sqrt(queries.shape[-1])
    old_scores = (
        jnp.einsum("rnd,rjd->rnj", queries, cache_keys, preferred_element_type=jnp.float32)
        * scaling
    )
    new_scores = (
        jnp.einsum("rnd,rjd->rnj", queries, fresh_keys, preferred_element_type=jnp.float32)
        * scaling
    )
    visible = jnp.arange(cache_keys.shape[1])[None, None, :] < lengths[:, None, None]
    old_scores = jnp.where(visible, old_scores, -1e30)
    fresh = jnp.arange(fresh_keys.shape[1])[None, None, :] <= query_steps[None, :, None]
    new_scores = jnp.where(fresh, new_scores, -1e30)
    highest = jnp.maximum(jnp.max(old_scores, axis=-1), jnp.max(new_scores, axis=-1))[..., None]
    old_exp = jnp.exp(old_scores - highest)
    new_exp = jnp.exp(new_scores - highest)
    denominator = jnp.sum(old_exp, axis=-1, keepdims=True) + jnp.sum(
        new_exp, axis=-1, keepdims=True
    )
    old_weights = (old_exp / denominator).astype(jnp.bfloat16)
    new_weights = (new_exp / denominator).astype(jnp.bfloat16)
    mixed = jnp.einsum(
        "rnj,rjd->rnd", old_weights, value_cache, preferred_element_type=jnp.float32
    )
    mixed = mixed + jnp.einsum(
        "rnj,rjd->rnd", new_weights, fresh_values, preferred_element_type=jnp.float32
    )
    return mixed.astype(jnp.bfloat16)


def on_device(
    inputs,
    gain,
    w_query,
    key_projection_weight,
    value_projection_weight,
    w_output,
    adapter_in,
    adapter_attn,
    adapter_out,
    pool_query,
    slot_keyvalue_matrices,
    cache_keys,
    value_cache,
    tasks,
    homes,
    moves,
    lengths,
):
    steps, all_rows, width_part = inputs.shape
    own_rows = lengths.shape[0]
    groups = all_rows // own_rows
    planes = lax.axis_size(PLANE)
    depth = lax.axis_size("z")
    task_count = homes.shape[0]
    rank = adapter_out.shape[1]
    head_dim = cache_keys.shape[3]
    query_width = w_query.shape[1]
    heads = query_width // head_dim
    key_end = query_width + head_dim
    base_end = key_end + head_dim
    per_group = steps * own_rows
    every_row = groups * per_group
    model_width = width_part * groups
    line = lax.axis_size("x")
    column_rows = depth * per_group

    group_tasks = tasks.reshape(groups, own_rows)
    matched = moves[:, 1][None, :] == jnp.arange(groups, dtype=jnp.int32)[:, None]
    moved = jnp.any(matched, axis=1)
    chosen = jnp.sum(jnp.where(matched, moves[:, 0][None, :], 0), axis=1)
    late = jnp.where(moved[:, None], chosen[:, None], group_tasks)
    active = jnp.stack([group_tasks if s < steps // 2 else late for s in range(steps)], axis=1)
    active = active.reshape(every_row)
    marks = active[:, None] == jnp.arange(task_count, dtype=jnp.int32)[None, :]
    row_home = jnp.sum(jnp.where(marks, homes[None, :], 0), axis=1)

    up = jnp.concatenate(
        [
            pool_query.reshape(rank, query_width),
            slot_keyvalue_matrices.reshape(rank, 2 * head_dim),
        ],
        axis=1,
    )
    with jax.named_scope("up_y_lo"):
        up_pair = jnp.stack([up, lax.ppermute(up, "y_lo", [(0, 1), (1, 0)])])
    with jax.named_scope("up_x"):
        up_plane = lax.all_gather(up_pair, "x", axis=0)

    partial = project(
        inputs,
        gain,
        w_query,
        key_projection_weight,
        value_projection_weight,
        adapter_in,
        tasks,
        moves,
        own_rows,
    )
    with jax.named_scope("sum_plane"):
        by_plane = exchange(partial.reshape(planes, column_rows, -1), PLANE)

    plane_sum = jnp.sum(by_plane.astype(jnp.float32), axis=0)

    low_end = 3 * rank
    low_part = plane_sum[:, base_end:]
    squares = low_part[:, low_end : low_end + 1] + low_part[:, low_end + 1 : low_end + 2]
    squares_high = lax.reduce_precision(squares, 8, 7)
    low_part = jnp.concatenate(
        [
            low_part[:, :low_end],
            squares_high,
            squares - squares_high,
            low_part[:, low_end + 2 :],
        ],
        axis=1,
    ).astype(jnp.bfloat16)
    with jax.named_scope("sum_low"):
        low_sum = exchange(
            jnp.broadcast_to(low_part[None], (depth, column_rows, PADDED_WIDTH)), "z"
        )
    low_sum = jnp.sum(low_sum.astype(jnp.float32), axis=0)
    inverse = lax.rsqrt(
        (low_sum[:, low_end : low_end + 1] + low_sum[:, low_end + 1 : low_end + 2]) / model_width
        + epsilon
    )
    lowrank = (inverse * low_sum[:, :low_end]).astype(jnp.bfloat16)

    x, y_lo, z = (lax.axis_index(name) for name in GROUP)
    column_home = lax.dynamic_slice_in_dim(
        row_home, (x * 2 + y_lo) * column_rows, column_rows, 0
    )

    halves = jnp.stack([y_lo, 1 - y_lo])
    slots = ((jnp.arange(line)[:, None] * 2 + halves[None, :]) * depth + z).reshape(-1)
    use = column_home[:, None] == slots[None, :]
    up_flat = up_plane.reshape(planes * rank, base_end)

    def lift(block, first, last):
        rows = lowrank[:, block * rank : (block + 1) * rank]
        spread = jnp.where(use[:, :, None], rows[:, None, :], 0).reshape(
            column_rows, planes * rank
        )
        return dot(spread, up_flat[:, first:last])

    lifted = jnp.concatenate(
        [lift(0, 0, query_width), lift(1, query_width, key_end), lift(2, key_end, base_end)],
        axis=1,
    )
    raw_part = (inverse * plane_sum[:, :base_end] + lifted).astype(jnp.bfloat16)
    with jax.named_scope("sum_z"):
        by_depth = exchange(raw_part.reshape(depth, per_group, base_end), "z")
    raw = jnp.sum(by_depth.astype(jnp.float32), axis=0)

    row_step = jnp.arange(per_group) // own_rows
    positions = jnp.tile(lengths, steps) + row_step
    queries = apply_rotary(raw[:, :query_width].reshape(per_group, heads, head_dim), positions)
    new_keys = apply_rotary(
        raw[:, query_width:key_end].reshape(per_group, 1, head_dim), positions
    )
    raw_value = raw[:, key_end:]

    def by_row(array):
        return (
            array.astype(jnp.bfloat16)
            .reshape(steps, own_rows, -1, head_dim)
            .transpose(1, 0, 2, 3)
            .reshape(own_rows, -1, head_dim)
        )

    attended = attend(
        by_row(queries),
        cache_keys.reshape(own_rows, -1, head_dim),
        value_cache.reshape(own_rows, -1, head_dim),
        by_row(new_keys),
        by_row(raw_value),
        lengths,
        jnp.arange(steps * heads) // heads,
    )
    attended = (
        attended.reshape(own_rows, steps, query_width)
        .transpose(1, 0, 2)
        .reshape(per_group, query_width)
    )

    with jax.named_scope("gather_z"):
        line = exchange(
            jnp.broadcast_to(attended[None], (depth, per_group, query_width)), "z"
        ).reshape(depth * per_group, query_width)
    with jax.named_scope("gather_plane"):
        piece_rows = exchange(
            jnp.broadcast_to(line[None], (planes, depth * per_group, query_width)), PLANE
        ).reshape(every_row, query_width)

    every_reduced = jnp.einsum(
        "rq,tqc->rtc", piece_rows, adapter_attn, preferred_element_type=jnp.float32
    )
    reduced = jnp.where(marks[:, :, None], every_reduced, 0).astype(jnp.bfloat16)
    mixed = dot(piece_rows, w_output) + dot(
        reduced.reshape(every_row, task_count * rank),
        adapter_out.reshape(task_count * rank, width_part),
    )
    mixed = mixed.astype(jnp.bfloat16)
    half = every_row // 2
    core = lax.axis_index("core")
    with jax.named_scope("sum_core"):
        pair = lax.all_gather(mixed, "core", axis=0)
    mine = lax.dynamic_slice_in_dim(pair, core * half, half, 1).astype(jnp.float32)
    mine = (mine[0] + mine[1]).astype(jnp.bfloat16)
    with jax.named_scope("sum_y_hi"):
        mine = exchange(
            jnp.broadcast_to(mine[None], (lax.axis_size("y_hi"), half, width_part)), "y_hi"
        )
    mine = jnp.sum(mine.astype(jnp.float32), axis=0)
    residual = (
        inputs.reshape(steps, groups, own_rows, width_part)
        .transpose(1, 0, 2, 3)
        .reshape(every_row, width_part)
    )
    residual = lax.dynamic_slice_in_dim(residual, core * half, half, 0)
    finished = residual.astype(jnp.float32) + mine
    with jax.named_scope("gather_core"):
        finished = lax.all_gather(finished.astype(jnp.bfloat16), "core", axis=0, tiled=True)
    return (
        finished.reshape(groups, steps, own_rows, width_part)
        .transpose(1, 0, 2, 3)
        .reshape(steps, all_rows, width_part)
    )


def solution(mesh):
    parts = Mesh(mesh.devices.reshape(4, 2, 8, 4, 2), GROUP + TENSOR)
    return jax.shard_map(
        on_device,
        mesh=parts,
        in_specs=(
            P(None, None, GROUP),
            P(GROUP),
            P(GROUP, TENSOR),
            P(GROUP, TENSOR),
            P(GROUP, TENSOR),
            P(TENSOR, GROUP),
            P(None, GROUP, None),
            P(None, TENSOR, None),
            P(None, None, GROUP),
            P(GROUP, None, TENSOR),
            P(GROUP, None, None, TENSOR),
            P(GROUP, TENSOR, None, None),
            P(GROUP, TENSOR, None, None),
            P(),
            P(),
            P(),
            P(GROUP),
        ),
        out_specs=P(None, None, GROUP),
        check_vma=False,
    )
```

```python
import functools
import math

import jax
import jax.numpy as jnp
from jax import lax
from jax.experimental import pallas as pl
from jax.experimental.pallas import tpu as pltpu
from jax.sharding import Mesh
from jax.sharding import PartitionSpec as P

epsilon = 1e-05
GROUP = ("x", "y_lo", "z")
PLANE = ("x", "y_lo")
TENSOR = ("y_hi", "core")
PADDED_WIDTH = 256


def exchange(blocks, axes):
    return lax.all_to_all(blocks, axes, 0, 0, tiled=True)


def apply_rotary(vectors, token_positions):
    half_width = vectors.shape[-1] // 2
    frequency = jnp.exp(
        -jnp.log(500000.0) * jnp.arange(half_width, dtype=jnp.float32) * (2.0 / vectors.shape[-1])
    )
    angles = token_positions.astype(jnp.float32)[:, None] * frequency[None, :]
    cosine = jnp.cos(angles)[:, None, :]
    sine_part = jnp.sin(angles)[:, None, :]
    leading = vectors[..., :half_width]
    trailing = vectors[..., half_width:]
    return jnp.concatenate(
        [leading * cosine - trailing * sine_part, leading * sine_part + trailing * cosine], axis=-1
    )


def dot(left, right):
    return jnp.dot(left, right, preferred_element_type=jnp.float32)


def project_kernel(
    own_rows,
    inputs_ref,
    gain_ref,
    query_ref,
    key_ref,
    value_ref,
    adapter_ref,
    tasks_ref,
    moves_ref,
    out_ref,
    held_inputs,
    held_query,
    held_key,
    held_value,
    held_adapter,
    arrived,
):
    steps, all_rows, width = inputs_ref.shape
    every_row = steps * all_rows
    per_group = steps * own_rows
    query_width = query_ref.shape[1]
    head_dim = key_ref.shape[1]
    low = adapter_ref.shape[1]
    base_end = query_width + 2 * head_dim
    block = 128
    pairs = (
        (inputs_ref, held_inputs),
        (query_ref, held_query),
        (key_ref, held_key),
        (value_ref, held_value),
        (adapter_ref, held_adapter),
    )
    copies = [
        pltpu.make_async_copy(source, held, arrived.at[number])
        for number, (source, held) in enumerate(pairs)
    ]
    for copy in copies:
        copy.start()
    for copy in copies:
        copy.wait()
    gathered = held_inputs[...].reshape(every_row, width)

    @pl.loop(0, every_row // block)
    def _(index):
        first = pl.multiple_of(index * block, block)
        rows = pl.ds(first, block)

        def row_of(width):
            return first + lax.broadcasted_iota(jnp.int32, (block, width), 0)

        def lane(width):
            return lax.broadcasted_iota(jnp.int32, (block, width), 1)

        def source_of(row):
            return row // per_group * own_rows + row % own_rows

        row = row_of(every_row)
        place = row % per_group // own_rows * all_rows + source_of(row)
        order = jnp.where(lane(every_row) == place, 1.0, 0.0).astype(jnp.bfloat16)
        states = dot(order, gathered)
        gained = (states * gain_ref[...]).astype(jnp.bfloat16)
        squares = jnp.sum(states * states, axis=1, keepdims=True)
        squares_high = squares.astype(jnp.bfloat16).astype(jnp.float32)

        own = lane(all_rows) == source_of(row_of(all_rows))
        task = jnp.sum(jnp.where(own, tasks_ref[...], 0), axis=1, keepdims=True)
        moves = moves_ref.shape[1]
        here = moves_ref[1:2, :] == row_of(moves) // per_group
        moved = jnp.sum(jnp.where(here, 1, 0), axis=1, keepdims=True) > 0
        chosen = jnp.sum(jnp.where(here, moves_ref[0:1, :], 0), axis=1, keepdims=True)
        late = row_of(1) % per_group >= per_group // 2
        task = jnp.where(jnp.logical_and(late, moved), chosen, task)

        out_ref[rows, 0:query_width] = dot(gained, held_query[...]).astype(jnp.bfloat16)
        out_ref[rows, query_width : query_width + head_dim] = dot(gained, held_key[...]).astype(
            jnp.bfloat16
        )
        out_ref[rows, query_width + head_dim : base_end] = dot(gained, held_value[...]).astype(
            jnp.bfloat16
        )
        total = jnp.zeros((block, low), jnp.float32)
        for adapter in range(adapter_ref.shape[0]):
            mine = jnp.where(task == adapter, gained, jnp.zeros_like(gained))
            total = total + lax.dot_general(
                mine,
                held_adapter[adapter],
                (((1,), (1,)), ((), ())),
                preferred_element_type=jnp.float32,
            )
        rest = PADDED_WIDTH - low
        extra = jnp.where(
            lane(rest) == 0,
            squares_high,
            jnp.where(lane(rest) == 1, squares - squares_high, 0.0),
        )
        out_ref[rows, base_end : base_end + PADDED_WIDTH] = jnp.concatenate(
            [total, extra], axis=1
        ).astype(jnp.bfloat16)


def project(inputs, gain, w_query, w_key, w_value, adapter_in, tasks, moves, own_rows):
    steps, all_rows, width = inputs.shape
    down = jnp.swapaxes(adapter_in, 1, 2)
    columns = w_query.shape[1] + w_key.shape[1] + w_value.shape[1] + PADDED_WIDTH
    return pl.pallas_call(
        functools.partial(project_kernel, own_rows),
        out_shape=jax.ShapeDtypeStruct((steps * all_rows, columns), jnp.bfloat16),
        in_specs=[
            pl.BlockSpec(memory_space=pl.ANY),
            pl.BlockSpec(memory_space=pltpu.VMEM),
            pl.BlockSpec(memory_space=pl.ANY),
            pl.BlockSpec(memory_space=pl.ANY),
            pl.BlockSpec(memory_space=pl.ANY),
            pl.BlockSpec(memory_space=pl.ANY),
            pl.BlockSpec(memory_space=pltpu.VMEM),
            pl.BlockSpec(memory_space=pltpu.VMEM),
        ],
        scratch_shapes=[
            pltpu.VMEM(inputs.shape, jnp.bfloat16),
            pltpu.VMEM(w_query.shape, jnp.bfloat16),
            pltpu.VMEM(w_key.shape, jnp.bfloat16),
            pltpu.VMEM(w_value.shape, jnp.bfloat16),
            pltpu.VMEM(down.shape, jnp.bfloat16),
            pltpu.SemaphoreType.DMA((5,)),
        ],
        compiler_params=pltpu.CompilerParams(vmem_limit_bytes=32 * 1024 * 1024),
        cost_estimate=pl.CostEstimate(
            flops=2 * steps * all_rows * width * 3328, bytes_accessed=3_000_000, transcendentals=0
        ),
    )(
        inputs,
        gain[None, :],
        w_query,
        w_key,
        w_value,
        down,
        tasks[None, :],
        moves.T,
    )


def attend(queries, cache_keys, value_cache, fresh_keys, fresh_values, lengths, query_steps):
    scaling = 1.0 / math.sqrt(queries.shape[-1])
    old_scores = (
        jnp.einsum("rnd,rjd->rnj", queries, cache_keys, preferred_element_type=jnp.float32)
        * scaling
    )
    new_scores = (
        jnp.einsum("rnd,rjd->rnj", queries, fresh_keys, preferred_element_type=jnp.float32)
        * scaling
    )
    visible = jnp.arange(cache_keys.shape[1])[None, None, :] < lengths[:, None, None]
    old_scores = jnp.where(visible, old_scores, -1e30)
    fresh = jnp.arange(fresh_keys.shape[1])[None, None, :] <= query_steps[None, :, None]
    new_scores = jnp.where(fresh, new_scores, -1e30)
    highest = jnp.maximum(jnp.max(old_scores, axis=-1), jnp.max(new_scores, axis=-1))[..., None]
    old_exp = jnp.exp(old_scores - highest)
    new_exp = jnp.exp(new_scores - highest)
    denominator = jnp.sum(old_exp, axis=-1, keepdims=True) + jnp.sum(
        new_exp, axis=-1, keepdims=True
    )
    old_weights = (old_exp / denominator).astype(jnp.bfloat16)
    new_weights = (new_exp / denominator).astype(jnp.bfloat16)
    mixed = jnp.einsum(
        "rnj,rjd->rnd", old_weights, value_cache, preferred_element_type=jnp.float32
    )
    mixed = mixed + jnp.einsum(
        "rnj,rjd->rnd", new_weights, fresh_values, preferred_element_type=jnp.float32
    )
    return mixed.astype(jnp.bfloat16)


def on_device(
    inputs,
    gain,
    w_query,
    key_projection_weight,
    value_projection_weight,
    w_output,
    adapter_in,
    adapter_attn,
    adapter_out,
    pool_query,
    slot_keyvalue_matrices,
    cache_keys,
    value_cache,
    tasks,
    homes,
    moves,
    lengths,
):
    steps, all_rows, width_part = inputs.shape
    own_rows = lengths.shape[0]
    groups = all_rows // own_rows
    planes = lax.axis_size(PLANE)
    depth = lax.axis_size("z")
    task_count = homes.shape[0]
    rank = adapter_out.shape[1]
    head_dim = cache_keys.shape[3]
    query_width = w_query.shape[1]
    heads = query_width // head_dim
    key_end = query_width + head_dim
    base_end = key_end + head_dim
    per_group = steps * own_rows
    every_row = groups * per_group
    model_width = width_part * groups
    column_rows = depth * per_group

    group_tasks = tasks.reshape(groups, own_rows)
    matched = moves[:, 1][None, :] == jnp.arange(groups, dtype=jnp.int32)[:, None]
    moved = jnp.any(matched, axis=1)
    chosen = jnp.sum(jnp.where(matched, moves[:, 0][None, :], 0), axis=1)
    late = jnp.where(moved[:, None], chosen[:, None], group_tasks)
    active = jnp.stack([group_tasks if s < steps // 2 else late for s in range(steps)], axis=1)
    active = active.reshape(every_row)
    marks = active[:, None] == jnp.arange(task_count, dtype=jnp.int32)[None, :]
    row_home = jnp.sum(jnp.where(marks, homes[None, :], 0), axis=1)

    up = jnp.concatenate(
        [
            pool_query.reshape(rank, query_width),
            slot_keyvalue_matrices.reshape(rank, 2 * head_dim),
        ],
        axis=1,
    )
    with jax.named_scope("up_plane"):
        up_plane = exchange(jnp.broadcast_to(up[None], (planes, rank, base_end)), PLANE)

    partial = project(
        inputs,
        gain,
        w_query,
        key_projection_weight,
        value_projection_weight,
        adapter_in,
        tasks,
        moves,
        own_rows,
    )
    with jax.named_scope("sum_plane"):
        by_plane = exchange(partial.reshape(planes, column_rows, -1), PLANE)

    plane_sum = jnp.sum(by_plane.astype(jnp.float32), axis=0)

    low_end = 3 * rank
    low_part = plane_sum[:, base_end:]
    squares = low_part[:, low_end : low_end + 1] + low_part[:, low_end + 1 : low_end + 2]
    squares_high = lax.reduce_precision(squares, 8, 7)
    low_part = jnp.concatenate(
        [
            low_part[:, :low_end],
            squares_high,
            squares - squares_high,
            low_part[:, low_end + 2 :],
        ],
        axis=1,
    ).astype(jnp.bfloat16)
    with jax.named_scope("sum_low"):
        low_sum = exchange(
            jnp.broadcast_to(low_part[None], (depth, column_rows, PADDED_WIDTH)), "z"
        )
    low_sum = jnp.sum(low_sum.astype(jnp.float32), axis=0)
    inverse = lax.rsqrt(
        (low_sum[:, low_end : low_end + 1] + low_sum[:, low_end + 1 : low_end + 2]) / model_width
        + epsilon
    )
    lowrank = (inverse * low_sum[:, :low_end]).astype(jnp.bfloat16)

    x, y_lo, z = (lax.axis_index(name) for name in GROUP)
    column_home = lax.dynamic_slice_in_dim(
        row_home, (x * 2 + y_lo) * column_rows, column_rows, 0
    )

    slots = jnp.arange(planes) * depth + z
    use = column_home[:, None] == slots[None, :]
    up_flat = up_plane.reshape(planes * rank, base_end)

    def lift(block, first, last):
        rows = lowrank[:, block * rank : (block + 1) * rank]
        spread = jnp.where(use[:, :, None], rows[:, None, :], 0).reshape(
            column_rows, planes * rank
        )
        return dot(spread, up_flat[:, first:last])

    lifted = jnp.concatenate(
        [lift(0, 0, query_width), lift(1, query_width, key_end), lift(2, key_end, base_end)],
        axis=1,
    )
    raw_part = (inverse * plane_sum[:, :base_end] + lifted).astype(jnp.bfloat16)
    with jax.named_scope("sum_z"):
        by_depth = exchange(raw_part.reshape(depth, per_group, base_end), "z")
    raw = jnp.sum(by_depth.astype(jnp.float32), axis=0)

    row_step = jnp.arange(per_group) // own_rows
    positions = jnp.tile(lengths, steps) + row_step
    queries = apply_rotary(raw[:, :query_width].reshape(per_group, heads, head_dim), positions)
    new_keys = apply_rotary(
        raw[:, query_width:key_end].reshape(per_group, 1, head_dim), positions
    )
    raw_value = raw[:, key_end:]

    def by_row(array):
        return (
            array.astype(jnp.bfloat16)
            .reshape(steps, own_rows, -1, head_dim)
            .transpose(1, 0, 2, 3)
            .reshape(own_rows, -1, head_dim)
        )

    attended = attend(
        by_row(queries),
        cache_keys.reshape(own_rows, -1, head_dim),
        value_cache.reshape(own_rows, -1, head_dim),
        by_row(new_keys),
        by_row(raw_value),
        lengths,
        jnp.arange(steps * heads) // heads,
    )
    attended = (
        attended.reshape(own_rows, steps, query_width)
        .transpose(1, 0, 2)
        .reshape(per_group, query_width)
    )

    with jax.named_scope("gather_z"):
        line = exchange(
            jnp.broadcast_to(attended[None], (depth, per_group, query_width)), "z"
        ).reshape(depth * per_group, query_width)
    with jax.named_scope("gather_plane"):
        piece_rows = exchange(
            jnp.broadcast_to(line[None], (planes, depth * per_group, query_width)), PLANE
        ).reshape(every_row, query_width)

    every_reduced = jnp.einsum(
        "rq,tqc->rtc", piece_rows, adapter_attn, preferred_element_type=jnp.float32
    )
    reduced = jnp.where(marks[:, :, None], every_reduced, 0).astype(jnp.bfloat16)
    mixed = dot(piece_rows, w_output) + dot(
        reduced.reshape(every_row, task_count * rank),
        adapter_out.reshape(task_count * rank, width_part),
    )
    mixed = mixed.astype(jnp.bfloat16)
    half = every_row // 2
    core = lax.axis_index("core")
    with jax.named_scope("sum_core"):
        pair = lax.all_gather(mixed, "core", axis=0)
    mine = lax.dynamic_slice_in_dim(pair, core * half, half, 1).astype(jnp.float32)
    mine = (mine[0] + mine[1]).astype(jnp.bfloat16)
    with jax.named_scope("sum_y_hi"):
        mine = exchange(
            jnp.broadcast_to(mine[None], (lax.axis_size("y_hi"), half, width_part)), "y_hi"
        )
    mine = jnp.sum(mine.astype(jnp.float32), axis=0)
    residual = (
        inputs.reshape(steps, groups, own_rows, width_part)
        .transpose(1, 0, 2, 3)
        .reshape(every_row, width_part)
    )
    residual = lax.dynamic_slice_in_dim(residual, core * half, half, 0)
    finished = residual.astype(jnp.float32) + mine
    with jax.named_scope("gather_core"):
        finished = lax.all_gather(finished.astype(jnp.bfloat16), "core", axis=0, tiled=True)
    return (
        finished.reshape(groups, steps, own_rows, width_part)
        .transpose(1, 0, 2, 3)
        .reshape(steps, all_rows, width_part)
    )


def solution(mesh):
    parts = Mesh(mesh.devices.reshape(4, 2, 8, 4, 2), GROUP + TENSOR)
    return jax.shard_map(
        on_device,
        mesh=parts,
        in_specs=(
            P(None, None, GROUP),
            P(GROUP),
            P(GROUP, TENSOR),
            P(GROUP, TENSOR),
            P(GROUP, TENSOR),
            P(TENSOR, GROUP),
            P(None, GROUP, None),
            P(None, TENSOR, None),
            P(None, None, GROUP),
            P(GROUP, None, TENSOR),
            P(GROUP, None, None, TENSOR),
            P(GROUP, TENSOR, None, None),
            P(GROUP, TENSOR, None, None),
            P(),
            P(),
            P(),
            P(GROUP),
        ),
        out_specs=P(None, None, GROUP),
        check_vma=False,
    )
```

```python
import functools
import math

import jax
import jax.numpy as jnp
from jax import lax
from jax.experimental import pallas as pl
from jax.experimental.pallas import tpu as pltpu
from jax.sharding import Mesh
from jax.sharding import PartitionSpec as P

epsilon = 1e-05
GROUP = ("x", "y_lo", "z")
PLANE = ("x", "y_lo")
TENSOR = ("y_hi", "core")
PADDED_WIDTH = 256


def exchange(blocks, axes):
    return lax.all_to_all(blocks, axes, 0, 0, tiled=True)


def apply_rotary(vectors, token_positions):
    half_width = vectors.shape[-1] // 2
    frequency = jnp.exp(
        -jnp.log(500000.0) * jnp.arange(half_width, dtype=jnp.float32) * (2.0 / vectors.shape[-1])
    )
    angles = token_positions.astype(jnp.float32)[:, None] * frequency[None, :]
    cosine = jnp.cos(angles)[:, None, :]
    sine_part = jnp.sin(angles)[:, None, :]
    leading = vectors[..., :half_width]
    trailing = vectors[..., half_width:]
    return jnp.concatenate(
        [leading * cosine - trailing * sine_part, leading * sine_part + trailing * cosine], axis=-1
    )


def dot(left, right):
    return jnp.dot(left, right, preferred_element_type=jnp.float32)


def project_kernel(
    own_rows,
    inputs_ref,
    gain_ref,
    query_ref,
    key_ref,
    value_ref,
    adapter_ref,
    tasks_ref,
    moves_ref,
    out_ref,
    held_inputs,
    held_query,
    held_key,
    held_value,
    held_adapter,
    arrived,
):
    steps, all_rows, width = inputs_ref.shape
    every_row = steps * all_rows
    per_group = steps * own_rows
    query_width = query_ref.shape[1]
    head_dim = key_ref.shape[1]
    low = adapter_ref.shape[1]
    base_end = query_width + 2 * head_dim
    block = 128
    pairs = (
        (inputs_ref, held_inputs),
        (query_ref, held_query),
        (key_ref, held_key),
        (value_ref, held_value),
        (adapter_ref, held_adapter),
    )
    copies = [
        pltpu.make_async_copy(source, held, arrived.at[number])
        for number, (source, held) in enumerate(pairs)
    ]
    for copy in copies:
        copy.start()
    for copy in copies:
        copy.wait()
    gathered = held_inputs[...].reshape(every_row, width)

    @pl.loop(0, every_row // block)
    def _(index):
        first = pl.multiple_of(index * block, block)
        rows = pl.ds(first, block)

        def row_of(width):
            return first + lax.broadcasted_iota(jnp.int32, (block, width), 0)

        def lane(width):
            return lax.broadcasted_iota(jnp.int32, (block, width), 1)

        def source_of(row):
            return row // per_group * own_rows + row % own_rows

        row = row_of(every_row)
        place = row % per_group // own_rows * all_rows + source_of(row)
        order = jnp.where(lane(every_row) == place, 1.0, 0.0).astype(jnp.bfloat16)
        states = dot(order, gathered)
        gained = (states * gain_ref[...]).astype(jnp.bfloat16)
        squares = jnp.sum(states * states, axis=1, keepdims=True)
        squares_high = squares.astype(jnp.bfloat16).astype(jnp.float32)

        own = lane(all_rows) == source_of(row_of(all_rows))
        task = jnp.sum(jnp.where(own, tasks_ref[...], 0), axis=1, keepdims=True)
        moves = moves_ref.shape[1]
        here = moves_ref[1:2, :] == row_of(moves) // per_group
        moved = jnp.sum(jnp.where(here, 1, 0), axis=1, keepdims=True) > 0
        chosen = jnp.sum(jnp.where(here, moves_ref[0:1, :], 0), axis=1, keepdims=True)
        late = row_of(1) % per_group >= per_group // 2
        task = jnp.where(jnp.logical_and(late, moved), chosen, task)

        out_ref[rows, 0:query_width] = dot(gained, held_query[...]).astype(jnp.bfloat16)
        out_ref[rows, query_width : query_width + head_dim] = dot(gained, held_key[...]).astype(
            jnp.bfloat16
        )
        out_ref[rows, query_width + head_dim : base_end] = dot(gained, held_value[...]).astype(
            jnp.bfloat16
        )
        total = jnp.zeros((block, low), jnp.float32)
        for adapter in range(adapter_ref.shape[0]):
            mine = jnp.where(task == adapter, gained, jnp.zeros_like(gained))
            total = total + lax.dot_general(
                mine,
                held_adapter[adapter],
                (((1,), (1,)), ((), ())),
                preferred_element_type=jnp.float32,
            )
        rest = PADDED_WIDTH - low
        extra = jnp.where(
            lane(rest) == 0,
            squares_high,
            jnp.where(lane(rest) == 1, squares - squares_high, 0.0),
        )
        out_ref[rows, base_end : base_end + PADDED_WIDTH] = jnp.concatenate(
            [total, extra], axis=1
        ).astype(jnp.bfloat16)


def project(inputs, gain, w_query, w_key, w_value, adapter_in, tasks, moves, own_rows):
    steps, all_rows, width = inputs.shape
    down = jnp.swapaxes(adapter_in, 1, 2)
    columns = w_query.shape[1] + w_key.shape[1] + w_value.shape[1] + PADDED_WIDTH
    return pl.pallas_call(
        functools.partial(project_kernel, own_rows),
        out_shape=jax.ShapeDtypeStruct((steps * all_rows, columns), jnp.bfloat16),
        in_specs=[
            pl.BlockSpec(memory_space=pl.ANY),
            pl.BlockSpec(memory_space=pltpu.VMEM),
            pl.BlockSpec(memory_space=pl.ANY),
            pl.BlockSpec(memory_space=pl.ANY),
            pl.BlockSpec(memory_space=pl.ANY),
            pl.BlockSpec(memory_space=pl.ANY),
            pl.BlockSpec(memory_space=pltpu.VMEM),
            pl.BlockSpec(memory_space=pltpu.VMEM),
        ],
        scratch_shapes=[
            pltpu.VMEM(inputs.shape, jnp.bfloat16),
            pltpu.VMEM(w_query.shape, jnp.bfloat16),
            pltpu.VMEM(w_key.shape, jnp.bfloat16),
            pltpu.VMEM(w_value.shape, jnp.bfloat16),
            pltpu.VMEM(down.shape, jnp.bfloat16),
            pltpu.SemaphoreType.DMA((5,)),
        ],
        cost_estimate=pl.CostEstimate(
            flops=2 * steps * all_rows * width * 3328, bytes_accessed=3_000_000, transcendentals=0
        ),
    )(
        inputs,
        gain[None, :],
        w_query,
        w_key,
        w_value,
        down,
        tasks[None, :],
        moves.T,
    )


def attend(queries, cache_keys, value_cache, fresh_keys, fresh_values, lengths, query_steps):
    scaling = 1.0 / math.sqrt(queries.shape[-1])
    old_scores = (
        jnp.einsum("rnd,rjd->rnj", queries, cache_keys, preferred_element_type=jnp.float32)
        * scaling
    )
    new_scores = (
        jnp.einsum("rnd,rjd->rnj", queries, fresh_keys, preferred_element_type=jnp.float32)
        * scaling
    )
    visible = jnp.arange(cache_keys.shape[1])[None, None, :] < lengths[:, None, None]
    old_scores = jnp.where(visible, old_scores, -1e30)
    fresh = jnp.arange(fresh_keys.shape[1])[None, None, :] <= query_steps[None, :, None]
    new_scores = jnp.where(fresh, new_scores, -1e30)
    highest = jnp.maximum(jnp.max(old_scores, axis=-1), jnp.max(new_scores, axis=-1))[..., None]
    old_exp = jnp.exp(old_scores - highest)
    new_exp = jnp.exp(new_scores - highest)
    denominator = jnp.sum(old_exp, axis=-1, keepdims=True) + jnp.sum(
        new_exp, axis=-1, keepdims=True
    )
    old_weights = (old_exp / denominator).astype(jnp.bfloat16)
    new_weights = (new_exp / denominator).astype(jnp.bfloat16)
    mixed = jnp.einsum(
        "rnj,rjd->rnd", old_weights, value_cache, preferred_element_type=jnp.float32
    )
    mixed = mixed + jnp.einsum(
        "rnj,rjd->rnd", new_weights, fresh_values, preferred_element_type=jnp.float32
    )
    return mixed.astype(jnp.bfloat16)


def on_device(
    inputs,
    gain,
    w_query,
    key_projection_weight,
    value_projection_weight,
    w_output,
    adapter_in,
    adapter_attn,
    adapter_out,
    pool_query,
    slot_keyvalue_matrices,
    cache_keys,
    value_cache,
    tasks,
    homes,
    moves,
    lengths,
):
    steps, all_rows, width_part = inputs.shape
    own_rows = lengths.shape[0]
    groups = all_rows // own_rows
    planes = lax.axis_size(PLANE)
    line = lax.axis_size("x")
    depth = lax.axis_size("z")
    task_count = homes.shape[0]
    rank = adapter_out.shape[1]
    head_dim = cache_keys.shape[3]
    query_width = w_query.shape[1]
    heads = query_width // head_dim
    key_end = query_width + head_dim
    base_end = key_end + head_dim
    per_group = steps * own_rows
    every_row = groups * per_group
    model_width = width_part * groups
    column_rows = depth * per_group

    group_tasks = tasks.reshape(groups, own_rows)
    matched = moves[:, 1][None, :] == jnp.arange(groups, dtype=jnp.int32)[:, None]
    moved = jnp.any(matched, axis=1)
    chosen = jnp.sum(jnp.where(matched, moves[:, 0][None, :], 0), axis=1)
    late = jnp.where(moved[:, None], chosen[:, None], group_tasks)
    active = jnp.stack([group_tasks if s < steps // 2 else late for s in range(steps)], axis=1)
    active = active.reshape(every_row)
    marks = active[:, None] == jnp.arange(task_count, dtype=jnp.int32)[None, :]
    row_home = jnp.sum(jnp.where(marks, homes[None, :], 0), axis=1)

    partial = project(
        inputs,
        gain,
        w_query,
        key_projection_weight,
        value_projection_weight,
        adapter_in,
        tasks,
        moves,
        own_rows,
    )
    partial, pool_query, slot_keyvalue_matrices = lax.optimization_barrier(
        (partial, pool_query, slot_keyvalue_matrices)
    )
    with jax.named_scope("sum_plane"):
        by_plane = exchange(partial.reshape(planes, column_rows, -1), PLANE)

    up = jnp.concatenate(
        [
            pool_query.reshape(rank, query_width),
            slot_keyvalue_matrices.reshape(rank, 2 * head_dim),
        ],
        axis=1,
    )
    with jax.named_scope("up_x"):
        up_line = lax.all_gather(up, "x", axis=0)
    with jax.named_scope("up_y_lo"):
        up_other = lax.ppermute(up_line, "y_lo", [(0, 1), (1, 0)])
    plane_sum = jnp.sum(by_plane.astype(jnp.float32), axis=0)

    low_end = 3 * rank
    low_part = plane_sum[:, base_end:]
    squares = low_part[:, low_end : low_end + 1] + low_part[:, low_end + 1 : low_end + 2]
    squares_high = lax.reduce_precision(squares, 8, 7)
    low_part = jnp.concatenate(
        [
            low_part[:, :low_end],
            squares_high,
            squares - squares_high,
            low_part[:, low_end + 2 :],
        ],
        axis=1,
    ).astype(jnp.bfloat16)
    with jax.named_scope("sum_low"):
        low_sum = exchange(
            jnp.broadcast_to(low_part[None], (depth, column_rows, PADDED_WIDTH)), "z"
        )
    low_sum = jnp.sum(low_sum.astype(jnp.float32), axis=0)
    inverse = lax.rsqrt(
        (low_sum[:, low_end : low_end + 1] + low_sum[:, low_end + 1 : low_end + 2]) / model_width
        + epsilon
    )
    lowrank = (inverse * low_sum[:, :low_end]).astype(jnp.bfloat16)

    x, y_lo, z = (lax.axis_index(name) for name in GROUP)
    column_home = lax.dynamic_slice_in_dim(
        row_home, (x * 2 + y_lo) * column_rows, column_rows, 0
    )

    use = [
        column_home[:, None] == ((jnp.arange(line) * 2 + half) * depth + z)[None, :]
        for half in (y_lo, 1 - y_lo)
    ]

    def lift(block, first, last):
        rows = lowrank[:, block * rank : (block + 1) * rank]
        total = jnp.zeros((column_rows, last - first), jnp.float32)
        for mask, matrices in zip(use, (up_line, up_other), strict=True):
            spread = jnp.where(mask[:, :, None], rows[:, None, :], 0).reshape(
                column_rows, line * rank
            )
            total = total + dot(spread, matrices.reshape(line * rank, base_end)[:, first:last])
        return total

    lifted = jnp.concatenate(
        [lift(0, 0, query_width), lift(1, query_width, key_end), lift(2, key_end, base_end)],
        axis=1,
    )
    raw_part = (inverse * plane_sum[:, :base_end] + lifted).astype(jnp.bfloat16)
    with jax.named_scope("sum_z"):
        by_depth = exchange(raw_part.reshape(depth, per_group, base_end), "z")
    raw = jnp.sum(by_depth.astype(jnp.float32), axis=0)

    row_step = jnp.arange(per_group) // own_rows
    positions = jnp.tile(lengths, steps) + row_step
    queries = apply_rotary(raw[:, :query_width].reshape(per_group, heads, head_dim), positions)
    new_keys = apply_rotary(
        raw[:, query_width:key_end].reshape(per_group, 1, head_dim), positions
    )
    raw_value = raw[:, key_end:]

    def by_row(array):
        return (
            array.astype(jnp.bfloat16)
            .reshape(steps, own_rows, -1, head_dim)
            .transpose(1, 0, 2, 3)
            .reshape(own_rows, -1, head_dim)
        )

    attended = attend(
        by_row(queries),
        cache_keys.reshape(own_rows, -1, head_dim),
        value_cache.reshape(own_rows, -1, head_dim),
        by_row(new_keys),
        by_row(raw_value),
        lengths,
        jnp.arange(steps * heads) // heads,
    )
    attended = (
        attended.reshape(own_rows, steps, query_width)
        .transpose(1, 0, 2)
        .reshape(per_group, query_width)
    )

    with jax.named_scope("gather_z"):
        line = exchange(
            jnp.broadcast_to(attended[None], (depth, per_group, query_width)), "z"
        ).reshape(depth * per_group, query_width)
    with jax.named_scope("gather_plane"):
        piece_rows = exchange(
            jnp.broadcast_to(line[None], (planes, depth * per_group, query_width)), PLANE
        ).reshape(every_row, query_width)

    every_reduced = jnp.einsum(
        "rq,tqc->rtc", piece_rows, adapter_attn, preferred_element_type=jnp.float32
    )
    reduced = jnp.where(marks[:, :, None], every_reduced, 0).astype(jnp.bfloat16)
    mixed = dot(piece_rows, w_output) + dot(
        reduced.reshape(every_row, task_count * rank),
        adapter_out.reshape(task_count * rank, width_part),
    )
    mixed = mixed.astype(jnp.bfloat16)
    half = every_row // 2
    core = lax.axis_index("core")
    with jax.named_scope("sum_core"):
        pair = lax.all_gather(mixed, "core", axis=0)
    mine = lax.dynamic_slice_in_dim(pair, core * half, half, 1).astype(jnp.float32)
    mine = (mine[0] + mine[1]).astype(jnp.bfloat16)
    with jax.named_scope("sum_y_hi"):
        mine = exchange(
            jnp.broadcast_to(mine[None], (lax.axis_size("y_hi"), half, width_part)), "y_hi"
        )
    mine = jnp.sum(mine.astype(jnp.float32), axis=0)
    residual = (
        inputs.reshape(steps, groups, own_rows, width_part)
        .transpose(1, 0, 2, 3)
        .reshape(every_row, width_part)
    )
    residual = lax.dynamic_slice_in_dim(residual, core * half, half, 0)
    finished = residual.astype(jnp.float32) + mine
    with jax.named_scope("gather_core"):
        finished = lax.all_gather(finished.astype(jnp.bfloat16), "core", axis=0, tiled=True)
    return (
        finished.reshape(groups, steps, own_rows, width_part)
        .transpose(1, 0, 2, 3)
        .reshape(steps, all_rows, width_part)
    )


def solution(mesh):
    parts = Mesh(mesh.devices.reshape(4, 2, 8, 4, 2), GROUP + TENSOR)
    return jax.shard_map(
        on_device,
        mesh=parts,
        in_specs=(
            P(None, None, GROUP),
            P(GROUP),
            P(GROUP, TENSOR),
            P(GROUP, TENSOR),
            P(GROUP, TENSOR),
            P(TENSOR, GROUP),
            P(None, GROUP, None),
            P(None, TENSOR, None),
            P(None, None, GROUP),
            P(GROUP, None, TENSOR),
            P(GROUP, None, None, TENSOR),
            P(GROUP, TENSOR, None, None),
            P(GROUP, TENSOR, None, None),
            P(),
            P(),
            P(),
            P(GROUP),
        ),
        out_specs=P(None, None, GROUP),
        check_vma=False,
    )
```

```python
import functools
import math

import jax
import jax.numpy as jnp
from jax import lax
from jax.experimental import pallas as pl
from jax.experimental.pallas import tpu as pltpu
from jax.sharding import Mesh
from jax.sharding import PartitionSpec as P

epsilon = 1e-05
GROUP = ("x", "y_lo", "z")
PLANE = ("x", "y_lo")
TENSOR = ("y_hi", "core")
PADDED_WIDTH = 256


def exchange(blocks, axes):
    return lax.all_to_all(blocks, axes, 0, 0, tiled=True)


def apply_rotary(vectors, token_positions):
    half_width = vectors.shape[-1] // 2
    frequency = jnp.exp(
        -jnp.log(500000.0) * jnp.arange(half_width, dtype=jnp.float32) * (2.0 / vectors.shape[-1])
    )
    angles = token_positions.astype(jnp.float32)[:, None] * frequency[None, :]
    cosine = jnp.cos(angles)[:, None, :]
    sine_part = jnp.sin(angles)[:, None, :]
    leading = vectors[..., :half_width]
    trailing = vectors[..., half_width:]
    return jnp.concatenate(
        [leading * cosine - trailing * sine_part, leading * sine_part + trailing * cosine], axis=-1
    )


def dot(left, right):
    return jnp.dot(left, right, preferred_element_type=jnp.float32)


def start_copies(pairs, arrived):
    copies = [
        pltpu.make_async_copy(source, held, arrived.at[number])
        for number, (source, held) in enumerate(pairs)
    ]
    for copy in copies:
        copy.start()
    return copies


def project_kernel(
    own_rows,
    gain_ref,
    tasks_ref,
    moves_ref,
    inputs_ref,
    adapter_ref,
    query_ref,
    key_ref,
    value_ref,
    out_ref,
    held_inputs,
    held_adapter,
    held_query,
    held_key,
    held_value,
    gained_ref,
    arrived,
):
    steps, all_rows, width = inputs_ref.shape
    every_row = steps * all_rows
    per_group = steps * own_rows
    query_width = query_ref.shape[1]
    head_dim = key_ref.shape[1]
    adapters, low, _ = adapter_ref.shape
    key_end = query_width + head_dim
    base_end = key_end + head_dim
    block = 128
    copies = start_copies(
        (
            (inputs_ref, held_inputs),
            (adapter_ref, held_adapter),
            (query_ref, held_query),
            (key_ref, held_key),
            (value_ref, held_value),
        ),
        arrived,
    )

    def lane(width):
        return lax.broadcasted_iota(jnp.int32, (block, width), 1)

    copies[0].wait()
    gathered = held_inputs[...].reshape(every_row, width)
    squares_of = []
    for first in range(0, every_row, block):
        row = first + lax.broadcasted_iota(jnp.int32, (block, every_row), 0)
        place = row % per_group // own_rows * all_rows + row // per_group * own_rows + row % own_rows
        order = jnp.where(lane(every_row) == place, 1.0, 0.0).astype(jnp.bfloat16)
        states = dot(order, gathered)
        gained_ref[first : first + block, :] = (states * gain_ref[...]).astype(jnp.bfloat16)
        squares_of.append(jnp.sum(states * states, axis=1, keepdims=True))

    copies[1].wait()
    for index, squares in enumerate(squares_of):
        first = index * block

        def row_of(width):
            return first + lax.broadcasted_iota(jnp.int32, (block, width), 0)

        row = row_of(all_rows)
        own = lane(all_rows) == row // per_group * own_rows + row % own_rows
        task = jnp.sum(jnp.where(own, tasks_ref[...], 0), axis=1, keepdims=True)
        moves = moves_ref.shape[1]
        here = moves_ref[1:2, :] == row_of(moves) // per_group
        moved = jnp.sum(jnp.where(here, 1, 0), axis=1, keepdims=True) > 0
        chosen = jnp.sum(jnp.where(here, moves_ref[0:1, :], 0), axis=1, keepdims=True)
        late = row_of(1) % per_group >= per_group // 2
        task = jnp.where(jnp.logical_and(late, moved), chosen, task)
        gained = gained_ref[first : first + block, :]
        total = jnp.zeros((block, low), jnp.float32)
        for adapter in range(0, adapters, 2):
            both = [
                jnp.where(task == number, gained, jnp.zeros_like(gained))
                for number in (adapter, adapter + 1)
            ]
            total = total + lax.dot_general(
                jnp.concatenate(both, axis=1),
                jnp.concatenate([held_adapter[adapter], held_adapter[adapter + 1]], axis=1),
                (((1,), (1,)), ((), ())),
                preferred_element_type=jnp.float32,
            )
        rest = PADDED_WIDTH - low
        squares_high = squares.astype(jnp.bfloat16).astype(jnp.float32)
        extra = jnp.where(
            lane(rest) == 0,
            squares_high,
            jnp.where(lane(rest) == 1, squares - squares_high, 0.0),
        )
        out_ref[first : first + block, base_end : base_end + PADDED_WIDTH] = jnp.concatenate(
            [total, extra], axis=1
        ).astype(jnp.bfloat16)

    for copy in copies[2:]:
        copy.wait()

    @pl.loop(0, every_row // block)
    def _(index):
        rows = pl.ds(pl.multiple_of(index * block, block), block)
        gained = gained_ref[rows, :]
        out_ref[rows, 0:query_width] = dot(gained, held_query[...]).astype(jnp.bfloat16)
        out_ref[rows, query_width:key_end] = dot(gained, held_key[...]).astype(jnp.bfloat16)
        out_ref[rows, key_end:base_end] = dot(gained, held_value[...]).astype(jnp.bfloat16)


def project(inputs, gain, w_query, w_key, w_value, adapter_in, tasks, moves, own_rows):
    steps, all_rows, width = inputs.shape
    columns = w_query.shape[1] + w_key.shape[1] + w_value.shape[1] + PADDED_WIDTH
    large = (inputs, jnp.swapaxes(adapter_in, 1, 2), w_query, w_key, w_value)
    return pl.pallas_call(
        functools.partial(project_kernel, own_rows),
        out_shape=jax.ShapeDtypeStruct((steps * all_rows, columns), jnp.bfloat16),
        in_specs=[pl.BlockSpec(memory_space=pltpu.VMEM)] * 3
        + [pl.BlockSpec(memory_space=pl.ANY)] * len(large),
        scratch_shapes=[pltpu.VMEM(array.shape, jnp.bfloat16) for array in large]
        + [
            pltpu.VMEM((steps * all_rows, width), jnp.bfloat16),
            pltpu.SemaphoreType.DMA((len(large),)),
        ],
        cost_estimate=pl.CostEstimate(
            flops=2 * steps * all_rows * width * 3328, bytes_accessed=3_000_000, transcendentals=0
        ),
    )(gain[None, :], tasks[None, :], moves.T, *large)


def plane_kernel(low, parts_ref, base_ref, low_ref):
    sources, rows, columns = parts_ref.shape
    base_end = base_ref.shape[1]
    @pl.loop(0, rows // 16)
    def _(index):
        part = pl.ds(pl.multiple_of(index * 16, 16), 16)
        total = parts_ref[0, part, :].astype(jnp.float32)
        for source in range(1, sources):
            total = total + parts_ref[source, part, :].astype(jnp.float32)
        base_ref[part, :] = total[:, :base_end]
        last = total[:, base_end:]
        lane = lax.broadcasted_iota(jnp.int32, last.shape, 1)
        squares = jnp.sum(jnp.where(lane >= low, last, 0.0), axis=1, keepdims=True)
        squares_high = squares.astype(jnp.bfloat16).astype(jnp.float32)
        last = jnp.where(
            lane < low,
            last,
            jnp.where(
                lane == low, squares_high, jnp.where(lane == low + 1, squares - squares_high, 0.0)
            ),
        ).astype(jnp.bfloat16)
        for target in range(low_ref.shape[0]):
            low_ref[target, part, :] = last


def sum_plane(parts, base_end, low, depth):
    sources, rows, columns = parts.shape
    return pl.pallas_call(
        functools.partial(plane_kernel, low),
        out_shape=[
            jax.ShapeDtypeStruct((rows, base_end), jnp.float32),
            jax.ShapeDtypeStruct((depth, rows, columns - base_end), jnp.bfloat16),
        ],
        in_specs=[pl.BlockSpec(memory_space=pltpu.VMEM)],
        out_specs=[pl.BlockSpec(memory_space=pltpu.VMEM)] * 2,
        compiler_params=pltpu.CompilerParams(vmem_limit_bytes=16 * 1024 * 1024),
        cost_estimate=pl.CostEstimate(
            flops=parts.size, bytes_accessed=2 * parts.size, transcendentals=0
        ),
    )(parts)


def lift_kernel(
    rank,
    head_dim,
    model_width,
    slot_ref,
    low_ref,
    line_ref,
    other_ref,
    base_ref,
    out_ref,
    held_base,
    arrived,
):
    copy = pltpu.make_async_copy(base_ref, held_base, arrived)
    copy.start()
    rows, columns = out_ref.shape
    line = line_ref.shape[0]
    low = 3 * rank
    total = low_ref[0].astype(jnp.float32)
    for source in range(1, low_ref.shape[0]):
        total = total + low_ref[source].astype(jnp.float32)
    lane = lax.broadcasted_iota(jnp.int32, total.shape, 1)
    squares = jnp.sum(jnp.where(lane >= low, total, 0.0), axis=1, keepdims=True)
    inverse = lax.rsqrt(squares / model_width + epsilon)
    lowrank = (inverse * total).astype(jnp.bfloat16)
    from_lane = lax.broadcasted_iota(jnp.int32, (PADDED_WIDTH, line * rank), 0)
    to_lane = lax.broadcasted_iota(jnp.int32, (PADDED_WIDTH, line * rank), 1)
    slot_lane = lax.broadcasted_iota(jnp.int32, (rows, line * rank), 1) // rank
    slot = slot_ref[...]
    spreads = []
    for number in range(3):
        pick = jnp.where(from_lane == number * rank + to_lane % rank, 1.0, 0.0)
        tiled = dot(lowrank, pick.astype(jnp.bfloat16))
        spreads.append(
            [
                jnp.where(slot == slot_lane + half * line, tiled, 0.0).astype(jnp.bfloat16)
                for half in range(2)
            ]
        )
    copy.wait()
    key_first, value_first = columns - 2 * head_dim, columns - head_dim
    bounds = ((0, key_first), (key_first, value_first), (value_first, columns))
    for (first, last), (near, far) in zip(bounds, spreads, strict=True):
        lifted = dot(near, line_ref[:, :, first:last].reshape(line * rank, last - first))
        lifted = lifted + dot(
            far, other_ref[:, :, first:last].reshape(line * rank, last - first)
        )
        out_ref[:, first:last] = (inverse * held_base[:, first:last] + lifted).astype(jnp.bfloat16)


def lift(slot, low_parts, base, up_line, up_other, rank, head_dim, model_width):
    return pl.pallas_call(
        functools.partial(lift_kernel, rank, head_dim, model_width),
        out_shape=jax.ShapeDtypeStruct(base.shape, jnp.bfloat16),
        in_specs=[pl.BlockSpec(memory_space=pltpu.VMEM)] * 4
        + [pl.BlockSpec(memory_space=pl.ANY)],
        out_specs=pl.BlockSpec(memory_space=pltpu.VMEM),
        scratch_shapes=[pltpu.VMEM(base.shape, jnp.float32), pltpu.SemaphoreType.DMA(())],
        compiler_params=pltpu.CompilerParams(vmem_limit_bytes=16 * 1024 * 1024),
        cost_estimate=pl.CostEstimate(
            flops=2 * base.size * up_line.shape[0] * 2 * rank,
            bytes_accessed=2_000_000,
            transcendentals=0,
        ),
    )(slot, low_parts, up_line, up_other, base)


def attend(queries, cache_keys, value_cache, fresh_keys, fresh_values, lengths, query_steps):
    scaling = 1.0 / math.sqrt(queries.shape[-1])
    old_scores = (
        jnp.einsum("rnd,rjd->rnj", queries, cache_keys, preferred_element_type=jnp.float32)
        * scaling
    )
    new_scores = (
        jnp.einsum("rnd,rjd->rnj", queries, fresh_keys, preferred_element_type=jnp.float32)
        * scaling
    )
    visible = jnp.arange(cache_keys.shape[1])[None, None, :] < lengths[:, None, None]
    old_scores = jnp.where(visible, old_scores, -1e30)
    fresh = jnp.arange(fresh_keys.shape[1])[None, None, :] <= query_steps[None, :, None]
    new_scores = jnp.where(fresh, new_scores, -1e30)
    highest = jnp.maximum(jnp.max(old_scores, axis=-1), jnp.max(new_scores, axis=-1))[..., None]
    old_exp = jnp.exp(old_scores - highest)
    new_exp = jnp.exp(new_scores - highest)
    denominator = jnp.sum(old_exp, axis=-1, keepdims=True) + jnp.sum(
        new_exp, axis=-1, keepdims=True
    )
    old_weights = (old_exp / denominator).astype(jnp.bfloat16)
    new_weights = (new_exp / denominator).astype(jnp.bfloat16)
    mixed = jnp.einsum(
        "rnj,rjd->rnd", old_weights, value_cache, preferred_element_type=jnp.float32
    )
    mixed = mixed + jnp.einsum(
        "rnj,rjd->rnd", new_weights, fresh_values, preferred_element_type=jnp.float32
    )
    return mixed.astype(jnp.bfloat16)


def on_device(
    inputs,
    gain,
    w_query,
    key_projection_weight,
    value_projection_weight,
    w_output,
    adapter_in,
    adapter_attn,
    adapter_out,
    pool_query,
    slot_keyvalue_matrices,
    cache_keys,
    value_cache,
    tasks,
    homes,
    moves,
    lengths,
):
    steps, all_rows, width_part = inputs.shape
    own_rows = lengths.shape[0]
    groups = all_rows // own_rows
    planes = lax.axis_size(PLANE)
    line = lax.axis_size("x")
    depth = lax.axis_size("z")
    task_count = homes.shape[0]
    rank = adapter_out.shape[1]
    head_dim = cache_keys.shape[3]
    query_width = w_query.shape[1]
    heads = query_width // head_dim
    key_end = query_width + head_dim
    base_end = key_end + head_dim
    per_group = steps * own_rows
    every_row = groups * per_group
    model_width = width_part * groups
    column_rows = depth * per_group

    group_tasks = tasks.reshape(groups, own_rows)
    matched = moves[:, 1][None, :] == jnp.arange(groups, dtype=jnp.int32)[:, None]
    moved = jnp.any(matched, axis=1)
    chosen = jnp.sum(jnp.where(matched, moves[:, 0][None, :], 0), axis=1)
    late = jnp.where(moved[:, None], chosen[:, None], group_tasks)
    active = jnp.stack([group_tasks if s < steps // 2 else late for s in range(steps)], axis=1)
    active = active.reshape(every_row)
    marks = active[:, None] == jnp.arange(task_count, dtype=jnp.int32)[None, :]
    row_home = jnp.sum(jnp.where(marks, homes[None, :], 0), axis=1)

    partial = project(
        inputs,
        gain,
        w_query,
        key_projection_weight,
        value_projection_weight,
        adapter_in,
        tasks,
        moves,
        own_rows,
    )
    partial, pool_query, slot_keyvalue_matrices = lax.optimization_barrier(
        (partial, pool_query, slot_keyvalue_matrices)
    )
    with jax.named_scope("sum_plane"):
        by_plane = exchange(partial.reshape(planes, column_rows, -1), PLANE)

    up = jnp.concatenate(
        [
            pool_query.reshape(rank, query_width),
            slot_keyvalue_matrices.reshape(rank, 2 * head_dim),
        ],
        axis=1,
    )
    with jax.named_scope("up_x"):
        up_line = lax.all_gather(up, "x", axis=0)
    with jax.named_scope("up_y_lo"):
        up_other = lax.ppermute(up_line, "y_lo", [(0, 1), (1, 0)])
    plane_sum, low_part = sum_plane(by_plane, base_end, 3 * rank, depth)
    with jax.named_scope("sum_low"):
        low_parts = exchange(low_part, "z")

    x, y_lo, z = (lax.axis_index(name) for name in GROUP)
    column_home = lax.dynamic_slice_in_dim(
        row_home, (x * 2 + y_lo) * column_rows, column_rows, 0
    )
    home_x = column_home // (2 * depth)
    other_half = jnp.where(column_home // depth % 2 == y_lo, 0, line)
    slot = jnp.where(column_home % depth == z, home_x + other_half, -1)
    raw_part = lift(
        slot[:, None], low_parts, plane_sum, up_line, up_other, rank, head_dim, model_width
    )
    with jax.named_scope("sum_z"):
        by_depth = exchange(raw_part.reshape(depth, per_group, base_end), "z")
    raw = jnp.sum(by_depth.astype(jnp.float32), axis=0)

    row_step = jnp.arange(per_group) // own_rows
    positions = jnp.tile(lengths, steps) + row_step
    queries = apply_rotary(raw[:, :query_width].reshape(per_group, heads, head_dim), positions)
    new_keys = apply_rotary(
        raw[:, query_width:key_end].reshape(per_group, 1, head_dim), positions
    )
    raw_value = raw[:, key_end:]

    def by_row(array):
        return (
            array.astype(jnp.bfloat16)
            .reshape(steps, own_rows, -1, head_dim)
            .transpose(1, 0, 2, 3)
            .reshape(own_rows, -1, head_dim)
        )

    attended = attend(
        by_row(queries),
        cache_keys.reshape(own_rows, -1, head_dim),
        value_cache.reshape(own_rows, -1, head_dim),
        by_row(new_keys),
        by_row(raw_value),
        lengths,
        jnp.arange(steps * heads) // heads,
    )
    attended = (
        attended.reshape(own_rows, steps, query_width)
        .transpose(1, 0, 2)
        .reshape(per_group, query_width)
    )

    with jax.named_scope("gather_z"):
        line = exchange(
            jnp.broadcast_to(attended[None], (depth, per_group, query_width)), "z"
        ).reshape(depth * per_group, query_width)
    with jax.named_scope("gather_plane"):
        piece_rows = exchange(
            jnp.broadcast_to(line[None], (planes, depth * per_group, query_width)), PLANE
        ).reshape(every_row, query_width)

    every_reduced = jnp.einsum(
        "rq,tqc->rtc", piece_rows, adapter_attn, preferred_element_type=jnp.float32
    )
    reduced = jnp.where(marks[:, :, None], every_reduced, 0).astype(jnp.bfloat16)
    mixed = dot(piece_rows, w_output) + dot(
        reduced.reshape(every_row, task_count * rank),
        adapter_out.reshape(task_count * rank, width_part),
    )
    mixed = mixed.astype(jnp.bfloat16)
    core = lax.axis_index("core")
    cores = lax.axis_size("core")
    half = steps // cores
    with jax.named_scope("sum_core"):
        pair = lax.all_gather(mixed, "core", axis=0)
    mine = lax.dynamic_slice_in_dim(
        pair.reshape(cores, groups, steps, own_rows, width_part), core * half, half, 2
    ).astype(jnp.float32)
    mine = jnp.sum(mine, axis=0).astype(jnp.bfloat16)
    mine = mine.transpose(1, 0, 2, 3).reshape(half, all_rows, width_part)
    y_his = lax.axis_size("y_hi")
    with jax.named_scope("sum_y_hi"):
        mine = exchange(
            jnp.broadcast_to(mine[None], (y_his, half, all_rows, width_part)).reshape(
                y_his * half, all_rows, width_part
            ),
            "y_hi",
        )
    mine = jnp.sum(
        mine.reshape(y_his, half, all_rows, width_part).astype(jnp.float32), axis=0
    )
    residual = lax.dynamic_slice_in_dim(inputs, core * half, half, 0)
    finished = (residual.astype(jnp.float32) + mine).astype(jnp.bfloat16)
    with jax.named_scope("gather_core"):
        return lax.all_gather(finished, "core", axis=0, tiled=True)


def solution(mesh):
    parts = Mesh(mesh.devices.reshape(4, 2, 8, 4, 2), GROUP + TENSOR)
    return jax.shard_map(
        on_device,
        mesh=parts,
        in_specs=(
            P(None, None, GROUP),
            P(GROUP),
            P(GROUP, TENSOR),
            P(GROUP, TENSOR),
            P(GROUP, TENSOR),
            P(TENSOR, GROUP),
            P(None, GROUP, None),
            P(None, TENSOR, None),
            P(None, None, GROUP),
            P(GROUP, None, TENSOR),
            P(GROUP, None, None, TENSOR),
            P(GROUP, TENSOR, None, None),
            P(GROUP, TENSOR, None, None),
            P(),
            P(),
            P(),
            P(GROUP),
        ),
        out_specs=P(None, None, GROUP),
        check_vma=False,
    )
```

```python
import functools
import math

import jax
import jax.numpy as jnp
from jax import lax
from jax.experimental import pallas as pl
from jax.experimental.pallas import tpu as pltpu
from jax.sharding import Mesh
from jax.sharding import PartitionSpec as P

epsilon = 1e-05
GROUP = ("x", "y_lo", "z")
PLANE = ("x", "y_lo")
TENSOR = ("y_hi", "core")
PADDED_WIDTH = 256


def exchange(blocks, axes):
    return lax.all_to_all(blocks, axes, 0, 0, tiled=True)


def apply_rotary(vectors, token_positions):
    half_width = vectors.shape[-1] // 2
    frequency = jnp.exp(
        -jnp.log(500000.0) * jnp.arange(half_width, dtype=jnp.float32) * (2.0 / vectors.shape[-1])
    )
    angles = token_positions.astype(jnp.float32)[:, None] * frequency[None, :]
    cosine = jnp.cos(angles)[:, None, :]
    sine_part = jnp.sin(angles)[:, None, :]
    leading = vectors[..., :half_width]
    trailing = vectors[..., half_width:]
    return jnp.concatenate(
        [leading * cosine - trailing * sine_part, leading * sine_part + trailing * cosine], axis=-1
    )


def dot(left, right):
    return jnp.dot(left, right, preferred_element_type=jnp.float32)


def start_copies(pairs, arrived):
    copies = [
        pltpu.make_async_copy(source, held, arrived.at[number])
        for number, (source, held) in enumerate(pairs)
    ]
    for copy in copies:
        copy.start()
    return copies


def project_kernel(
    own_rows,
    gain_ref,
    tasks_ref,
    moves_ref,
    inputs_ref,
    adapter_ref,
    query_ref,
    key_ref,
    value_ref,
    out_ref,
    held_inputs,
    held_adapter,
    held_query,
    held_key,
    held_value,
    gained_ref,
    arrived,
):
    steps, all_rows, width = inputs_ref.shape
    every_row = steps * all_rows
    per_group = steps * own_rows
    query_width = query_ref.shape[1]
    head_dim = key_ref.shape[1]
    adapters, low, _ = adapter_ref.shape
    key_end = query_width + head_dim
    base_end = key_end + head_dim
    block = 128
    copies = start_copies(
        (
            (inputs_ref, held_inputs),
            (adapter_ref, held_adapter),
            (query_ref, held_query),
            (key_ref, held_key),
            (value_ref, held_value),
        ),
        arrived,
    )

    def lane(width):
        return lax.broadcasted_iota(jnp.int32, (block, width), 1)

    copies[0].wait()
    gathered = held_inputs[...].reshape(every_row, width)
    squares_of = []
    for first in range(0, every_row, block):
        row = first + lax.broadcasted_iota(jnp.int32, (block, every_row), 0)
        place = row % per_group // own_rows * all_rows + row // per_group * own_rows + row % own_rows
        order = jnp.where(lane(every_row) == place, 1.0, 0.0).astype(jnp.bfloat16)
        states = dot(order, gathered)
        gained_ref[first : first + block, :] = (states * gain_ref[...]).astype(jnp.bfloat16)
        squares_of.append(jnp.sum(states * states, axis=1, keepdims=True))

    copies[1].wait()
    for index, squares in enumerate(squares_of):
        first = index * block

        def row_of(width):
            return first + lax.broadcasted_iota(jnp.int32, (block, width), 0)

        row = row_of(all_rows)
        own = lane(all_rows) == row // per_group * own_rows + row % own_rows
        task = jnp.sum(jnp.where(own, tasks_ref[...], 0), axis=1, keepdims=True)
        moves = moves_ref.shape[1]
        here = moves_ref[1:2, :] == row_of(moves) // per_group
        moved = jnp.sum(jnp.where(here, 1, 0), axis=1, keepdims=True) > 0
        chosen = jnp.sum(jnp.where(here, moves_ref[0:1, :], 0), axis=1, keepdims=True)
        late = row_of(1) % per_group >= per_group // 2
        task = jnp.where(jnp.logical_and(late, moved), chosen, task)
        gained = gained_ref[first : first + block, :]
        total = jnp.zeros((block, low), jnp.float32)
        for adapter in range(0, adapters, 2):
            both = [
                jnp.where(task == number, gained, jnp.zeros_like(gained))
                for number in (adapter, adapter + 1)
            ]
            total = total + lax.dot_general(
                jnp.concatenate(both, axis=1),
                jnp.concatenate([held_adapter[adapter], held_adapter[adapter + 1]], axis=1),
                (((1,), (1,)), ((), ())),
                preferred_element_type=jnp.float32,
            )
        rest = PADDED_WIDTH - low
        squares_high = squares.astype(jnp.bfloat16).astype(jnp.float32)
        extra = jnp.where(
            lane(rest) == 0,
            squares_high,
            jnp.where(lane(rest) == 1, squares - squares_high, 0.0),
        )
        out_ref[first : first + block, base_end : base_end + PADDED_WIDTH] = jnp.concatenate(
            [total, extra], axis=1
        ).astype(jnp.bfloat16)

    for copy in copies[2:]:
        copy.wait()

    @pl.loop(0, every_row // block)
    def _(index):
        rows = pl.ds(pl.multiple_of(index * block, block), block)
        gained = gained_ref[rows, :]
        out_ref[rows, 0:query_width] = dot(gained, held_query[...]).astype(jnp.bfloat16)
        out_ref[rows, query_width:key_end] = dot(gained, held_key[...]).astype(jnp.bfloat16)
        out_ref[rows, key_end:base_end] = dot(gained, held_value[...]).astype(jnp.bfloat16)


def project(inputs, gain, w_query, w_key, w_value, adapter_in, tasks, moves, own_rows):
    steps, all_rows, width = inputs.shape
    columns = w_query.shape[1] + w_key.shape[1] + w_value.shape[1] + PADDED_WIDTH
    large = (inputs, jnp.swapaxes(adapter_in, 1, 2), w_query, w_key, w_value)
    return pl.pallas_call(
        functools.partial(project_kernel, own_rows),
        out_shape=jax.ShapeDtypeStruct((steps * all_rows, columns), jnp.bfloat16),
        in_specs=[pl.BlockSpec(memory_space=pltpu.VMEM)] * 3
        + [pl.BlockSpec(memory_space=pl.ANY)] * len(large),
        scratch_shapes=[pltpu.VMEM(array.shape, jnp.bfloat16) for array in large]
        + [
            pltpu.VMEM((steps * all_rows, width), jnp.bfloat16),
            pltpu.SemaphoreType.DMA((len(large),)),
        ],
        cost_estimate=pl.CostEstimate(
            flops=2 * steps * all_rows * width * 3328, bytes_accessed=3_000_000, transcendentals=0
        ),
    )(gain[None, :], tasks[None, :], moves.T, *large)


def plane_kernel(low, parts_ref, base_ref, low_ref):
    sources, rows, columns = parts_ref.shape
    base_end = base_ref.shape[1]
    @pl.loop(0, rows // 16)
    def _(index):
        part = pl.ds(pl.multiple_of(index * 16, 16), 16)
        total = parts_ref[0, part, :].astype(jnp.float32)
        for source in range(1, sources):
            total = total + parts_ref[source, part, :].astype(jnp.float32)
        base_ref[part, :] = total[:, :base_end]
        last = total[:, base_end:]
        lane = lax.broadcasted_iota(jnp.int32, last.shape, 1)
        squares = jnp.sum(jnp.where(lane >= low, last, 0.0), axis=1, keepdims=True)
        squares_high = squares.astype(jnp.bfloat16).astype(jnp.float32)
        last = jnp.where(
            lane < low,
            last,
            jnp.where(
                lane == low, squares_high, jnp.where(lane == low + 1, squares - squares_high, 0.0)
            ),
        ).astype(jnp.bfloat16)
        for target in range(low_ref.shape[0]):
            low_ref[target, part, :] = last


def sum_plane(parts, base_end, low, depth):
    sources, rows, columns = parts.shape
    return pl.pallas_call(
        functools.partial(plane_kernel, low),
        out_shape=[
            jax.ShapeDtypeStruct((rows, base_end), jnp.float32),
            jax.ShapeDtypeStruct((depth, rows, columns - base_end), jnp.bfloat16),
        ],
        in_specs=[pl.BlockSpec(memory_space=pltpu.VMEM)],
        out_specs=[pl.BlockSpec(memory_space=pltpu.VMEM)] * 2,
        compiler_params=pltpu.CompilerParams(vmem_limit_bytes=16 * 1024 * 1024),
        cost_estimate=pl.CostEstimate(
            flops=parts.size, bytes_accessed=2 * parts.size, transcendentals=0
        ),
    )(parts)


def lift_kernel(
    rank,
    head_dim,
    model_width,
    slot_ref,
    low_ref,
    line_ref,
    other_ref,
    base_ref,
    out_ref,
    held_base,
    arrived,
):
    copy = pltpu.make_async_copy(base_ref, held_base, arrived)
    copy.start()
    rows, columns = out_ref.shape
    line = line_ref.shape[0]
    low = 3 * rank
    total = low_ref[0].astype(jnp.float32)
    for source in range(1, low_ref.shape[0]):
        total = total + low_ref[source].astype(jnp.float32)
    lane = lax.broadcasted_iota(jnp.int32, total.shape, 1)
    squares = jnp.sum(jnp.where(lane >= low, total, 0.0), axis=1, keepdims=True)
    inverse = lax.rsqrt(squares / model_width + epsilon)
    lowrank = (inverse * total).astype(jnp.bfloat16)
    from_lane = lax.broadcasted_iota(jnp.int32, (PADDED_WIDTH, line * rank), 0)
    to_lane = lax.broadcasted_iota(jnp.int32, (PADDED_WIDTH, line * rank), 1)
    slot_lane = lax.broadcasted_iota(jnp.int32, (rows, line * rank), 1) // rank
    slot = slot_ref[...]
    spreads = []
    for number in range(3):
        pick = jnp.where(from_lane == number * rank + to_lane % rank, 1.0, 0.0)
        tiled = dot(lowrank, pick.astype(jnp.bfloat16))
        spreads.append(
            [
                jnp.where(slot == slot_lane + half * line, tiled, 0.0).astype(jnp.bfloat16)
                for half in range(2)
            ]
        )
    copy.wait()
    key_first, value_first = columns - 2 * head_dim, columns - head_dim
    bounds = ((0, key_first), (key_first, value_first), (value_first, columns))
    for (first, last), (near, far) in zip(bounds, spreads, strict=True):
        lifted = dot(near, line_ref[:, :, first:last].reshape(line * rank, last - first))
        lifted = lifted + dot(
            far, other_ref[:, :, first:last].reshape(line * rank, last - first)
        )
        out_ref[:, first:last] = (inverse * held_base[:, first:last] + lifted).astype(jnp.bfloat16)


def lift(slot, low_parts, base, up_line, up_other, rank, head_dim, model_width):
    return pl.pallas_call(
        functools.partial(lift_kernel, rank, head_dim, model_width),
        out_shape=jax.ShapeDtypeStruct(base.shape, jnp.bfloat16),
        in_specs=[pl.BlockSpec(memory_space=pltpu.VMEM)] * 4
        + [pl.BlockSpec(memory_space=pl.ANY)],
        out_specs=pl.BlockSpec(memory_space=pltpu.VMEM),
        scratch_shapes=[pltpu.VMEM(base.shape, jnp.float32), pltpu.SemaphoreType.DMA(())],
        compiler_params=pltpu.CompilerParams(vmem_limit_bytes=16 * 1024 * 1024),
        cost_estimate=pl.CostEstimate(
            flops=2 * base.size * up_line.shape[0] * 2 * rank,
            bytes_accessed=2_000_000,
            transcendentals=0,
        ),
    )(slot, low_parts, up_line, up_other, base)


def attend(queries, cache_keys, value_cache, fresh_keys, fresh_values, lengths, query_steps):
    scaling = 1.0 / math.sqrt(queries.shape[-1])
    old_scores = (
        jnp.einsum("rnd,rjd->rnj", queries, cache_keys, preferred_element_type=jnp.float32)
        * scaling
    )
    new_scores = (
        jnp.einsum("rnd,rjd->rnj", queries, fresh_keys, preferred_element_type=jnp.float32)
        * scaling
    )
    visible = jnp.arange(cache_keys.shape[1])[None, None, :] < lengths[:, None, None]
    old_scores = jnp.where(visible, old_scores, -1e30)
    fresh = jnp.arange(fresh_keys.shape[1])[None, None, :] <= query_steps[None, :, None]
    new_scores = jnp.where(fresh, new_scores, -1e30)
    highest = jnp.maximum(jnp.max(old_scores, axis=-1), jnp.max(new_scores, axis=-1))[..., None]
    old_exp = jnp.exp(old_scores - highest)
    new_exp = jnp.exp(new_scores - highest)
    denominator = jnp.sum(old_exp, axis=-1, keepdims=True) + jnp.sum(
        new_exp, axis=-1, keepdims=True
    )
    old_weights = (old_exp / denominator).astype(jnp.bfloat16)
    new_weights = (new_exp / denominator).astype(jnp.bfloat16)
    mixed = jnp.einsum(
        "rnj,rjd->rnd", old_weights, value_cache, preferred_element_type=jnp.float32
    )
    mixed = mixed + jnp.einsum(
        "rnj,rjd->rnd", new_weights, fresh_values, preferred_element_type=jnp.float32
    )
    return mixed.astype(jnp.bfloat16)


def on_device(
    inputs,
    gain,
    w_query,
    key_projection_weight,
    value_projection_weight,
    w_output,
    adapter_in,
    adapter_attn,
    adapter_out,
    pool_query,
    slot_keyvalue_matrices,
    cache_keys,
    value_cache,
    tasks,
    homes,
    moves,
    lengths,
):
    steps, all_rows, width_part = inputs.shape
    own_rows = lengths.shape[0]
    groups = all_rows // own_rows
    planes = lax.axis_size(PLANE)
    line = lax.axis_size("x")
    depth = lax.axis_size("z")
    task_count = homes.shape[0]
    rank = adapter_out.shape[1]
    head_dim = cache_keys.shape[3]
    query_width = w_query.shape[1]
    heads = query_width // head_dim
    key_end = query_width + head_dim
    base_end = key_end + head_dim
    per_group = steps * own_rows
    every_row = groups * per_group
    model_width = width_part * groups
    column_rows = depth * per_group

    group_tasks = tasks.reshape(groups, own_rows)
    matched = moves[:, 1][None, :] == jnp.arange(groups, dtype=jnp.int32)[:, None]
    moved = jnp.any(matched, axis=1)
    chosen = jnp.sum(jnp.where(matched, moves[:, 0][None, :], 0), axis=1)
    late = jnp.where(moved[:, None], chosen[:, None], group_tasks)
    active = jnp.stack([group_tasks if s < steps // 2 else late for s in range(steps)], axis=1)
    active = active.reshape(every_row)
    marks = active[:, None] == jnp.arange(task_count, dtype=jnp.int32)[None, :]
    row_home = jnp.sum(jnp.where(marks, homes[None, :], 0), axis=1)

    partial = project(
        inputs,
        gain,
        w_query,
        key_projection_weight,
        value_projection_weight,
        adapter_in,
        tasks,
        moves,
        own_rows,
    )
    partial, pool_query, slot_keyvalue_matrices = lax.optimization_barrier(
        (partial, pool_query, slot_keyvalue_matrices)
    )
    with jax.named_scope("sum_plane"):
        by_plane = exchange(partial.reshape(planes, column_rows, -1), PLANE)

    up = jnp.concatenate(
        [
            pool_query.reshape(rank, query_width),
            slot_keyvalue_matrices.reshape(rank, 2 * head_dim),
        ],
        axis=1,
    )
    with jax.named_scope("up_x"):
        ahead = [(i, (i + 1) % line) for i in range(line)]
        back = [(i, (i - 1) % line) for i in range(line)]
        half_rank = rank // 2
        from_left = lax.ppermute(up, "x", ahead)
        from_right = lax.ppermute(up, "x", back)
        from_far = jnp.concatenate(
            [
                lax.ppermute(from_left[:half_rank], "x", ahead),
                lax.ppermute(from_right[half_rank:], "x", back),
            ]
        )
        up_line = jnp.stack([up, from_left, from_right, from_far])
    with jax.named_scope("up_y_lo"):
        up_other = lax.ppermute(up_line, "y_lo", [(0, 1), (1, 0)])
    plane_sum, low_part = sum_plane(by_plane, base_end, 3 * rank, depth)
    with jax.named_scope("sum_low"):
        low_parts = exchange(low_part, "z")

    x, y_lo, z = (lax.axis_index(name) for name in GROUP)
    column_home = lax.dynamic_slice_in_dim(
        row_home, (x * 2 + y_lo) * column_rows, column_rows, 0
    )
    offset = (column_home // (2 * depth) - x) % line
    near_slot = jnp.where(offset == line - 1, 1, jnp.where(offset == 0, 0, offset + 1))
    other_half = jnp.where(column_home // depth % 2 == y_lo, 0, line)
    slot = jnp.where(column_home % depth == z, near_slot + other_half, -1)
    raw_part = lift(
        slot[:, None], low_parts, plane_sum, up_line, up_other, rank, head_dim, model_width
    )
    with jax.named_scope("sum_z"):
        by_depth = exchange(raw_part.reshape(depth, per_group, base_end), "z")
    raw = jnp.sum(by_depth.astype(jnp.float32), axis=0)

    row_step = jnp.arange(per_group) // own_rows
    positions = jnp.tile(lengths, steps) + row_step
    queries = apply_rotary(raw[:, :query_width].reshape(per_group, heads, head_dim), positions)
    new_keys = apply_rotary(
        raw[:, query_width:key_end].reshape(per_group, 1, head_dim), positions
    )
    raw_value = raw[:, key_end:]

    def by_row(array):
        return (
            array.astype(jnp.bfloat16)
            .reshape(steps, own_rows, -1, head_dim)
            .transpose(1, 0, 2, 3)
            .reshape(own_rows, -1, head_dim)
        )

    attended = attend(
        by_row(queries),
        cache_keys.reshape(own_rows, -1, head_dim),
        value_cache.reshape(own_rows, -1, head_dim),
        by_row(new_keys),
        by_row(raw_value),
        lengths,
        jnp.arange(steps * heads) // heads,
    )
    attended = (
        attended.reshape(own_rows, steps, query_width)
        .transpose(1, 0, 2)
        .reshape(per_group, query_width)
    )

    with jax.named_scope("gather_z"):
        line = exchange(
            jnp.broadcast_to(attended[None], (depth, per_group, query_width)), "z"
        ).reshape(depth * per_group, query_width)
    with jax.named_scope("gather_plane"):
        piece_rows = exchange(
            jnp.broadcast_to(line[None], (planes, depth * per_group, query_width)), PLANE
        ).reshape(every_row, query_width)

    every_reduced = jnp.einsum(
        "rq,tqc->rtc", piece_rows, adapter_attn, preferred_element_type=jnp.float32
    )
    reduced = jnp.where(marks[:, :, None], every_reduced, 0).astype(jnp.bfloat16)
    mixed = dot(piece_rows, w_output) + dot(
        reduced.reshape(every_row, task_count * rank),
        adapter_out.reshape(task_count * rank, width_part),
    )
    mixed = mixed.astype(jnp.bfloat16)
    core = lax.axis_index("core")
    cores = lax.axis_size("core")
    half = steps // cores
    with jax.named_scope("sum_core"):
        pair = lax.all_gather(mixed, "core", axis=0)
    mine = lax.dynamic_slice_in_dim(
        pair.reshape(cores, groups, steps, own_rows, width_part), core * half, half, 2
    ).astype(jnp.float32)
    mine = jnp.sum(mine, axis=0).astype(jnp.bfloat16)
    mine = mine.transpose(1, 0, 2, 3).reshape(half, all_rows, width_part)
    y_his = lax.axis_size("y_hi")
    with jax.named_scope("sum_y_hi"):
        mine = exchange(
            jnp.broadcast_to(mine[None], (y_his, half, all_rows, width_part)).reshape(
                y_his * half, all_rows, width_part
            ),
            "y_hi",
        )
    mine = jnp.sum(
        mine.reshape(y_his, half, all_rows, width_part).astype(jnp.float32), axis=0
    )
    residual = lax.dynamic_slice_in_dim(inputs, core * half, half, 0)
    finished = (residual.astype(jnp.float32) + mine).astype(jnp.bfloat16)
    with jax.named_scope("gather_core"):
        return lax.all_gather(finished, "core", axis=0, tiled=True)


def solution(mesh):
    parts = Mesh(mesh.devices.reshape(4, 2, 8, 4, 2), GROUP + TENSOR)
    return jax.shard_map(
        on_device,
        mesh=parts,
        in_specs=(
            P(None, None, GROUP),
            P(GROUP),
            P(GROUP, TENSOR),
            P(GROUP, TENSOR),
            P(GROUP, TENSOR),
            P(TENSOR, GROUP),
            P(None, GROUP, None),
            P(None, TENSOR, None),
            P(None, None, GROUP),
            P(GROUP, None, TENSOR),
            P(GROUP, None, None, TENSOR),
            P(GROUP, TENSOR, None, None),
            P(GROUP, TENSOR, None, None),
            P(),
            P(),
            P(),
            P(GROUP),
        ),
        out_specs=P(None, None, GROUP),
        check_vma=False,
    )
```

```python
import functools
import math

import jax
import jax.numpy as jnp
from jax import lax
from jax.experimental import pallas as pl
from jax.experimental.pallas import tpu as pltpu
from jax.sharding import Mesh
from jax.sharding import PartitionSpec as P

epsilon = 1e-05
GROUP = ("x", "y_lo", "z")
PLANE = ("x", "y_lo")
TENSOR = ("y_hi", "core")
PADDED_WIDTH = 256


def exchange(blocks, axes):
    return lax.all_to_all(blocks, axes, 0, 0, tiled=True)


def apply_rotary(vectors, token_positions):
    half_width = vectors.shape[-1] // 2
    frequency = jnp.exp(
        -jnp.log(500000.0) * jnp.arange(half_width, dtype=jnp.float32) * (2.0 / vectors.shape[-1])
    )
    angles = token_positions.astype(jnp.float32)[:, None] * frequency[None, :]
    cosine = jnp.cos(angles)[:, None, :]
    sine_part = jnp.sin(angles)[:, None, :]
    leading = vectors[..., :half_width]
    trailing = vectors[..., half_width:]
    return jnp.concatenate(
        [leading * cosine - trailing * sine_part, leading * sine_part + trailing * cosine], axis=-1
    )


def dot(left, right):
    return jnp.dot(left, right, preferred_element_type=jnp.float32)


def start_copies(pairs, arrived):
    copies = [
        pltpu.make_async_copy(source, held, arrived.at[number])
        for number, (source, held) in enumerate(pairs)
    ]
    for copy in copies:
        copy.start()
    return copies


def project_kernel(
    own_rows,
    gain_ref,
    tasks_ref,
    moves_ref,
    inputs_ref,
    adapter_ref,
    query_ref,
    key_ref,
    value_ref,
    out_ref,
    held_inputs,
    held_adapter,
    held_query,
    held_key,
    held_value,
    gained_ref,
    arrived,
):
    steps, all_rows, width = inputs_ref.shape
    every_row = steps * all_rows
    per_group = steps * own_rows
    query_width = query_ref.shape[1]
    head_dim = key_ref.shape[1]
    adapters, low, _ = adapter_ref.shape
    key_end = query_width + head_dim
    base_end = key_end + head_dim
    block = 128
    copies = start_copies(
        (
            (inputs_ref, held_inputs),
            (adapter_ref, held_adapter),
            (query_ref, held_query),
            (key_ref, held_key),
            (value_ref, held_value),
        ),
        arrived,
    )

    def lane(width):
        return lax.broadcasted_iota(jnp.int32, (block, width), 1)

    copies[0].wait()
    gathered = held_inputs[...].reshape(every_row, width)
    squares_of = []
    for first in range(0, every_row, block):
        row = first + lax.broadcasted_iota(jnp.int32, (block, every_row), 0)
        place = row % per_group // own_rows * all_rows + row // per_group * own_rows + row % own_rows
        order = jnp.where(lane(every_row) == place, 1.0, 0.0).astype(jnp.bfloat16)
        states = dot(order, gathered)
        gained_ref[first : first + block, :] = (states * gain_ref[...]).astype(jnp.bfloat16)
        squares_of.append(jnp.sum(states * states, axis=1, keepdims=True))

    copies[1].wait()
    for index, squares in enumerate(squares_of):
        first = index * block

        def row_of(width):
            return first + lax.broadcasted_iota(jnp.int32, (block, width), 0)

        row = row_of(all_rows)
        own = lane(all_rows) == row // per_group * own_rows + row % own_rows
        task = jnp.sum(jnp.where(own, tasks_ref[...], 0), axis=1, keepdims=True)
        moves = moves_ref.shape[1]
        here = moves_ref[1:2, :] == row_of(moves) // per_group
        moved = jnp.sum(jnp.where(here, 1, 0), axis=1, keepdims=True) > 0
        chosen = jnp.sum(jnp.where(here, moves_ref[0:1, :], 0), axis=1, keepdims=True)
        late = row_of(1) % per_group >= per_group // 2
        task = jnp.where(jnp.logical_and(late, moved), chosen, task)
        gained = gained_ref[first : first + block, :]
        total = jnp.zeros((block, low), jnp.float32)
        for adapter in range(0, adapters, 2):
            both = [
                jnp.where(task == number, gained, jnp.zeros_like(gained))
                for number in (adapter, adapter + 1)
            ]
            total = total + lax.dot_general(
                jnp.concatenate(both, axis=1),
                jnp.concatenate([held_adapter[adapter], held_adapter[adapter + 1]], axis=1),
                (((1,), (1,)), ((), ())),
                preferred_element_type=jnp.float32,
            )
        rest = PADDED_WIDTH - low
        squares_high = squares.astype(jnp.bfloat16).astype(jnp.float32)
        extra = jnp.where(
            lane(rest) == 0,
            squares_high,
            jnp.where(lane(rest) == 1, squares - squares_high, 0.0),
        )
        out_ref[first : first + block, base_end : base_end + PADDED_WIDTH] = jnp.concatenate(
            [total, extra], axis=1
        ).astype(jnp.bfloat16)

    for copy in copies[2:]:
        copy.wait()

    @pl.loop(0, every_row // block)
    def _(index):
        rows = pl.ds(pl.multiple_of(index * block, block), block)
        gained = gained_ref[rows, :]
        out_ref[rows, 0:query_width] = dot(gained, held_query[...]).astype(jnp.bfloat16)
        out_ref[rows, query_width:key_end] = dot(gained, held_key[...]).astype(jnp.bfloat16)
        out_ref[rows, key_end:base_end] = dot(gained, held_value[...]).astype(jnp.bfloat16)


def project(inputs, gain, w_query, w_key, w_value, adapter_in, tasks, moves, own_rows):
    steps, all_rows, width = inputs.shape
    columns = w_query.shape[1] + w_key.shape[1] + w_value.shape[1] + PADDED_WIDTH
    large = (inputs, jnp.swapaxes(adapter_in, 1, 2), w_query, w_key, w_value)
    return pl.pallas_call(
        functools.partial(project_kernel, own_rows),
        out_shape=jax.ShapeDtypeStruct((steps * all_rows, columns), jnp.bfloat16),
        in_specs=[pl.BlockSpec(memory_space=pltpu.VMEM)] * 3
        + [pl.BlockSpec(memory_space=pl.ANY)] * len(large),
        scratch_shapes=[pltpu.VMEM(array.shape, jnp.bfloat16) for array in large]
        + [
            pltpu.VMEM((steps * all_rows, width), jnp.bfloat16),
            pltpu.SemaphoreType.DMA((len(large),)),
        ],
        cost_estimate=pl.CostEstimate(
            flops=2 * steps * all_rows * width * 3328, bytes_accessed=3_000_000, transcendentals=0
        ),
    )(gain[None, :], tasks[None, :], moves.T, *large)


def low_kernel(low, parts_ref, low_ref):
    sources, rows, columns = parts_ref.shape
    targets, _, width = low_ref.shape
    total = parts_ref[0, :, columns - width :].astype(jnp.float32)
    for source in range(1, sources):
        total = total + parts_ref[source, :, columns - width :].astype(jnp.float32)
    lane = lax.broadcasted_iota(jnp.int32, total.shape, 1)
    squares = jnp.sum(jnp.where(lane >= low, total, 0.0), axis=1, keepdims=True)
    squares_high = squares.astype(jnp.bfloat16).astype(jnp.float32)
    total = jnp.where(
        lane < low,
        total,
        jnp.where(
            lane == low, squares_high, jnp.where(lane == low + 1, squares - squares_high, 0.0)
        ),
    ).astype(jnp.bfloat16)
    for target in range(targets):
        low_ref[target] = total


def sum_low(parts, base_end, low, depth):
    _, rows, columns = parts.shape
    return pl.pallas_call(
        functools.partial(low_kernel, low),
        out_shape=jax.ShapeDtypeStruct((depth, rows, columns - base_end), jnp.bfloat16),
        in_specs=[pl.BlockSpec(memory_space=pltpu.VMEM)],
        out_specs=pl.BlockSpec(memory_space=pltpu.VMEM),
        compiler_params=pltpu.CompilerParams(vmem_limit_bytes=16 * 1024 * 1024),
        cost_estimate=pl.CostEstimate(
            flops=parts.size // 6, bytes_accessed=parts.size // 3, transcendentals=0
        ),
    )(parts)


def lift_kernel(
    rank,
    head_dim,
    model_width,
    slot_ref,
    low_ref,
    line_ref,
    other_ref,
    base_ref,
    out_ref,
):
    rows, columns = out_ref.shape
    line = line_ref.shape[0]
    low = 3 * rank
    total = low_ref[0].astype(jnp.float32)
    for source in range(1, low_ref.shape[0]):
        total = total + low_ref[source].astype(jnp.float32)
    lane = lax.broadcasted_iota(jnp.int32, total.shape, 1)
    squares = jnp.sum(jnp.where(lane >= low, total, 0.0), axis=1, keepdims=True)
    inverse = lax.rsqrt(squares / model_width + epsilon)
    lowrank = (inverse * total).astype(jnp.bfloat16)
    from_lane = lax.broadcasted_iota(jnp.int32, (PADDED_WIDTH, line * rank), 0)
    to_lane = lax.broadcasted_iota(jnp.int32, (PADDED_WIDTH, line * rank), 1)
    slot_lane = lax.broadcasted_iota(jnp.int32, (rows, line * rank), 1) // rank
    slot = slot_ref[...]
    spreads = []
    for number in range(3):
        pick = jnp.where(from_lane == number * rank + to_lane % rank, 1.0, 0.0)
        tiled = dot(lowrank, pick.astype(jnp.bfloat16))
        spreads.append(
            [
                jnp.where(slot == slot_lane + half * line, tiled, 0.0).astype(jnp.bfloat16)
                for half in range(2)
            ]
        )
    key_first, value_first = columns - 2 * head_dim, columns - head_dim
    bounds = ((0, key_first), (key_first, value_first), (value_first, columns))
    for (first, last), (near, far) in zip(bounds, spreads, strict=True):
        lifted = dot(near, line_ref[:, :, first:last].reshape(line * rank, last - first))
        lifted = lifted + dot(
            far, other_ref[:, :, first:last].reshape(line * rank, last - first)
        )
        out_ref[:, first:last] = (inverse * base_ref[:, first:last] + lifted).astype(jnp.bfloat16)


def lift(slot, low_parts, base, up_line, up_other, rank, head_dim, model_width):
    return pl.pallas_call(
        functools.partial(lift_kernel, rank, head_dim, model_width),
        out_shape=jax.ShapeDtypeStruct(base.shape, jnp.bfloat16),
        in_specs=[pl.BlockSpec(memory_space=pltpu.VMEM)] * 5,
        out_specs=pl.BlockSpec(memory_space=pltpu.VMEM),
        compiler_params=pltpu.CompilerParams(vmem_limit_bytes=16 * 1024 * 1024),
        cost_estimate=pl.CostEstimate(
            flops=2 * base.size * up_line.shape[0] * 2 * rank,
            bytes_accessed=2_000_000,
            transcendentals=0,
        ),
    )(slot, low_parts, up_line, up_other, base)


def attend(queries, cache_keys, value_cache, fresh_keys, fresh_values, lengths, query_steps):
    scaling = 1.0 / math.sqrt(queries.shape[-1])
    old_scores = (
        jnp.einsum("rnd,rjd->rnj", queries, cache_keys, preferred_element_type=jnp.float32)
        * scaling
    )
    new_scores = (
        jnp.einsum("rnd,rjd->rnj", queries, fresh_keys, preferred_element_type=jnp.float32)
        * scaling
    )
    visible = jnp.arange(cache_keys.shape[1])[None, None, :] < lengths[:, None, None]
    old_scores = jnp.where(visible, old_scores, -1e30)
    fresh = jnp.arange(fresh_keys.shape[1])[None, None, :] <= query_steps[None, :, None]
    new_scores = jnp.where(fresh, new_scores, -1e30)
    highest = jnp.maximum(jnp.max(old_scores, axis=-1), jnp.max(new_scores, axis=-1))[..., None]
    old_exp = jnp.exp(old_scores - highest)
    new_exp = jnp.exp(new_scores - highest)
    denominator = jnp.sum(old_exp, axis=-1, keepdims=True) + jnp.sum(
        new_exp, axis=-1, keepdims=True
    )
    old_weights = (old_exp / denominator).astype(jnp.bfloat16)
    new_weights = (new_exp / denominator).astype(jnp.bfloat16)
    mixed = jnp.einsum(
        "rnj,rjd->rnd", old_weights, value_cache, preferred_element_type=jnp.float32
    )
    mixed = mixed + jnp.einsum(
        "rnj,rjd->rnd", new_weights, fresh_values, preferred_element_type=jnp.float32
    )
    return mixed.astype(jnp.bfloat16)


def on_device(
    inputs,
    gain,
    w_query,
    key_projection_weight,
    value_projection_weight,
    w_output,
    adapter_in,
    adapter_attn,
    adapter_out,
    pool_query,
    slot_keyvalue_matrices,
    cache_keys,
    value_cache,
    tasks,
    homes,
    moves,
    lengths,
):
    steps, all_rows, width_part = inputs.shape
    own_rows = lengths.shape[0]
    groups = all_rows // own_rows
    planes = lax.axis_size(PLANE)
    line = lax.axis_size("x")
    depth = lax.axis_size("z")
    task_count = homes.shape[0]
    rank = adapter_out.shape[1]
    head_dim = cache_keys.shape[3]
    query_width = w_query.shape[1]
    heads = query_width // head_dim
    key_end = query_width + head_dim
    base_end = key_end + head_dim
    per_group = steps * own_rows
    every_row = groups * per_group
    model_width = width_part * groups
    column_rows = depth * per_group

    group_tasks = tasks.reshape(groups, own_rows)
    matched = moves[:, 1][None, :] == jnp.arange(groups, dtype=jnp.int32)[:, None]
    moved = jnp.any(matched, axis=1)
    chosen = jnp.sum(jnp.where(matched, moves[:, 0][None, :], 0), axis=1)
    late = jnp.where(moved[:, None], chosen[:, None], group_tasks)
    active = jnp.stack([group_tasks if s < steps // 2 else late for s in range(steps)], axis=1)
    active = active.reshape(every_row)
    marks = active[:, None] == jnp.arange(task_count, dtype=jnp.int32)[None, :]
    row_home = jnp.sum(jnp.where(marks, homes[None, :], 0), axis=1)

    up = jnp.concatenate(
        [
            pool_query.reshape(rank, query_width),
            slot_keyvalue_matrices.reshape(rank, 2 * head_dim),
        ],
        axis=1,
    )
    with jax.named_scope("up_x"):
        up_line = exchange(
            jnp.broadcast_to(up[None], (line, rank, base_end)), "x"
        )

    partial = project(
        inputs,
        gain,
        w_query,
        key_projection_weight,
        value_projection_weight,
        adapter_in,
        tasks,
        moves,
        own_rows,
    )
    partial, up_line = lax.optimization_barrier((partial, up_line))
    with jax.named_scope("sum_plane"):
        by_plane = exchange(partial.reshape(planes, column_rows, -1), PLANE)

    up_line, by_plane = lax.optimization_barrier((up_line, by_plane))
    with jax.named_scope("up_y_lo"):
        up_other = lax.ppermute(up_line, "y_lo", [(0, 1), (1, 0)])

    low_part = sum_low(by_plane, base_end, 3 * rank, depth)
    plane_sum = jnp.sum(by_plane[:, :, :base_end].astype(jnp.float32), axis=0)
    with jax.named_scope("sum_low"):
        low_parts = exchange(low_part, "z")

    x, y_lo, z = (lax.axis_index(name) for name in GROUP)
    column_home = lax.dynamic_slice_in_dim(
        row_home, (x * 2 + y_lo) * column_rows, column_rows, 0
    )
    home_x = column_home // (2 * depth)
    other_half = jnp.where(column_home // depth % 2 == y_lo, 0, line)
    slot = jnp.where(column_home % depth == z, home_x + other_half, -1)
    raw_part = lift(
        slot[:, None], low_parts, plane_sum, up_line, up_other, rank, head_dim, model_width
    )
    with jax.named_scope("sum_z"):
        by_depth = exchange(raw_part.reshape(depth, per_group, base_end), "z")
    raw = jnp.sum(by_depth.astype(jnp.float32), axis=0)

    row_step = jnp.arange(per_group) // own_rows
    positions = jnp.tile(lengths, steps) + row_step
    queries = apply_rotary(raw[:, :query_width].reshape(per_group, heads, head_dim), positions)
    new_keys = apply_rotary(
        raw[:, query_width:key_end].reshape(per_group, 1, head_dim), positions
    )
    raw_value = raw[:, key_end:]

    def by_row(array):
        return (
            array.astype(jnp.bfloat16)
            .reshape(steps, own_rows, -1, head_dim)
            .transpose(1, 0, 2, 3)
            .reshape(own_rows, -1, head_dim)
        )

    attended = attend(
        by_row(queries),
        cache_keys.reshape(own_rows, -1, head_dim),
        value_cache.reshape(own_rows, -1, head_dim),
        by_row(new_keys),
        by_row(raw_value),
        lengths,
        jnp.arange(steps * heads) // heads,
    )
    attended = (
        attended.reshape(own_rows, steps, query_width)
        .transpose(1, 0, 2)
        .reshape(per_group, query_width)
    )

    with jax.named_scope("gather_z"):
        line = exchange(
            jnp.broadcast_to(attended[None], (depth, per_group, query_width)), "z"
        ).reshape(depth * per_group, query_width)
    with jax.named_scope("gather_plane"):
        piece_rows = exchange(
            jnp.broadcast_to(line[None], (planes, depth * per_group, query_width)), PLANE
        ).reshape(every_row, query_width)

    every_reduced = jnp.einsum(
        "rq,tqc->rtc", piece_rows, adapter_attn, preferred_element_type=jnp.float32
    )
    reduced = jnp.where(marks[:, :, None], every_reduced, 0).astype(jnp.bfloat16)
    mixed = dot(piece_rows, w_output) + dot(
        reduced.reshape(every_row, task_count * rank),
        adapter_out.reshape(task_count * rank, width_part),
    )
    mixed = mixed.astype(jnp.bfloat16)
    core = lax.axis_index("core")
    cores = lax.axis_size("core")
    half = steps // cores
    with jax.named_scope("sum_core"):
        pair = lax.all_gather(mixed, "core", axis=0)
    mine = lax.dynamic_slice_in_dim(
        pair.reshape(cores, groups, steps, own_rows, width_part), core * half, half, 2
    ).astype(jnp.float32)
    mine = jnp.sum(mine, axis=0).astype(jnp.bfloat16)
    mine = mine.transpose(1, 0, 2, 3).reshape(half, all_rows, width_part)
    y_his = lax.axis_size("y_hi")
    with jax.named_scope("sum_y_hi"):
        mine = exchange(
            jnp.broadcast_to(mine[None], (y_his, half, all_rows, width_part)).reshape(
                y_his * half, all_rows, width_part
            ),
            "y_hi",
        )
    mine = jnp.sum(
        mine.reshape(y_his, half, all_rows, width_part).astype(jnp.float32), axis=0
    )
    residual = lax.dynamic_slice_in_dim(inputs, core * half, half, 0)
    finished = (residual.astype(jnp.float32) + mine).astype(jnp.bfloat16)
    with jax.named_scope("gather_core"):
        return lax.all_gather(finished, "core", axis=0, tiled=True)


def solution(mesh):
    parts = Mesh(mesh.devices.reshape(4, 2, 8, 4, 2), GROUP + TENSOR)
    return jax.shard_map(
        on_device,
        mesh=parts,
        in_specs=(
            P(None, None, GROUP),
            P(GROUP),
            P(GROUP, TENSOR),
            P(GROUP, TENSOR),
            P(GROUP, TENSOR),
            P(TENSOR, GROUP),
            P(None, GROUP, None),
            P(None, TENSOR, None),
            P(None, None, GROUP),
            P(GROUP, None, TENSOR),
            P(GROUP, None, None, TENSOR),
            P(GROUP, TENSOR, None, None),
            P(GROUP, TENSOR, None, None),
            P(),
            P(),
            P(),
            P(GROUP),
        ),
        out_specs=P(None, None, GROUP),
        check_vma=False,
    )
```

```python
import functools
import math

import jax
import jax.numpy as jnp
from jax import lax
from jax.experimental import pallas as pl
from jax.experimental.pallas import tpu as pltpu
from jax.sharding import Mesh
from jax.sharding import PartitionSpec as P

epsilon = 1e-05
GROUP = ("x", "y_lo", "z")
PLANE = ("x", "y_lo")
TENSOR = ("y_hi", "core")
PADDED_WIDTH = 256


def exchange(blocks, axes):
    return lax.all_to_all(blocks, axes, 0, 0, tiled=True)


def apply_rotary(vectors, token_positions):
    half_width = vectors.shape[-1] // 2
    frequency = jnp.exp(
        -jnp.log(500000.0) * jnp.arange(half_width, dtype=jnp.float32) * (2.0 / vectors.shape[-1])
    )
    angles = token_positions.astype(jnp.float32)[:, None] * frequency[None, :]
    cosine = jnp.cos(angles)[:, None, :]
    sine_part = jnp.sin(angles)[:, None, :]
    leading = vectors[..., :half_width]
    trailing = vectors[..., half_width:]
    return jnp.concatenate(
        [leading * cosine - trailing * sine_part, leading * sine_part + trailing * cosine], axis=-1
    )


def dot(left, right):
    return jnp.dot(left, right, preferred_element_type=jnp.float32)


def start_copies(pairs, arrived):
    copies = [
        pltpu.make_async_copy(source, held, arrived.at[number])
        for number, (source, held) in enumerate(pairs)
    ]
    for copy in copies:
        copy.start()
    return copies


def project_kernel(
    own_rows,
    gain_ref,
    tasks_ref,
    moves_ref,
    inputs_ref,
    adapter_ref,
    query_ref,
    key_ref,
    value_ref,
    out_ref,
    held_inputs,
    held_adapter,
    held_query,
    held_key,
    held_value,
    gained_ref,
    arrived,
):
    steps, all_rows, width = inputs_ref.shape
    every_row = steps * all_rows
    per_group = steps * own_rows
    query_width = query_ref.shape[1]
    head_dim = key_ref.shape[1]
    adapters, low, _ = adapter_ref.shape
    key_end = query_width + head_dim
    base_end = key_end + head_dim
    block = 128
    copies = start_copies(
        (
            (inputs_ref, held_inputs),
            (adapter_ref, held_adapter),
            (query_ref, held_query),
            (key_ref, held_key),
            (value_ref, held_value),
        ),
        arrived,
    )

    def lane(width):
        return lax.broadcasted_iota(jnp.int32, (block, width), 1)

    copies[0].wait()
    gathered = held_inputs[...].reshape(every_row, width)
    squares_of = []
    for first in range(0, every_row, block):
        row = first + lax.broadcasted_iota(jnp.int32, (block, 1), 0)
        place = row % per_group // own_rows * all_rows + row // per_group * own_rows + row % own_rows
        order = jnp.where(lane(every_row) == place, 1.0, 0.0).astype(jnp.bfloat16)
        states = dot(order, gathered)
        gained_ref[first : first + block, :] = (states * gain_ref[...]).astype(jnp.bfloat16)
        squares_of.append(jnp.sum(states * states, axis=1, keepdims=True))

    copies[1].wait()
    for index, squares in enumerate(squares_of):
        first = index * block

        row = first + lax.broadcasted_iota(jnp.int32, (block, 1), 0)
        own = lane(all_rows) == row // per_group * own_rows + row % own_rows
        task = jnp.sum(jnp.where(own, tasks_ref[...], 0), axis=1, keepdims=True)
        here = moves_ref[1:2, :] == row // per_group
        moved = jnp.sum(jnp.where(here, 1, 0), axis=1, keepdims=True) > 0
        chosen = jnp.sum(jnp.where(here, moves_ref[0:1, :], 0), axis=1, keepdims=True)
        late = row % per_group >= per_group // 2
        task = jnp.where(jnp.logical_and(late, moved), chosen, task)
        gained = gained_ref[first : first + block, :]
        total = jnp.zeros((block, low), jnp.float32)
        for adapter in range(0, adapters, 2):
            both = [
                jnp.where(task == number, gained, jnp.zeros_like(gained))
                for number in (adapter, adapter + 1)
            ]
            total = total + lax.dot_general(
                jnp.concatenate(both, axis=1),
                jnp.concatenate([held_adapter[adapter], held_adapter[adapter + 1]], axis=1),
                (((1,), (1,)), ((), ())),
                preferred_element_type=jnp.float32,
            )
        rest = PADDED_WIDTH - low
        squares_high = squares.astype(jnp.bfloat16).astype(jnp.float32)
        extra = jnp.where(
            lane(rest) == 0,
            squares_high,
            jnp.where(lane(rest) == 1, squares - squares_high, 0.0),
        )
        out_ref[first : first + block, base_end : base_end + PADDED_WIDTH] = jnp.concatenate(
            [total, extra], axis=1
        ).astype(jnp.bfloat16)

    for copy in copies[2:]:
        copy.wait()

    @pl.loop(0, every_row // block)
    def _(index):
        rows = pl.ds(pl.multiple_of(index * block, block), block)
        gained = gained_ref[rows, :]
        out_ref[rows, 0:query_width] = dot(gained, held_query[...]).astype(jnp.bfloat16)
        out_ref[rows, query_width:key_end] = dot(gained, held_key[...]).astype(jnp.bfloat16)
        out_ref[rows, key_end:base_end] = dot(gained, held_value[...]).astype(jnp.bfloat16)


def project(inputs, gain, w_query, w_key, w_value, adapter_in, tasks, moves, own_rows):
    steps, all_rows, width = inputs.shape
    columns = w_query.shape[1] + w_key.shape[1] + w_value.shape[1] + PADDED_WIDTH
    large = (inputs, jnp.swapaxes(adapter_in, 1, 2), w_query, w_key, w_value)
    return pl.pallas_call(
        functools.partial(project_kernel, own_rows),
        out_shape=jax.ShapeDtypeStruct((steps * all_rows, columns), jnp.bfloat16),
        in_specs=[pl.BlockSpec(memory_space=pltpu.VMEM)] * 3
        + [pl.BlockSpec(memory_space=pl.ANY)] * len(large),
        scratch_shapes=[pltpu.VMEM(array.shape, jnp.bfloat16) for array in large]
        + [
            pltpu.VMEM((steps * all_rows, width), jnp.bfloat16),
            pltpu.SemaphoreType.DMA((len(large),)),
        ],
        cost_estimate=pl.CostEstimate(
            flops=2 * steps * all_rows * width * 3328, bytes_accessed=3_000_000, transcendentals=0
        ),
    )(gain[None, :], tasks[None, :], moves.T, *large)


def low_kernel(low, parts_ref, low_ref):
    sources, rows, columns = parts_ref.shape
    targets, _, width = low_ref.shape
    total = parts_ref[0, :, columns - width :].astype(jnp.float32)
    for source in range(1, sources):
        total = total + parts_ref[source, :, columns - width :].astype(jnp.float32)
    lane = lax.broadcasted_iota(jnp.int32, total.shape, 1)
    squares = jnp.sum(jnp.where(lane >= low, total, 0.0), axis=1, keepdims=True)
    squares_high = squares.astype(jnp.bfloat16).astype(jnp.float32)
    total = jnp.where(
        lane < low,
        total,
        jnp.where(
            lane == low, squares_high, jnp.where(lane == low + 1, squares - squares_high, 0.0)
        ),
    ).astype(jnp.bfloat16)
    for target in range(targets):
        low_ref[target] = total


def sum_low(parts, base_end, low, depth):
    _, rows, columns = parts.shape
    return pl.pallas_call(
        functools.partial(low_kernel, low),
        out_shape=jax.ShapeDtypeStruct((depth, rows, columns - base_end), jnp.bfloat16),
        in_specs=[pl.BlockSpec(memory_space=pltpu.VMEM)],
        out_specs=pl.BlockSpec(memory_space=pltpu.VMEM),
        compiler_params=pltpu.CompilerParams(vmem_limit_bytes=16 * 1024 * 1024),
        cost_estimate=pl.CostEstimate(
            flops=parts.size // 6, bytes_accessed=parts.size // 3, transcendentals=0
        ),
    )(parts)


def lift_kernel(
    rank,
    head_dim,
    model_width,
    slot_ref,
    low_ref,
    line_ref,
    other_ref,
    base_ref,
    out_ref,
):
    rows, columns = out_ref.shape
    line = line_ref.shape[0]
    low = 3 * rank
    total = low_ref[0].astype(jnp.float32)
    for source in range(1, low_ref.shape[0]):
        total = total + low_ref[source].astype(jnp.float32)
    lane = lax.broadcasted_iota(jnp.int32, total.shape, 1)
    squares = jnp.sum(jnp.where(lane >= low, total, 0.0), axis=1, keepdims=True)
    inverse = lax.rsqrt(squares / model_width + epsilon)
    lowrank = (inverse * total).astype(jnp.bfloat16)
    from_lane = lax.broadcasted_iota(jnp.int32, (PADDED_WIDTH, line * rank), 0)
    to_lane = lax.broadcasted_iota(jnp.int32, (PADDED_WIDTH, line * rank), 1)
    slot_lane = lax.broadcasted_iota(jnp.int32, (rows, line * rank), 1) // rank
    slot = slot_ref[...]
    spreads = []
    for number in range(3):
        pick = jnp.where(from_lane == number * rank + to_lane % rank, 1.0, 0.0)
        tiled = dot(lowrank, pick.astype(jnp.bfloat16))
        spreads.append(
            [
                jnp.where(slot == slot_lane + half * line, tiled, 0.0).astype(jnp.bfloat16)
                for half in range(2)
            ]
        )
    key_first, value_first = columns - 2 * head_dim, columns - head_dim
    bounds = ((0, key_first), (key_first, value_first), (value_first, columns))
    for (first, last), (near, far) in zip(bounds, spreads, strict=True):
        lifted = dot(near, line_ref[:, :, first:last].reshape(line * rank, last - first))
        lifted = lifted + dot(
            far, other_ref[:, :, first:last].reshape(line * rank, last - first)
        )
        out_ref[:, first:last] = (inverse * base_ref[:, first:last] + lifted).astype(jnp.bfloat16)


def lift(slot, low_parts, base, up_line, up_other, rank, head_dim, model_width):
    return pl.pallas_call(
        functools.partial(lift_kernel, rank, head_dim, model_width),
        out_shape=jax.ShapeDtypeStruct(base.shape, jnp.bfloat16),
        in_specs=[pl.BlockSpec(memory_space=pltpu.VMEM)] * 5,
        out_specs=pl.BlockSpec(memory_space=pltpu.VMEM),
        compiler_params=pltpu.CompilerParams(vmem_limit_bytes=16 * 1024 * 1024),
        cost_estimate=pl.CostEstimate(
            flops=2 * base.size * up_line.shape[0] * 2 * rank,
            bytes_accessed=2_000_000,
            transcendentals=0,
        ),
    )(slot, low_parts, up_line, up_other, base)


def attend(queries, cache_keys, value_cache, fresh_keys, fresh_values, lengths, query_steps):
    scaling = 1.0 / math.sqrt(queries.shape[-1])
    old_scores = (
        jnp.einsum("rnd,rjd->rnj", queries, cache_keys, preferred_element_type=jnp.float32)
        * scaling
    )
    new_scores = (
        jnp.einsum("rnd,rjd->rnj", queries, fresh_keys, preferred_element_type=jnp.float32)
        * scaling
    )
    visible = jnp.arange(cache_keys.shape[1])[None, None, :] < lengths[:, None, None]
    old_scores = jnp.where(visible, old_scores, -1e30)
    fresh = jnp.arange(fresh_keys.shape[1])[None, None, :] <= query_steps[None, :, None]
    new_scores = jnp.where(fresh, new_scores, -1e30)
    highest = jnp.maximum(jnp.max(old_scores, axis=-1), jnp.max(new_scores, axis=-1))[..., None]
    old_exp = jnp.exp(old_scores - highest)
    new_exp = jnp.exp(new_scores - highest)
    denominator = jnp.sum(old_exp, axis=-1, keepdims=True) + jnp.sum(
        new_exp, axis=-1, keepdims=True
    )
    old_weights = (old_exp / denominator).astype(jnp.bfloat16)
    new_weights = (new_exp / denominator).astype(jnp.bfloat16)
    mixed = jnp.einsum(
        "rnj,rjd->rnd", old_weights, value_cache, preferred_element_type=jnp.float32
    )
    mixed = mixed + jnp.einsum(
        "rnj,rjd->rnd", new_weights, fresh_values, preferred_element_type=jnp.float32
    )
    return mixed.astype(jnp.bfloat16)


def on_device(
    inputs,
    gain,
    w_query,
    key_projection_weight,
    value_projection_weight,
    w_output,
    adapter_in,
    adapter_attn,
    adapter_out,
    pool_query,
    slot_keyvalue_matrices,
    cache_keys,
    value_cache,
    tasks,
    homes,
    moves,
    lengths,
):
    steps, all_rows, width_part = inputs.shape
    own_rows = lengths.shape[0]
    groups = all_rows // own_rows
    planes = lax.axis_size(PLANE)
    line = lax.axis_size("x")
    depth = lax.axis_size("z")
    task_count = homes.shape[0]
    rank = adapter_out.shape[1]
    head_dim = cache_keys.shape[3]
    query_width = w_query.shape[1]
    heads = query_width // head_dim
    key_end = query_width + head_dim
    base_end = key_end + head_dim
    per_group = steps * own_rows
    every_row = groups * per_group
    model_width = width_part * groups
    column_rows = depth * per_group

    group_tasks = tasks.reshape(groups, own_rows)
    matched = moves[:, 1][None, :] == jnp.arange(groups, dtype=jnp.int32)[:, None]
    moved = jnp.any(matched, axis=1)
    chosen = jnp.sum(jnp.where(matched, moves[:, 0][None, :], 0), axis=1)
    late = jnp.where(moved[:, None], chosen[:, None], group_tasks)
    active = jnp.stack([group_tasks if s < steps // 2 else late for s in range(steps)], axis=1)
    active = active.reshape(every_row)
    marks = active[:, None] == jnp.arange(task_count, dtype=jnp.int32)[None, :]
    row_home = jnp.sum(jnp.where(marks, homes[None, :], 0), axis=1)

    partial = project(
        inputs,
        gain,
        w_query,
        key_projection_weight,
        value_projection_weight,
        adapter_in,
        tasks,
        moves,
        own_rows,
    )
    partial, pool_query, slot_keyvalue_matrices = lax.optimization_barrier(
        (partial, pool_query, slot_keyvalue_matrices)
    )
    with jax.named_scope("sum_plane"):
        by_plane = exchange(partial.reshape(planes, column_rows, -1), PLANE)

    up = jnp.concatenate(
        [
            pool_query.reshape(rank, query_width),
            slot_keyvalue_matrices.reshape(rank, 2 * head_dim),
        ],
        axis=1,
    )
    with jax.named_scope("up_x"):
        ahead = [(i, (i + 1) % line) for i in range(line)]
        back = [(i, (i - 1) % line) for i in range(line)]
        across = [(i, (i + 2) % line) for i in range(line)]
        from_left = lax.ppermute(up, "x", ahead)
        from_right = lax.ppermute(up, "x", back)
        from_far = lax.ppermute(up, "x", across)
        up_line = jnp.stack([up, from_left, from_right, from_far])
    with jax.named_scope("up_y_lo"):
        up_other = lax.ppermute(up_line, "y_lo", [(0, 1), (1, 0)])
    low_part = sum_low(by_plane, base_end, 3 * rank, depth)
    plane_sum = jnp.sum(by_plane[:, :, :base_end].astype(jnp.float32), axis=0)
    with jax.named_scope("sum_low"):
        low_parts = exchange(low_part, "z")

    x, y_lo, z = (lax.axis_index(name) for name in GROUP)
    column_home = lax.dynamic_slice_in_dim(
        row_home, (x * 2 + y_lo) * column_rows, column_rows, 0
    )
    offset = (column_home // (2 * depth) - x) % line
    near_slot = jnp.where(offset == line - 1, 1, jnp.where(offset == 0, 0, offset + 1))
    other_half = jnp.where(column_home // depth % 2 == y_lo, 0, line)
    slot = jnp.where(column_home % depth == z, near_slot + other_half, -1)
    raw_part = lift(
        slot[:, None], low_parts, plane_sum, up_line, up_other, rank, head_dim, model_width
    )
    with jax.named_scope("sum_z"):
        by_depth = exchange(raw_part.reshape(depth, per_group, base_end), "z")
    raw = jnp.sum(by_depth.astype(jnp.float32), axis=0)

    row_step = jnp.arange(per_group) // own_rows
    positions = jnp.tile(lengths, steps) + row_step
    queries = apply_rotary(raw[:, :query_width].reshape(per_group, heads, head_dim), positions)
    new_keys = apply_rotary(
        raw[:, query_width:key_end].reshape(per_group, 1, head_dim), positions
    )
    raw_value = raw[:, key_end:]

    def by_row(array):
        return (
            array.astype(jnp.bfloat16)
            .reshape(steps, own_rows, -1, head_dim)
            .transpose(1, 0, 2, 3)
            .reshape(own_rows, -1, head_dim)
        )

    attended = attend(
        by_row(queries),
        cache_keys.reshape(own_rows, -1, head_dim),
        value_cache.reshape(own_rows, -1, head_dim),
        by_row(new_keys),
        by_row(raw_value),
        lengths,
        jnp.arange(steps * heads) // heads,
    )
    attended = (
        attended.reshape(own_rows, steps, query_width)
        .transpose(1, 0, 2)
        .reshape(per_group, query_width)
    )

    with jax.named_scope("gather_z"):
        line = exchange(
            jnp.broadcast_to(attended[None], (depth, per_group, query_width)), "z"
        ).reshape(depth * per_group, query_width)
    with jax.named_scope("gather_plane"):
        piece_rows = exchange(
            jnp.broadcast_to(line[None], (planes, depth * per_group, query_width)), PLANE
        ).reshape(every_row, query_width)

    every_reduced = jnp.einsum(
        "rq,tqc->rtc", piece_rows, adapter_attn, preferred_element_type=jnp.float32
    )
    reduced = jnp.where(marks[:, :, None], every_reduced, 0).astype(jnp.bfloat16)
    mixed = dot(piece_rows, w_output) + dot(
        reduced.reshape(every_row, task_count * rank),
        adapter_out.reshape(task_count * rank, width_part),
    )
    mixed = mixed.astype(jnp.bfloat16)
    core = lax.axis_index("core")
    cores = lax.axis_size("core")
    half = steps // cores
    with jax.named_scope("sum_core"):
        pair = lax.all_gather(mixed, "core", axis=0)
    mine = lax.dynamic_slice_in_dim(
        pair.reshape(cores, groups, steps, own_rows, width_part), core * half, half, 2
    ).astype(jnp.float32)
    mine = jnp.sum(mine, axis=0).astype(jnp.bfloat16)
    mine = mine.transpose(1, 0, 2, 3).reshape(half, all_rows, width_part)
    y_his = lax.axis_size("y_hi")
    with jax.named_scope("sum_y_hi"):
        mine = exchange(
            jnp.broadcast_to(mine[None], (y_his, half, all_rows, width_part)).reshape(
                y_his * half, all_rows, width_part
            ),
            "y_hi",
        )
    mine = jnp.sum(
        mine.reshape(y_his, half, all_rows, width_part).astype(jnp.float32), axis=0
    )
    residual = lax.dynamic_slice_in_dim(inputs, core * half, half, 0)
    finished = (residual.astype(jnp.float32) + mine).astype(jnp.bfloat16)
    with jax.named_scope("gather_core"):
        return lax.all_gather(finished, "core", axis=0, tiled=True)


def solution(mesh):
    parts = Mesh(mesh.devices.reshape(4, 2, 8, 4, 2), GROUP + TENSOR)
    return jax.shard_map(
        on_device,
        mesh=parts,
        in_specs=(
            P(None, None, GROUP),
            P(GROUP),
            P(GROUP, TENSOR),
            P(GROUP, TENSOR),
            P(GROUP, TENSOR),
            P(TENSOR, GROUP),
            P(None, GROUP, None),
            P(None, TENSOR, None),
            P(None, None, GROUP),
            P(GROUP, None, TENSOR),
            P(GROUP, None, None, TENSOR),
            P(GROUP, TENSOR, None, None),
            P(GROUP, TENSOR, None, None),
            P(),
            P(),
            P(),
            P(GROUP),
        ),
        out_specs=P(None, None, GROUP),
        check_vma=False,
    )
```

```python
import functools
import math

import jax
import jax.numpy as jnp
from jax import lax
from jax.experimental import pallas as pl
from jax.experimental.pallas import tpu as pltpu
from jax.sharding import Mesh
from jax.sharding import PartitionSpec as P

epsilon = 1e-05
GROUP = ("x", "y_lo", "z")
PLANE = ("x", "y_lo")
TENSOR = ("y_hi", "core")
PADDED_WIDTH = 256


def exchange(blocks, axes):
    return lax.all_to_all(blocks, axes, 0, 0, tiled=True)


def apply_rotary(vectors, token_positions):
    half_width = vectors.shape[-1] // 2
    frequency = jnp.exp(
        -jnp.log(500000.0) * jnp.arange(half_width, dtype=jnp.float32) * (2.0 / vectors.shape[-1])
    )
    angles = token_positions.astype(jnp.float32)[:, None] * frequency[None, :]
    cosine = jnp.cos(angles)[:, None, :]
    sine_part = jnp.sin(angles)[:, None, :]
    leading = vectors[..., :half_width]
    trailing = vectors[..., half_width:]
    return jnp.concatenate(
        [leading * cosine - trailing * sine_part, leading * sine_part + trailing * cosine], axis=-1
    )


def dot(left, right):
    return jnp.dot(left, right, preferred_element_type=jnp.float32)


def start_copies(pairs, arrived):
    copies = [
        pltpu.make_async_copy(source, held, arrived.at[number])
        for number, (source, held) in enumerate(pairs)
    ]
    for copy in copies:
        copy.start()
    return copies


def project_kernel(
    own_rows,
    gain_ref,
    tasks_ref,
    moves_ref,
    inputs_ref,
    adapter_ref,
    query_ref,
    key_ref,
    value_ref,
    out_ref,
    held_inputs,
    held_adapter,
    held_query,
    held_key,
    held_value,
    gained_ref,
    arrived,
):
    steps, all_rows, width = inputs_ref.shape
    every_row = steps * all_rows
    per_group = steps * own_rows
    query_width = query_ref.shape[1]
    head_dim = key_ref.shape[1]
    adapters, low, _ = adapter_ref.shape
    key_end = query_width + head_dim
    base_end = key_end + head_dim
    block = 128
    copies = start_copies(
        (
            (inputs_ref, held_inputs),
            (adapter_ref, held_adapter),
            (query_ref, held_query),
            (key_ref, held_key),
            (value_ref, held_value),
        ),
        arrived,
    )

    def lane(width):
        return lax.broadcasted_iota(jnp.int32, (block, width), 1)

    copies[0].wait()
    gathered = held_inputs[...].reshape(every_row, width)
    squares_of = []
    for first in range(0, every_row, block):
        row = first + lax.broadcasted_iota(jnp.int32, (block, 1), 0)
        place = row % per_group // own_rows * all_rows + row // per_group * own_rows + row % own_rows
        order = jnp.where(lane(every_row) == place, 1.0, 0.0).astype(jnp.bfloat16)
        states = dot(order, gathered)
        gained_ref[first : first + block, :] = (states * gain_ref[...]).astype(jnp.bfloat16)
        squares_of.append(jnp.sum(states * states, axis=1, keepdims=True))

    copies[1].wait()
    for index, squares in enumerate(squares_of):
        first = index * block

        row = first + lax.broadcasted_iota(jnp.int32, (block, 1), 0)
        own = lane(all_rows) == row // per_group * own_rows + row % own_rows
        task = jnp.sum(jnp.where(own, tasks_ref[...], 0), axis=1, keepdims=True)
        here = moves_ref[1:2, :] == row // per_group
        moved = jnp.sum(jnp.where(here, 1, 0), axis=1, keepdims=True) > 0
        chosen = jnp.sum(jnp.where(here, moves_ref[0:1, :], 0), axis=1, keepdims=True)
        late = row % per_group >= per_group // 2
        task = jnp.where(jnp.logical_and(late, moved), chosen, task)
        gained = gained_ref[first : first + block, :]
        total = jnp.zeros((block, low), jnp.float32)
        for adapter in range(0, adapters, 2):
            both = [
                jnp.where(task == number, gained, jnp.zeros_like(gained))
                for number in (adapter, adapter + 1)
            ]
            total = total + lax.dot_general(
                jnp.concatenate(both, axis=1),
                jnp.concatenate([held_adapter[adapter], held_adapter[adapter + 1]], axis=1),
                (((1,), (1,)), ((), ())),
                preferred_element_type=jnp.float32,
            )
        rest = PADDED_WIDTH - low
        squares_high = squares.astype(jnp.bfloat16).astype(jnp.float32)
        extra = jnp.where(
            lane(rest) == 0,
            squares_high,
            jnp.where(lane(rest) == 1, squares - squares_high, 0.0),
        )
        out_ref[first : first + block, base_end : base_end + PADDED_WIDTH] = jnp.concatenate(
            [total, extra], axis=1
        ).astype(jnp.bfloat16)

    for copy in copies[2:]:
        copy.wait()

    @pl.loop(0, every_row // block)
    def _(index):
        rows = pl.ds(pl.multiple_of(index * block, block), block)
        gained = gained_ref[rows, :]
        out_ref[rows, 0:query_width] = dot(gained, held_query[...]).astype(jnp.bfloat16)
        out_ref[rows, query_width:key_end] = dot(gained, held_key[...]).astype(jnp.bfloat16)
        out_ref[rows, key_end:base_end] = dot(gained, held_value[...]).astype(jnp.bfloat16)


def project(inputs, gain, w_query, w_key, w_value, adapter_in, tasks, moves, own_rows):
    steps, all_rows, width = inputs.shape
    columns = w_query.shape[1] + w_key.shape[1] + w_value.shape[1] + PADDED_WIDTH
    large = (inputs, jnp.swapaxes(adapter_in, 1, 2), w_query, w_key, w_value)
    return pl.pallas_call(
        functools.partial(project_kernel, own_rows),
        out_shape=jax.ShapeDtypeStruct((steps * all_rows, columns), jnp.bfloat16),
        in_specs=[pl.BlockSpec(memory_space=pltpu.VMEM)] * 3
        + [pl.BlockSpec(memory_space=pl.ANY)] * len(large),
        scratch_shapes=[pltpu.VMEM(array.shape, jnp.bfloat16) for array in large]
        + [
            pltpu.VMEM((steps * all_rows, width), jnp.bfloat16),
            pltpu.SemaphoreType.DMA((len(large),)),
        ],
        cost_estimate=pl.CostEstimate(
            flops=2 * steps * all_rows * width * 3328, bytes_accessed=3_000_000, transcendentals=0
        ),
    )(gain[None, :], tasks[None, :], moves.T, *large)


def low_kernel(low, parts_ref, low_ref):
    sources, rows, columns = parts_ref.shape
    targets, _, width = low_ref.shape
    total = parts_ref[0, :, columns - width :].astype(jnp.float32)
    for source in range(1, sources):
        total = total + parts_ref[source, :, columns - width :].astype(jnp.float32)
    lane = lax.broadcasted_iota(jnp.int32, total.shape, 1)
    squares = jnp.sum(jnp.where(lane >= low, total, 0.0), axis=1, keepdims=True)
    squares_high = squares.astype(jnp.bfloat16).astype(jnp.float32)
    total = jnp.where(
        lane < low,
        total,
        jnp.where(
            lane == low, squares_high, jnp.where(lane == low + 1, squares - squares_high, 0.0)
        ),
    ).astype(jnp.bfloat16)
    for target in range(targets):
        low_ref[target] = total


def sum_low(parts, base_end, low, depth):
    _, rows, columns = parts.shape
    return pl.pallas_call(
        functools.partial(low_kernel, low),
        out_shape=jax.ShapeDtypeStruct((depth, rows, columns - base_end), jnp.bfloat16),
        in_specs=[pl.BlockSpec(memory_space=pltpu.VMEM)],
        out_specs=pl.BlockSpec(memory_space=pltpu.VMEM),
        compiler_params=pltpu.CompilerParams(vmem_limit_bytes=16 * 1024 * 1024),
        cost_estimate=pl.CostEstimate(
            flops=parts.size // 6, bytes_accessed=parts.size // 3, transcendentals=0
        ),
    )(parts)


def lift_kernel(
    rank,
    head_dim,
    model_width,
    slot_ref,
    low_ref,
    line_ref,
    other_ref,
    base_ref,
    out_ref,
):
    rows, columns = out_ref.shape
    line = line_ref.shape[0]
    low = 3 * rank
    total = low_ref[0].astype(jnp.float32)
    for source in range(1, low_ref.shape[0]):
        total = total + low_ref[source].astype(jnp.float32)
    lane = lax.broadcasted_iota(jnp.int32, total.shape, 1)
    squares = jnp.sum(jnp.where(lane >= low, total, 0.0), axis=1, keepdims=True)
    inverse = lax.rsqrt(squares / model_width + epsilon)
    lowrank = (inverse * total).astype(jnp.bfloat16)
    from_lane = lax.broadcasted_iota(jnp.int32, (PADDED_WIDTH, line * rank), 0)
    to_lane = lax.broadcasted_iota(jnp.int32, (PADDED_WIDTH, line * rank), 1)
    slot_lane = lax.broadcasted_iota(jnp.int32, (rows, line * rank), 1) // rank
    slot = slot_ref[...]
    spreads = []
    for number in range(3):
        pick = jnp.where(from_lane == number * rank + to_lane % rank, 1.0, 0.0)
        tiled = dot(lowrank, pick.astype(jnp.bfloat16))
        spreads.append(
            [
                jnp.where(slot == slot_lane + half * line, tiled, 0.0).astype(jnp.bfloat16)
                for half in range(2)
            ]
        )
    key_first, value_first = columns - 2 * head_dim, columns - head_dim
    bounds = ((0, key_first), (key_first, value_first), (value_first, columns))
    for (first, last), (near, far) in zip(bounds, spreads, strict=True):
        lifted = dot(near, line_ref[:, :, first:last].reshape(line * rank, last - first))
        lifted = lifted + dot(
            far, other_ref[:, :, first:last].reshape(line * rank, last - first)
        )
        out_ref[:, first:last] = (inverse * base_ref[:, first:last] + lifted).astype(jnp.bfloat16)


def lift(slot, low_parts, base, up_line, up_other, rank, head_dim, model_width):
    return pl.pallas_call(
        functools.partial(lift_kernel, rank, head_dim, model_width),
        out_shape=jax.ShapeDtypeStruct(base.shape, jnp.bfloat16),
        in_specs=[pl.BlockSpec(memory_space=pltpu.VMEM)] * 5,
        out_specs=pl.BlockSpec(memory_space=pltpu.VMEM),
        compiler_params=pltpu.CompilerParams(vmem_limit_bytes=16 * 1024 * 1024),
        cost_estimate=pl.CostEstimate(
            flops=2 * base.size * up_line.shape[0] * 2 * rank,
            bytes_accessed=2_000_000,
            transcendentals=0,
        ),
    )(slot, low_parts, up_line, up_other, base)


def attend(queries, cache_keys, value_cache, fresh_keys, fresh_values, lengths, query_steps):
    scaling = 1.0 / math.sqrt(queries.shape[-1])
    old_scores = (
        jnp.einsum("rnd,rjd->rnj", queries, cache_keys, preferred_element_type=jnp.float32)
        * scaling
    )
    new_scores = (
        jnp.einsum("rnd,rjd->rnj", queries, fresh_keys, preferred_element_type=jnp.float32)
        * scaling
    )
    visible = jnp.arange(cache_keys.shape[1])[None, None, :] < lengths[:, None, None]
    old_scores = jnp.where(visible, old_scores, -1e30)
    fresh = jnp.arange(fresh_keys.shape[1])[None, None, :] <= query_steps[None, :, None]
    new_scores = jnp.where(fresh, new_scores, -1e30)
    highest = jnp.maximum(jnp.max(old_scores, axis=-1), jnp.max(new_scores, axis=-1))[..., None]
    old_exp = jnp.exp(old_scores - highest)
    new_exp = jnp.exp(new_scores - highest)
    denominator = jnp.sum(old_exp, axis=-1, keepdims=True) + jnp.sum(
        new_exp, axis=-1, keepdims=True
    )
    old_weights = (old_exp / denominator).astype(jnp.bfloat16)
    new_weights = (new_exp / denominator).astype(jnp.bfloat16)
    mixed = jnp.einsum(
        "rnj,rjd->rnd", old_weights, value_cache, preferred_element_type=jnp.float32
    )
    mixed = mixed + jnp.einsum(
        "rnj,rjd->rnd", new_weights, fresh_values, preferred_element_type=jnp.float32
    )
    return mixed.astype(jnp.bfloat16)


def on_device(
    inputs,
    gain,
    w_query,
    key_projection_weight,
    value_projection_weight,
    w_output,
    adapter_in,
    adapter_attn,
    adapter_out,
    pool_query,
    slot_keyvalue_matrices,
    cache_keys,
    value_cache,
    tasks,
    homes,
    moves,
    lengths,
):
    steps, all_rows, width_part = inputs.shape
    own_rows = lengths.shape[0]
    groups = all_rows // own_rows
    planes = lax.axis_size(PLANE)
    line = lax.axis_size("x")
    depth = lax.axis_size("z")
    task_count = homes.shape[0]
    rank = adapter_out.shape[1]
    head_dim = cache_keys.shape[3]
    query_width = w_query.shape[1]
    heads = query_width // head_dim
    key_end = query_width + head_dim
    base_end = key_end + head_dim
    per_group = steps * own_rows
    every_row = groups * per_group
    model_width = width_part * groups
    column_rows = depth * per_group

    group_tasks = tasks.reshape(groups, own_rows)
    matched = moves[:, 1][None, :] == jnp.arange(groups, dtype=jnp.int32)[:, None]
    moved = jnp.any(matched, axis=1)
    chosen = jnp.sum(jnp.where(matched, moves[:, 0][None, :], 0), axis=1)
    late = jnp.where(moved[:, None], chosen[:, None], group_tasks)
    active = jnp.stack([group_tasks if s < steps // 2 else late for s in range(steps)], axis=1)
    active = active.reshape(every_row)
    marks = active[:, None] == jnp.arange(task_count, dtype=jnp.int32)[None, :]
    row_home = jnp.sum(jnp.where(marks, homes[None, :], 0), axis=1)

    partial = project(
        inputs,
        gain,
        w_query,
        key_projection_weight,
        value_projection_weight,
        adapter_in,
        tasks,
        moves,
        own_rows,
    )
    partial, pool_query, slot_keyvalue_matrices = lax.optimization_barrier(
        (partial, pool_query, slot_keyvalue_matrices)
    )
    with jax.named_scope("sum_plane"):
        by_plane = exchange(partial.reshape(planes, column_rows, -1), PLANE)

    up = jnp.concatenate(
        [
            pool_query.reshape(rank, query_width),
            slot_keyvalue_matrices.reshape(rank, 2 * head_dim),
        ],
        axis=1,
    )
    with jax.named_scope("up_x"):
        up_line = lax.all_gather(up, "x", axis=0)
    with jax.named_scope("up_y_lo"):
        up_other = lax.ppermute(up_line, "y_lo", [(0, 1), (1, 0)])
    low_part = sum_low(by_plane, base_end, 3 * rank, depth)
    plane_sum = jnp.sum(by_plane[:, :, :base_end].astype(jnp.float32), axis=0)
    with jax.named_scope("sum_low"):
        low_parts = exchange(low_part, "z")

    x, y_lo, z = (lax.axis_index(name) for name in GROUP)
    column_home = lax.dynamic_slice_in_dim(
        row_home, (x * 2 + y_lo) * column_rows, column_rows, 0
    )
    home_x = column_home // (2 * depth)
    other_half = jnp.where(column_home // depth % 2 == y_lo, 0, line)
    slot = jnp.where(column_home % depth == z, home_x + other_half, -1)
    raw_part = lift(
        slot[:, None], low_parts, plane_sum, up_line, up_other, rank, head_dim, model_width
    )
    with jax.named_scope("sum_z"):
        by_depth = exchange(raw_part.reshape(depth, per_group, base_end), "z")
    raw = jnp.sum(by_depth.astype(jnp.float32), axis=0)

    row_step = jnp.arange(per_group) // own_rows
    positions = jnp.tile(lengths, steps) + row_step
    queries = apply_rotary(raw[:, :query_width].reshape(per_group, heads, head_dim), positions)
    new_keys = apply_rotary(
        raw[:, query_width:key_end].reshape(per_group, 1, head_dim), positions
    )
    raw_value = raw[:, key_end:]

    def by_row(array):
        return (
            array.astype(jnp.bfloat16)
            .reshape(steps, own_rows, -1, head_dim)
            .transpose(1, 0, 2, 3)
            .reshape(own_rows, -1, head_dim)
        )

    attended = attend(
        by_row(queries),
        cache_keys.reshape(own_rows, -1, head_dim),
        value_cache.reshape(own_rows, -1, head_dim),
        by_row(new_keys),
        by_row(raw_value),
        lengths,
        jnp.arange(steps * heads) // heads,
    )
    attended = (
        attended.reshape(own_rows, steps, query_width)
        .transpose(1, 0, 2)
        .reshape(per_group, query_width)
    )

    with jax.named_scope("gather_z"):
        line = exchange(
            jnp.broadcast_to(attended[None], (depth, per_group, query_width)), "z"
        ).reshape(depth * per_group, query_width)
    with jax.named_scope("gather_plane"):
        piece_rows = exchange(
            jnp.broadcast_to(line[None], (planes, depth * per_group, query_width)), PLANE
        ).reshape(every_row, query_width)

    every_reduced = jnp.einsum(
        "rq,tqc->rtc", piece_rows, adapter_attn, preferred_element_type=jnp.float32
    )
    reduced = jnp.where(marks[:, :, None], every_reduced, 0).astype(jnp.bfloat16)
    mixed = dot(piece_rows, w_output) + dot(
        reduced.reshape(every_row, task_count * rank),
        adapter_out.reshape(task_count * rank, width_part),
    )
    mixed = mixed.astype(jnp.bfloat16)
    core = lax.axis_index("core")
    cores = lax.axis_size("core")
    half = steps // cores
    with jax.named_scope("sum_core"):
        pair = lax.all_gather(mixed, "core", axis=0)
    mine = lax.dynamic_slice_in_dim(
        pair.reshape(cores, groups, steps, own_rows, width_part), core * half, half, 2
    ).astype(jnp.float32)
    mine = jnp.sum(mine, axis=0)
    mine = mine.transpose(1, 0, 2, 3).reshape(half, all_rows, width_part)
    for pairs in ([[0, 1], [2, 3]], [[1, 2], [3, 0]]):
        with jax.named_scope("sum_y_hi"):
            both = lax.all_gather(
                mine.astype(jnp.bfloat16), "y_hi", axis=0, axis_index_groups=pairs
            )
        mine = both[0].astype(jnp.float32) + both[1].astype(jnp.float32)
    residual = lax.dynamic_slice_in_dim(inputs, core * half, half, 0)
    finished = (residual.astype(jnp.float32) + mine).astype(jnp.bfloat16)
    with jax.named_scope("gather_core"):
        return lax.all_gather(finished, "core", axis=0, tiled=True)


def solution(mesh):
    parts = Mesh(mesh.devices.reshape(4, 2, 8, 4, 2), GROUP + TENSOR)
    return jax.shard_map(
        on_device,
        mesh=parts,
        in_specs=(
            P(None, None, GROUP),
            P(GROUP),
            P(GROUP, TENSOR),
            P(GROUP, TENSOR),
            P(GROUP, TENSOR),
            P(TENSOR, GROUP),
            P(None, GROUP, None),
            P(None, TENSOR, None),
            P(None, None, GROUP),
            P(GROUP, None, TENSOR),
            P(GROUP, None, None, TENSOR),
            P(GROUP, TENSOR, None, None),
            P(GROUP, TENSOR, None, None),
            P(),
            P(),
            P(),
            P(GROUP),
        ),
        out_specs=P(None, None, GROUP),
        check_vma=False,
    )
```

```python
import functools
import math

import jax
import jax.numpy as jnp
from jax import lax
from jax.experimental import pallas as pl
from jax.experimental.pallas import tpu as pltpu
from jax.sharding import Mesh
from jax.sharding import PartitionSpec as P

epsilon = 1e-05
GROUP = ("x", "y_lo", "z")
PLANE = ("x", "y_lo")
TENSOR = ("y_hi", "core")
PADDED_WIDTH = 256


def exchange(blocks, axes):
    return lax.all_to_all(blocks, axes, 0, 0, tiled=True)


def apply_rotary(vectors, token_positions):
    half_width = vectors.shape[-1] // 2
    frequency = jnp.exp(
        -jnp.log(500000.0) * jnp.arange(half_width, dtype=jnp.float32) * (2.0 / vectors.shape[-1])
    )
    angles = token_positions.astype(jnp.float32)[:, None] * frequency[None, :]
    cosine = jnp.cos(angles)[:, None, :]
    sine_part = jnp.sin(angles)[:, None, :]
    leading = vectors[..., :half_width]
    trailing = vectors[..., half_width:]
    return jnp.concatenate(
        [leading * cosine - trailing * sine_part, leading * sine_part + trailing * cosine], axis=-1
    )


def dot(left, right):
    return jnp.dot(left, right, preferred_element_type=jnp.float32)


def start_copies(pairs, arrived):
    copies = [
        pltpu.make_async_copy(source, held, arrived.at[number])
        for number, (source, held) in enumerate(pairs)
    ]
    for copy in copies:
        copy.start()
    return copies


def project_kernel(
    own_rows,
    gain_ref,
    tasks_ref,
    moves_ref,
    inputs_ref,
    adapter_ref,
    query_ref,
    key_ref,
    value_ref,
    out_ref,
    held_inputs,
    held_adapter,
    held_query,
    held_key,
    held_value,
    gained_ref,
    arrived,
):
    steps, all_rows, width = inputs_ref.shape
    every_row = steps * all_rows
    per_group = steps * own_rows
    query_width = query_ref.shape[1]
    head_dim = key_ref.shape[1]
    adapters, low, _ = adapter_ref.shape
    key_end = query_width + head_dim
    base_end = key_end + head_dim
    block = 128
    copies = start_copies(
        (
            (inputs_ref, held_inputs),
            (adapter_ref, held_adapter),
            (query_ref, held_query),
            (key_ref, held_key),
            (value_ref, held_value),
        ),
        arrived,
    )

    def lane(width):
        return lax.broadcasted_iota(jnp.int32, (block, width), 1)

    copies[0].wait()
    gathered = held_inputs[...].reshape(every_row, width)
    squares_of = []
    for first in range(0, every_row, block):
        row = first + lax.broadcasted_iota(jnp.int32, (block, 1), 0)
        place = row % per_group // own_rows * all_rows + row // per_group * own_rows + row % own_rows
        order = jnp.where(lane(every_row) == place, 1.0, 0.0).astype(jnp.bfloat16)
        states = dot(order, gathered)
        gained_ref[first : first + block, :] = (states * gain_ref[...]).astype(jnp.bfloat16)
        squares_of.append(jnp.sum(states * states, axis=1, keepdims=True))

    copies[1].wait()
    for index, squares in enumerate(squares_of):
        first = index * block

        row = first + lax.broadcasted_iota(jnp.int32, (block, 1), 0)
        own = lane(all_rows) == row // per_group * own_rows + row % own_rows
        task = jnp.sum(jnp.where(own, tasks_ref[...], 0), axis=1, keepdims=True)
        here = moves_ref[1:2, :] == row // per_group
        moved = jnp.sum(jnp.where(here, 1, 0), axis=1, keepdims=True) > 0
        chosen = jnp.sum(jnp.where(here, moves_ref[0:1, :], 0), axis=1, keepdims=True)
        late = row % per_group >= per_group // 2
        task = jnp.where(jnp.logical_and(late, moved), chosen, task)
        gained = gained_ref[first : first + block, :]
        total = jnp.zeros((block, low), jnp.float32)
        for adapter in range(0, adapters, 2):
            both = [
                jnp.where(task == number, gained, jnp.zeros_like(gained))
                for number in (adapter, adapter + 1)
            ]
            total = total + lax.dot_general(
                jnp.concatenate(both, axis=1),
                jnp.concatenate([held_adapter[adapter], held_adapter[adapter + 1]], axis=1),
                (((1,), (1,)), ((), ())),
                preferred_element_type=jnp.float32,
            )
        rest = PADDED_WIDTH - low
        squares_high = squares.astype(jnp.bfloat16).astype(jnp.float32)
        extra = jnp.where(
            lane(rest) == 0,
            squares_high,
            jnp.where(lane(rest) == 1, squares - squares_high, 0.0),
        )
        out_ref[first : first + block, base_end : base_end + PADDED_WIDTH] = jnp.concatenate(
            [total, extra], axis=1
        ).astype(jnp.bfloat16)

    for copy in copies[2:]:
        copy.wait()

    @pl.loop(0, every_row // block)
    def _(index):
        rows = pl.ds(pl.multiple_of(index * block, block), block)
        gained = gained_ref[rows, :]
        out_ref[rows, 0:query_width] = dot(gained, held_query[...]).astype(jnp.bfloat16)
        out_ref[rows, query_width:key_end] = dot(gained, held_key[...]).astype(jnp.bfloat16)
        out_ref[rows, key_end:base_end] = dot(gained, held_value[...]).astype(jnp.bfloat16)


def project(inputs, gain, w_query, w_key, w_value, adapter_in, tasks, moves, own_rows):
    steps, all_rows, width = inputs.shape
    columns = w_query.shape[1] + w_key.shape[1] + w_value.shape[1] + PADDED_WIDTH
    large = (inputs, jnp.swapaxes(adapter_in, 1, 2), w_query, w_key, w_value)
    return pl.pallas_call(
        functools.partial(project_kernel, own_rows),
        out_shape=jax.ShapeDtypeStruct((steps * all_rows, columns), jnp.bfloat16),
        in_specs=[pl.BlockSpec(memory_space=pltpu.VMEM)] * 3
        + [pl.BlockSpec(memory_space=pl.ANY)] * len(large),
        scratch_shapes=[pltpu.VMEM(array.shape, jnp.bfloat16) for array in large]
        + [
            pltpu.VMEM((steps * all_rows, width), jnp.bfloat16),
            pltpu.SemaphoreType.DMA((len(large),)),
        ],
        cost_estimate=pl.CostEstimate(
            flops=2 * steps * all_rows * width * 3328, bytes_accessed=3_000_000, transcendentals=0
        ),
    )(gain[None, :], tasks[None, :], moves.T, *large)


def low_kernel(low, parts_ref, low_ref):
    sources, rows, columns = parts_ref.shape
    targets, _, width = low_ref.shape
    total = parts_ref[0, :, columns - width :].astype(jnp.float32)
    for source in range(1, sources):
        total = total + parts_ref[source, :, columns - width :].astype(jnp.float32)
    lane = lax.broadcasted_iota(jnp.int32, total.shape, 1)
    squares = jnp.sum(jnp.where(lane >= low, total, 0.0), axis=1, keepdims=True)
    squares_high = squares.astype(jnp.bfloat16).astype(jnp.float32)
    total = jnp.where(
        lane < low,
        total,
        jnp.where(
            lane == low, squares_high, jnp.where(lane == low + 1, squares - squares_high, 0.0)
        ),
    ).astype(jnp.bfloat16)
    for target in range(targets):
        low_ref[target] = total


def sum_low(parts, base_end, low, depth):
    _, rows, columns = parts.shape
    return pl.pallas_call(
        functools.partial(low_kernel, low),
        out_shape=jax.ShapeDtypeStruct((depth, rows, columns - base_end), jnp.bfloat16),
        in_specs=[pl.BlockSpec(memory_space=pltpu.VMEM)],
        out_specs=pl.BlockSpec(memory_space=pltpu.VMEM),
        compiler_params=pltpu.CompilerParams(vmem_limit_bytes=16 * 1024 * 1024),
        cost_estimate=pl.CostEstimate(
            flops=parts.size // 6, bytes_accessed=parts.size // 3, transcendentals=0
        ),
    )(parts)


def lift_kernel(
    rank,
    head_dim,
    model_width,
    slot_ref,
    low_ref,
    line_ref,
    other_ref,
    base_ref,
    out_ref,
):
    rows, columns = out_ref.shape
    line = line_ref.shape[0]
    low = 3 * rank
    total = low_ref[0].astype(jnp.float32)
    for source in range(1, low_ref.shape[0]):
        total = total + low_ref[source].astype(jnp.float32)
    lane = lax.broadcasted_iota(jnp.int32, total.shape, 1)
    squares = jnp.sum(jnp.where(lane >= low, total, 0.0), axis=1, keepdims=True)
    inverse = lax.rsqrt(squares / model_width + epsilon)
    lowrank = (inverse * total).astype(jnp.bfloat16)
    from_lane = lax.broadcasted_iota(jnp.int32, (PADDED_WIDTH, line * rank), 0)
    to_lane = lax.broadcasted_iota(jnp.int32, (PADDED_WIDTH, line * rank), 1)
    slot_lane = lax.broadcasted_iota(jnp.int32, (rows, line * rank), 1) // rank
    slot = slot_ref[...]
    spreads = []
    for number in range(3):
        pick = jnp.where(from_lane == number * rank + to_lane % rank, 1.0, 0.0)
        tiled = dot(lowrank, pick.astype(jnp.bfloat16))
        spreads.append(
            [
                jnp.where(slot == slot_lane + half * line, tiled, 0.0).astype(jnp.bfloat16)
                for half in range(2)
            ]
        )
    key_first, value_first = columns - 2 * head_dim, columns - head_dim
    bounds = ((0, key_first), (key_first, value_first), (value_first, columns))
    for (first, last), (near, far) in zip(bounds, spreads, strict=True):
        lifted = dot(near, line_ref[:, :, first:last].reshape(line * rank, last - first))
        lifted = lifted + dot(
            far, other_ref[:, :, first:last].reshape(line * rank, last - first)
        )
        out_ref[:, first:last] = (inverse * base_ref[:, first:last] + lifted).astype(jnp.bfloat16)


def lift(slot, low_parts, base, up_line, up_other, rank, head_dim, model_width):
    return pl.pallas_call(
        functools.partial(lift_kernel, rank, head_dim, model_width),
        out_shape=jax.ShapeDtypeStruct(base.shape, jnp.bfloat16),
        in_specs=[pl.BlockSpec(memory_space=pltpu.VMEM)] * 5,
        out_specs=pl.BlockSpec(memory_space=pltpu.VMEM),
        compiler_params=pltpu.CompilerParams(vmem_limit_bytes=16 * 1024 * 1024),
        cost_estimate=pl.CostEstimate(
            flops=2 * base.size * up_line.shape[0] * 2 * rank,
            bytes_accessed=2_000_000,
            transcendentals=0,
        ),
    )(slot, low_parts, up_line, up_other, base)


def attend(queries, cache_keys, value_cache, fresh_keys, fresh_values, lengths, query_steps):
    scaling = 1.0 / math.sqrt(queries.shape[-1])
    old_scores = (
        jnp.einsum("rnd,rjd->rnj", queries, cache_keys, preferred_element_type=jnp.float32)
        * scaling
    )
    new_scores = (
        jnp.einsum("rnd,rjd->rnj", queries, fresh_keys, preferred_element_type=jnp.float32)
        * scaling
    )
    visible = jnp.arange(cache_keys.shape[1])[None, None, :] < lengths[:, None, None]
    old_scores = jnp.where(visible, old_scores, -1e30)
    fresh = jnp.arange(fresh_keys.shape[1])[None, None, :] <= query_steps[None, :, None]
    new_scores = jnp.where(fresh, new_scores, -1e30)
    highest = jnp.maximum(jnp.max(old_scores, axis=-1), jnp.max(new_scores, axis=-1))[..., None]
    old_exp = jnp.exp(old_scores - highest)
    new_exp = jnp.exp(new_scores - highest)
    denominator = jnp.sum(old_exp, axis=-1, keepdims=True) + jnp.sum(
        new_exp, axis=-1, keepdims=True
    )
    old_weights = (old_exp / denominator).astype(jnp.bfloat16)
    new_weights = (new_exp / denominator).astype(jnp.bfloat16)
    mixed = jnp.einsum(
        "rnj,rjd->rnd", old_weights, value_cache, preferred_element_type=jnp.float32
    )
    mixed = mixed + jnp.einsum(
        "rnj,rjd->rnd", new_weights, fresh_values, preferred_element_type=jnp.float32
    )
    return mixed.astype(jnp.bfloat16)


def on_device(
    inputs,
    gain,
    w_query,
    key_projection_weight,
    value_projection_weight,
    w_output,
    adapter_in,
    adapter_attn,
    adapter_out,
    pool_query,
    slot_keyvalue_matrices,
    cache_keys,
    value_cache,
    tasks,
    homes,
    moves,
    lengths,
):
    steps, all_rows, width_part = inputs.shape
    own_rows = lengths.shape[0]
    groups = all_rows // own_rows
    planes = lax.axis_size(PLANE)
    line = lax.axis_size("x")
    depth = lax.axis_size("z")
    task_count = homes.shape[0]
    rank = adapter_out.shape[1]
    head_dim = cache_keys.shape[3]
    query_width = w_query.shape[1]
    heads = query_width // head_dim
    key_end = query_width + head_dim
    base_end = key_end + head_dim
    per_group = steps * own_rows
    every_row = groups * per_group
    model_width = width_part * groups
    column_rows = depth * per_group

    group_tasks = tasks.reshape(groups, own_rows)
    matched = moves[:, 1][None, :] == jnp.arange(groups, dtype=jnp.int32)[:, None]
    moved = jnp.any(matched, axis=1)
    chosen = jnp.sum(jnp.where(matched, moves[:, 0][None, :], 0), axis=1)
    late = jnp.where(moved[:, None], chosen[:, None], group_tasks)
    active = jnp.stack([group_tasks if s < steps // 2 else late for s in range(steps)], axis=1)
    active = active.reshape(every_row)
    marks = active[:, None] == jnp.arange(task_count, dtype=jnp.int32)[None, :]
    row_home = jnp.sum(jnp.where(marks, homes[None, :], 0), axis=1)

    near = [(0, 1), (1, 0), (2, 3), (3, 2)]
    far = [(0, 3), (1, 2), (2, 1), (3, 0)]
    with jax.named_scope("up_x"):
        pool_near = lax.ppermute(pool_query, "x", near)

    partial = project(
        inputs,
        gain,
        w_query,
        key_projection_weight,
        value_projection_weight,
        adapter_in,
        tasks,
        moves,
        own_rows,
    )
    partial, pool_near, slot_keyvalue_matrices = lax.optimization_barrier(
        (partial, pool_near, slot_keyvalue_matrices)
    )
    with jax.named_scope("sum_plane"):
        by_plane = exchange(partial.reshape(planes, column_rows, -1), PLANE)

    with jax.named_scope("up_x"):
        keyvalue_near = lax.ppermute(slot_keyvalue_matrices, "x", near)
        query_pair = jnp.concatenate([pool_query, pool_near])
        keyvalue_pair = jnp.concatenate([slot_keyvalue_matrices, keyvalue_near])
        query_far = lax.ppermute(query_pair, "x", far)
        keyvalue_far = lax.ppermute(keyvalue_pair, "x", far)
    up_line = jnp.concatenate(
        [
            jnp.concatenate([query_pair, query_far]),
            jnp.concatenate([keyvalue_pair, keyvalue_far]).reshape(line, rank, 2 * head_dim),
        ],
        axis=2,
    )
    with jax.named_scope("up_y_lo"):
        up_other = lax.ppermute(up_line, "y_lo", [(0, 1), (1, 0)])
    low_part = sum_low(by_plane, base_end, 3 * rank, depth)
    plane_sum = jnp.sum(by_plane[:, :, :base_end].astype(jnp.float32), axis=0)
    with jax.named_scope("sum_low"):
        low_parts = exchange(low_part, "z")

    x, y_lo, z = (lax.axis_index(name) for name in GROUP)
    column_home = lax.dynamic_slice_in_dim(
        row_home, (x * 2 + y_lo) * column_rows, column_rows, 0
    )
    home_x = column_home // (2 * depth)
    order = jnp.stack([x, x ^ 1, 3 - x, (3 - x) ^ 1])
    near_slot = jnp.sum(jnp.where(home_x[:, None] == order[None, :], jnp.arange(line), 0), axis=1)
    other_half = jnp.where(column_home // depth % 2 == y_lo, 0, line)
    slot = jnp.where(column_home % depth == z, near_slot + other_half, -1)
    raw_part = lift(
        slot[:, None], low_parts, plane_sum, up_line, up_other, rank, head_dim, model_width
    )
    with jax.named_scope("sum_z"):
        by_depth = exchange(raw_part.reshape(depth, per_group, base_end), "z")
    raw = jnp.sum(by_depth.astype(jnp.float32), axis=0)

    row_step = jnp.arange(per_group) // own_rows
    positions = jnp.tile(lengths, steps) + row_step
    queries = apply_rotary(raw[:, :query_width].reshape(per_group, heads, head_dim), positions)
    new_keys = apply_rotary(
        raw[:, query_width:key_end].reshape(per_group, 1, head_dim), positions
    )
    raw_value = raw[:, key_end:]

    def by_row(array):
        return (
            array.astype(jnp.bfloat16)
            .reshape(steps, own_rows, -1, head_dim)
            .transpose(1, 0, 2, 3)
            .reshape(own_rows, -1, head_dim)
        )

    attended = attend(
        by_row(queries),
        cache_keys.reshape(own_rows, -1, head_dim),
        value_cache.reshape(own_rows, -1, head_dim),
        by_row(new_keys),
        by_row(raw_value),
        lengths,
        jnp.arange(steps * heads) // heads,
    )
    attended = (
        attended.reshape(own_rows, steps, query_width)
        .transpose(1, 0, 2)
        .reshape(per_group, query_width)
    )

    with jax.named_scope("gather_z"):
        line = exchange(
            jnp.broadcast_to(attended[None], (depth, per_group, query_width)), "z"
        ).reshape(depth * per_group, query_width)
    with jax.named_scope("gather_plane"):
        piece_rows = exchange(
            jnp.broadcast_to(line[None], (planes, depth * per_group, query_width)), PLANE
        ).reshape(every_row, query_width)

    every_reduced = jnp.einsum(
        "rq,tqc->rtc", piece_rows, adapter_attn, preferred_element_type=jnp.float32
    )
    reduced = jnp.where(marks[:, :, None], every_reduced, 0).astype(jnp.bfloat16)
    mixed = dot(piece_rows, w_output) + dot(
        reduced.reshape(every_row, task_count * rank),
        adapter_out.reshape(task_count * rank, width_part),
    )
    mixed = mixed.astype(jnp.bfloat16)
    core = lax.axis_index("core")
    cores = lax.axis_size("core")
    half = steps // cores
    with jax.named_scope("sum_core"):
        pair = lax.all_gather(mixed, "core", axis=0)
    mine = lax.dynamic_slice_in_dim(
        pair.reshape(cores, groups, steps, own_rows, width_part), core * half, half, 2
    ).astype(jnp.float32)
    mine = jnp.sum(mine, axis=0)
    mine = mine.transpose(1, 0, 2, 3).reshape(half, all_rows, width_part)
    for pairs in ([[0, 1], [2, 3]], [[1, 2], [3, 0]]):
        with jax.named_scope("sum_y_hi"):
            both = lax.all_gather(
                mine.astype(jnp.bfloat16), "y_hi", axis=0, axis_index_groups=pairs
            )
        mine = both[0].astype(jnp.float32) + both[1].astype(jnp.float32)
    residual = lax.dynamic_slice_in_dim(inputs, core * half, half, 0)
    finished = (residual.astype(jnp.float32) + mine).astype(jnp.bfloat16)
    with jax.named_scope("gather_core"):
        return lax.all_gather(finished, "core", axis=0, tiled=True)


def solution(mesh):
    parts = Mesh(mesh.devices.reshape(4, 2, 8, 4, 2), GROUP + TENSOR)
    return jax.shard_map(
        on_device,
        mesh=parts,
        in_specs=(
            P(None, None, GROUP),
            P(GROUP),
            P(GROUP, TENSOR),
            P(GROUP, TENSOR),
            P(GROUP, TENSOR),
            P(TENSOR, GROUP),
            P(None, GROUP, None),
            P(None, TENSOR, None),
            P(None, None, GROUP),
            P(GROUP, None, TENSOR),
            P(GROUP, None, None, TENSOR),
            P(GROUP, TENSOR, None, None),
            P(GROUP, TENSOR, None, None),
            P(),
            P(),
            P(),
            P(GROUP),
        ),
        out_specs=P(None, None, GROUP),
        check_vma=False,
    )
```

```python
import functools
import math

import jax
import jax.numpy as jnp
import numpy as np
from jax import lax
from jax.experimental import pallas as pl
from jax.experimental.pallas import tpu as pltpu
from jax.sharding import Mesh
from jax.sharding import PartitionSpec as P

epsilon = 1e-05
GROUP = ("x", "y_lo", "z")
PLANE = ("x", "y_lo")
TENSOR = ("y_hi", "core")
PADDED_WIDTH = 256


def exchange(blocks, axes):
    return lax.all_to_all(blocks, axes, 0, 0, tiled=True)


def apply_rotary(vectors, token_positions):
    half_width = vectors.shape[-1] // 2
    frequency = jnp.exp(
        -jnp.log(500000.0) * jnp.arange(half_width, dtype=jnp.float32) * (2.0 / vectors.shape[-1])
    )
    angles = token_positions.astype(jnp.float32)[:, None] * frequency[None, :]
    cosine = jnp.cos(angles)[:, None, :]
    sine_part = jnp.sin(angles)[:, None, :]
    leading = vectors[..., :half_width]
    trailing = vectors[..., half_width:]
    return jnp.concatenate(
        [leading * cosine - trailing * sine_part, leading * sine_part + trailing * cosine], axis=-1
    )


def dot(left, right):
    return jnp.dot(left, right, preferred_element_type=jnp.float32)


def start_copies(pairs, arrived):
    copies = [
        pltpu.make_async_copy(source, held, arrived.at[number])
        for number, (source, held) in enumerate(pairs)
    ]
    for copy in copies:
        copy.start()
    return copies


def project_kernel(
    own_rows,
    gain_ref,
    tasks_ref,
    moves_ref,
    homes_ref,
    inputs_ref,
    adapter_ref,
    query_ref,
    key_ref,
    value_ref,
    out_ref,
    held_inputs,
    held_adapter,
    held_query,
    held_key,
    held_value,
    gained_ref,
    arrived,
):
    steps, all_rows, width = inputs_ref.shape
    every_row = steps * all_rows
    per_group = steps * own_rows
    query_width = query_ref.shape[1]
    head_dim = key_ref.shape[1]
    adapters, low, _ = adapter_ref.shape
    key_end = query_width + head_dim
    base_end = key_end + head_dim
    block = 128
    copies = start_copies(
        (
            (inputs_ref, held_inputs),
            (adapter_ref, held_adapter),
            (query_ref, held_query),
            (key_ref, held_key),
            (value_ref, held_value),
        ),
        arrived,
    )

    def lane(width):
        return lax.broadcasted_iota(jnp.int32, (block, width), 1)

    copies[0].wait()
    gathered = held_inputs[...].reshape(every_row, width)
    squares_of = []
    for first in range(0, every_row, block):
        row = first + lax.broadcasted_iota(jnp.int32, (block, 1), 0)
        place = row % per_group // own_rows * all_rows + row // per_group * own_rows + row % own_rows
        order = jnp.where(lane(every_row) == place, 1.0, 0.0).astype(jnp.bfloat16)
        states = dot(order, gathered)
        gained_ref[first : first + block, :] = (states * gain_ref[...]).astype(jnp.bfloat16)
        squares_of.append(jnp.sum(states * states, axis=1, keepdims=True))

    copies[1].wait()
    for index, squares in enumerate(squares_of):
        first = index * block

        row = first + lax.broadcasted_iota(jnp.int32, (block, 1), 0)
        own = lane(all_rows) == row // per_group * own_rows + row % own_rows
        task = jnp.sum(jnp.where(own, tasks_ref[...], 0), axis=1, keepdims=True)
        here = moves_ref[1:2, :] == row // per_group
        moved = jnp.sum(jnp.where(here, 1, 0), axis=1, keepdims=True) > 0
        chosen = jnp.sum(jnp.where(here, moves_ref[0:1, :], 0), axis=1, keepdims=True)
        late = row % per_group >= per_group // 2
        task = jnp.where(jnp.logical_and(late, moved), chosen, task)
        home = jnp.sum(
            jnp.where(lane(adapters) == task, homes_ref[...], 0), axis=1, keepdims=True
        ).astype(jnp.float32)
        gained = gained_ref[first : first + block, :]
        total = jnp.zeros((block, low), jnp.float32)
        for adapter in range(0, adapters, 2):
            both = [
                jnp.where(task == number, gained, jnp.zeros_like(gained))
                for number in (adapter, adapter + 1)
            ]
            total = total + lax.dot_general(
                jnp.concatenate(both, axis=1),
                jnp.concatenate([held_adapter[adapter], held_adapter[adapter + 1]], axis=1),
                (((1,), (1,)), ((), ())),
                preferred_element_type=jnp.float32,
            )
        rest = PADDED_WIDTH - low
        squares_high = squares.astype(jnp.bfloat16).astype(jnp.float32)
        extra = jnp.where(
            lane(rest) == 0,
            squares_high,
            jnp.where(
                lane(rest) == 1, squares - squares_high, jnp.where(lane(rest) == 2, home, 0.0)
            ),
        )
        out_ref[first : first + block, base_end : base_end + PADDED_WIDTH] = jnp.concatenate(
            [total, extra], axis=1
        ).astype(jnp.bfloat16)

    for copy in copies[2:]:
        copy.wait()

    @pl.loop(0, every_row // block)
    def _(index):
        rows = pl.ds(pl.multiple_of(index * block, block), block)
        gained = gained_ref[rows, :]
        out_ref[rows, 0:query_width] = dot(gained, held_query[...]).astype(jnp.bfloat16)
        out_ref[rows, query_width:key_end] = dot(gained, held_key[...]).astype(jnp.bfloat16)
        out_ref[rows, key_end:base_end] = dot(gained, held_value[...]).astype(jnp.bfloat16)


def project(inputs, gain, w_query, w_key, w_value, adapter_in, tasks, moves, homes, own_rows):
    steps, all_rows, width = inputs.shape
    columns = w_query.shape[1] + w_key.shape[1] + w_value.shape[1] + PADDED_WIDTH
    large = (inputs, jnp.swapaxes(adapter_in, 1, 2), w_query, w_key, w_value)
    return pl.pallas_call(
        functools.partial(project_kernel, own_rows),
        out_shape=jax.ShapeDtypeStruct((steps * all_rows, columns), jnp.bfloat16),
        in_specs=[pl.BlockSpec(memory_space=pltpu.VMEM)] * 4
        + [pl.BlockSpec(memory_space=pl.ANY)] * len(large),
        scratch_shapes=[pltpu.VMEM(array.shape, jnp.bfloat16) for array in large]
        + [
            pltpu.VMEM((steps * all_rows, width), jnp.bfloat16),
            pltpu.SemaphoreType.DMA((len(large),)),
        ],
        cost_estimate=pl.CostEstimate(
            flops=2 * steps * all_rows * width * 3328, bytes_accessed=3_000_000, transcendentals=0
        ),
    )(gain[None, :], tasks[None, :], moves.T, homes[None, :], *large)


def low_kernel(low, parts_ref, low_ref):
    sources, rows, columns = parts_ref.shape
    targets, _, width = low_ref.shape
    total = parts_ref[0, :, columns - width :].astype(jnp.float32)
    for source in range(1, sources):
        total = total + parts_ref[source, :, columns - width :].astype(jnp.float32)
    lane = lax.broadcasted_iota(jnp.int32, total.shape, 1)
    terms = jnp.logical_or(lane == low, lane == low + 1)
    squares = jnp.sum(jnp.where(terms, total, 0.0), axis=1, keepdims=True)
    squares_high = squares.astype(jnp.bfloat16).astype(jnp.float32)
    total = jnp.where(
        lane == low,
        squares_high,
        jnp.where(lane == low + 1, squares - squares_high, total),
    ).astype(jnp.bfloat16)
    for target in range(targets):
        low_ref[target] = total


def sum_low(parts, base_end, low, depth):
    _, rows, columns = parts.shape
    return pl.pallas_call(
        functools.partial(low_kernel, low),
        out_shape=jax.ShapeDtypeStruct((depth, rows, columns - base_end), jnp.bfloat16),
        in_specs=[pl.BlockSpec(memory_space=pltpu.VMEM)],
        out_specs=pl.BlockSpec(memory_space=pltpu.VMEM),
        compiler_params=pltpu.CompilerParams(vmem_limit_bytes=16 * 1024 * 1024),
        cost_estimate=pl.CostEstimate(
            flops=parts.size // 6, bytes_accessed=parts.size // 3, transcendentals=0
        ),
    )(parts)


def lift_kernel(
    rank,
    head_dim,
    model_width,
    groups,
    low_ref,
    line_ref,
    other_ref,
    base_ref,
    out_ref,
):
    rows, columns = out_ref.shape
    line = line_ref.shape[0]
    low = 3 * rank
    total = low_ref[0].astype(jnp.float32)
    for source in range(1, low_ref.shape[0]):
        total = total + low_ref[source].astype(jnp.float32)
    lane = lax.broadcasted_iota(jnp.int32, total.shape, 1)
    terms = jnp.logical_or(lane == low, lane == low + 1)
    squares = jnp.sum(jnp.where(terms, total, 0.0), axis=1, keepdims=True)
    inverse = lax.rsqrt(squares / model_width + epsilon)
    lowrank = (inverse * total).astype(jnp.bfloat16)
    from_lane = lax.broadcasted_iota(jnp.int32, (PADDED_WIDTH, line * rank), 0)
    to_lane = lax.broadcasted_iota(jnp.int32, (PADDED_WIDTH, line * rank), 1)
    slot_lane = lax.broadcasted_iota(jnp.int32, (rows, line * rank), 1) // rank
    home = jnp.sum(jnp.where(lane == low + 2, total, 0.0), axis=1, keepdims=True) / groups
    home = home.astype(jnp.int32)
    depth = low_ref.shape[0]
    same_half = home // depth % 2 == lax.axis_index("y_lo")
    slot = home // (2 * depth) + jnp.where(same_half, 0, line)
    slot = jnp.where(home % depth == lax.axis_index("z"), slot, -1)
    spreads = []
    for number in range(3):
        pick = jnp.where(from_lane == number * rank + to_lane % rank, 1.0, 0.0)
        tiled = dot(lowrank, pick.astype(jnp.bfloat16))
        spreads.append(
            [
                jnp.where(slot == slot_lane + half * line, tiled, 0.0).astype(jnp.bfloat16)
                for half in range(2)
            ]
        )
    key_first, value_first = columns - 2 * head_dim, columns - head_dim
    bounds = ((0, key_first), (key_first, value_first), (value_first, columns))
    for (first, last), (near, far) in zip(bounds, spreads, strict=True):
        lifted = dot(near, line_ref[:, :, first:last].reshape(line * rank, last - first))
        lifted = lifted + dot(
            far, other_ref[:, :, first:last].reshape(line * rank, last - first)
        )
        out_ref[:, first:last] = (inverse * base_ref[:, first:last] + lifted).astype(jnp.bfloat16)


def lift(low_parts, base, up_line, up_other, rank, head_dim, model_width, groups):
    return pl.pallas_call(
        functools.partial(lift_kernel, rank, head_dim, model_width, groups),
        out_shape=jax.ShapeDtypeStruct(base.shape, jnp.bfloat16),
        in_specs=[pl.BlockSpec(memory_space=pltpu.VMEM)] * 4,
        out_specs=pl.BlockSpec(memory_space=pltpu.VMEM),
        compiler_params=pltpu.CompilerParams(vmem_limit_bytes=16 * 1024 * 1024),
        cost_estimate=pl.CostEstimate(
            flops=2 * base.size * up_line.shape[0] * 2 * rank,
            bytes_accessed=2_000_000,
            transcendentals=0,
        ),
    )(low_parts, up_line, up_other, base)


def attend(queries, cache_keys, value_cache, fresh_keys, fresh_values, lengths, query_steps):
    scaling = 1.0 / math.sqrt(queries.shape[-1])
    old_scores = (
        jnp.einsum("rnd,rjd->rnj", queries, cache_keys, preferred_element_type=jnp.float32)
        * scaling
    )
    new_scores = (
        jnp.einsum("rnd,rjd->rnj", queries, fresh_keys, preferred_element_type=jnp.float32)
        * scaling
    )
    visible = jnp.arange(cache_keys.shape[1])[None, None, :] < lengths[:, None, None]
    old_scores = jnp.where(visible, old_scores, -1e30)
    fresh = np.arange(fresh_keys.shape[1])[None, None, :] <= query_steps[None, :, None]
    new_scores = jnp.where(fresh, new_scores, -1e30)
    highest = jnp.maximum(jnp.max(old_scores, axis=-1), jnp.max(new_scores, axis=-1))[..., None]
    old_exp = jnp.exp(old_scores - highest)
    new_exp = jnp.exp(new_scores - highest)
    denominator = jnp.sum(old_exp, axis=-1, keepdims=True) + jnp.sum(
        new_exp, axis=-1, keepdims=True
    )
    old_weights = (old_exp / denominator).astype(jnp.bfloat16)
    new_weights = (new_exp / denominator).astype(jnp.bfloat16)
    mixed = jnp.einsum(
        "rnj,rjd->rnd", old_weights, value_cache, preferred_element_type=jnp.float32
    )
    mixed = mixed + jnp.einsum(
        "rnj,rjd->rnd", new_weights, fresh_values, preferred_element_type=jnp.float32
    )
    return mixed.astype(jnp.bfloat16)


def on_device(
    inputs,
    gain,
    w_query,
    key_projection_weight,
    value_projection_weight,
    w_output,
    adapter_in,
    adapter_attn,
    adapter_out,
    pool_query,
    slot_keyvalue_matrices,
    cache_keys,
    value_cache,
    tasks,
    homes,
    moves,
    lengths,
):
    steps, all_rows, width_part = inputs.shape
    own_rows = lengths.shape[0]
    groups = all_rows // own_rows
    planes = lax.axis_size(PLANE)
    line = lax.axis_size("x")
    depth = lax.axis_size("z")
    task_count = homes.shape[0]
    rank = adapter_out.shape[1]
    head_dim = cache_keys.shape[3]
    query_width = w_query.shape[1]
    heads = query_width // head_dim
    key_end = query_width + head_dim
    base_end = key_end + head_dim
    per_group = steps * own_rows
    every_row = groups * per_group
    model_width = width_part * groups
    column_rows = depth * per_group

    partial = project(
        inputs,
        gain,
        w_query,
        key_projection_weight,
        value_projection_weight,
        adapter_in,
        tasks,
        moves,
        homes,
        own_rows,
    )
    partial, pool_query, slot_keyvalue_matrices = lax.optimization_barrier(
        (partial, pool_query, slot_keyvalue_matrices)
    )
    with jax.named_scope("sum_plane"):
        by_plane = exchange(partial.reshape(planes, column_rows, -1), PLANE)

    up = jnp.concatenate(
        [
            pool_query.reshape(rank, query_width),
            slot_keyvalue_matrices.reshape(rank, 2 * head_dim),
        ],
        axis=1,
    )
    with jax.named_scope("up_x"):
        up_line = lax.all_gather(up, "x", axis=0)
    with jax.named_scope("up_y_lo"):
        up_other = lax.ppermute(up_line, "y_lo", [(0, 1), (1, 0)])
    low_part = sum_low(by_plane, base_end, 3 * rank, depth)
    plane_sum = jnp.sum(by_plane[:, :, :base_end].astype(jnp.float32), axis=0)
    with jax.named_scope("sum_low"):
        low_parts = exchange(low_part, "z")

    raw_part = lift(
        low_parts, plane_sum, up_line, up_other, rank, head_dim, model_width, groups
    )
    with jax.named_scope("sum_z"):
        by_depth = exchange(raw_part.reshape(depth, per_group, base_end), "z")
    raw = jnp.sum(by_depth.astype(jnp.float32), axis=0)

    row_step = jnp.arange(per_group) // own_rows
    positions = jnp.tile(lengths, steps) + row_step
    queries = apply_rotary(raw[:, :query_width].reshape(per_group, heads, head_dim), positions)
    new_keys = apply_rotary(
        raw[:, query_width:key_end].reshape(per_group, 1, head_dim), positions
    )
    raw_value = raw[:, key_end:]

    def by_row(array):
        return (
            array.astype(jnp.bfloat16)
            .reshape(steps, own_rows, -1, head_dim)
            .transpose(1, 0, 2, 3)
            .reshape(own_rows, -1, head_dim)
        )

    attended = attend(
        by_row(queries),
        cache_keys.reshape(own_rows, -1, head_dim),
        value_cache.reshape(own_rows, -1, head_dim),
        by_row(new_keys),
        by_row(raw_value),
        lengths,
        np.arange(steps * heads) // heads,
    )
    attended = (
        attended.reshape(own_rows, steps, query_width)
        .transpose(1, 0, 2)
        .reshape(per_group, query_width)
    )

    with jax.named_scope("gather_z"):
        column = exchange(
            jnp.broadcast_to(attended[None], (depth, per_group, query_width)), "z"
        ).reshape(depth * per_group, query_width)
    column, tasks, moves = lax.optimization_barrier((column, tasks, moves))
    with jax.named_scope("gather_plane"):
        piece_rows = exchange(
            jnp.broadcast_to(column[None], (planes, depth * per_group, query_width)), PLANE
        ).reshape(every_row, query_width)

    group_tasks = tasks.reshape(groups, own_rows)
    matched = moves[:, 1][None, :] == jnp.arange(groups, dtype=jnp.int32)[:, None]
    moved = jnp.any(matched, axis=1)
    chosen = jnp.sum(jnp.where(matched, moves[:, 0][None, :], 0), axis=1)
    late = jnp.where(moved[:, None], chosen[:, None], group_tasks)
    active = jnp.stack([group_tasks if s < steps // 2 else late for s in range(steps)], axis=1)
    active = active.reshape(every_row)
    marks = active[:, None] == jnp.arange(task_count, dtype=jnp.int32)[None, :]

    every_reduced = jnp.einsum(
        "rq,tqc->rtc", piece_rows, adapter_attn, preferred_element_type=jnp.float32
    )
    reduced = jnp.where(marks[:, :, None], every_reduced, 0).astype(jnp.bfloat16)
    mixed = dot(piece_rows, w_output) + dot(
        reduced.reshape(every_row, task_count * rank),
        adapter_out.reshape(task_count * rank, width_part),
    )
    mixed = mixed.astype(jnp.bfloat16)
    core = lax.axis_index("core")
    cores = lax.axis_size("core")
    half = steps // cores
    with jax.named_scope("sum_core"):
        pair = lax.all_gather(mixed, "core", axis=0)
    mine = lax.dynamic_slice_in_dim(
        pair.reshape(cores, groups, steps, own_rows, width_part), core * half, half, 2
    ).astype(jnp.float32)
    mine = jnp.sum(mine, axis=0)
    mine = mine.transpose(1, 0, 2, 3).reshape(half, all_rows, width_part)
    for pairs in ([[0, 1], [2, 3]], [[1, 2], [3, 0]]):
        with jax.named_scope("sum_y_hi"):
            both = lax.all_gather(
                mine.astype(jnp.bfloat16), "y_hi", axis=0, axis_index_groups=pairs
            )
        mine = both[0].astype(jnp.float32) + both[1].astype(jnp.float32)
    residual = lax.dynamic_slice_in_dim(inputs, core * half, half, 0)
    finished = (residual.astype(jnp.float32) + mine).astype(jnp.bfloat16)
    with jax.named_scope("gather_core"):
        return lax.all_gather(finished, "core", axis=0, tiled=True)


def solution(mesh):
    parts = Mesh(mesh.devices.reshape(4, 2, 8, 4, 2), GROUP + TENSOR)
    return jax.shard_map(
        on_device,
        mesh=parts,
        in_specs=(
            P(None, None, GROUP),
            P(GROUP),
            P(GROUP, TENSOR),
            P(GROUP, TENSOR),
            P(GROUP, TENSOR),
            P(TENSOR, GROUP),
            P(None, GROUP, None),
            P(None, TENSOR, None),
            P(None, None, GROUP),
            P(GROUP, None, TENSOR),
            P(GROUP, None, None, TENSOR),
            P(GROUP, TENSOR, None, None),
            P(GROUP, TENSOR, None, None),
            P(),
            P(),
            P(),
            P(GROUP),
        ),
        out_specs=P(None, None, GROUP),
        check_vma=False,
    )
```

```python
import functools
import math

import jax
import jax.numpy as jnp
import numpy as np
from jax import lax
from jax.experimental import pallas as pl
from jax.experimental.pallas import tpu as pltpu
from jax.sharding import Mesh
from jax.sharding import PartitionSpec as P

epsilon = 1e-05
GROUP = ("x", "y_lo", "z")
PLANE = ("x", "y_lo")
TENSOR = ("y_hi", "core")
PADDED_WIDTH = 256


def exchange(blocks, axes):
    return lax.all_to_all(blocks, axes, 0, 0, tiled=True)


def apply_rotary(vectors, token_positions):
    half_width = vectors.shape[-1] // 2
    frequency = jnp.exp(
        -jnp.log(500000.0) * jnp.arange(half_width, dtype=jnp.float32) * (2.0 / vectors.shape[-1])
    )
    angles = token_positions.astype(jnp.float32)[:, None] * frequency[None, :]
    cosine = jnp.cos(angles)[:, None, :]
    sine_part = jnp.sin(angles)[:, None, :]
    leading = vectors[..., :half_width]
    trailing = vectors[..., half_width:]
    return jnp.concatenate(
        [leading * cosine - trailing * sine_part, leading * sine_part + trailing * cosine], axis=-1
    )


def dot(left, right):
    return jnp.dot(left, right, preferred_element_type=jnp.float32)


def start_copies(pairs, arrived):
    copies = [
        pltpu.make_async_copy(source, held, arrived.at[number])
        for number, (source, held) in enumerate(pairs)
    ]
    for copy in copies:
        copy.start()
    return copies


def project_kernel(
    own_rows,
    gain_ref,
    tasks_ref,
    moves_ref,
    homes_ref,
    inputs_ref,
    adapter_ref,
    query_ref,
    key_ref,
    value_ref,
    out_ref,
    held_inputs,
    held_adapter,
    held_query,
    held_key,
    held_value,
    gained_ref,
    held_out,
    arrived,
    left,
):
    steps, all_rows, width = inputs_ref.shape
    every_row = steps * all_rows
    per_group = steps * own_rows
    query_width = query_ref.shape[1]
    head_dim = key_ref.shape[1]
    adapters, low, _ = adapter_ref.shape
    key_end = query_width + head_dim
    base_end = key_end + head_dim
    block = 128
    copies = start_copies(
        (
            (inputs_ref, held_inputs),
            (adapter_ref, held_adapter),
            (query_ref, held_query),
            (key_ref, held_key),
            (value_ref, held_value),
        ),
        arrived,
    )

    def lane(width):
        return lax.broadcasted_iota(jnp.int32, (block, width), 1)

    copies[0].wait()
    gathered = held_inputs[...].reshape(every_row, width)
    squares_of = []
    for first in range(0, every_row, block):
        row = first + lax.broadcasted_iota(jnp.int32, (block, 1), 0)
        place = row % per_group // own_rows * all_rows + row // per_group * own_rows + row % own_rows
        order = jnp.where(lane(every_row) == place, 1.0, 0.0).astype(jnp.bfloat16)
        states = dot(order, gathered)
        gained_ref[first : first + block, :] = (states * gain_ref[...]).astype(jnp.bfloat16)
        squares_of.append(jnp.sum(states * states, axis=1, keepdims=True))

    copies[1].wait()
    for index, squares in enumerate(squares_of):
        first = index * block

        row = first + lax.broadcasted_iota(jnp.int32, (block, 1), 0)
        own = lane(all_rows) == row // per_group * own_rows + row % own_rows
        task = jnp.sum(jnp.where(own, tasks_ref[...], 0), axis=1, keepdims=True)
        here = moves_ref[1:2, :] == row // per_group
        moved = jnp.sum(jnp.where(here, 1, 0), axis=1, keepdims=True) > 0
        chosen = jnp.sum(jnp.where(here, moves_ref[0:1, :], 0), axis=1, keepdims=True)
        late = row % per_group >= per_group // 2
        task = jnp.where(jnp.logical_and(late, moved), chosen, task)
        home = jnp.sum(
            jnp.where(lane(adapters) == task, homes_ref[...], 0), axis=1, keepdims=True
        ).astype(jnp.float32)
        gained = gained_ref[first : first + block, :]
        total = jnp.zeros((block, low), jnp.float32)
        for adapter in range(0, adapters, 2):
            both = [
                jnp.where(task == number, gained, jnp.zeros_like(gained))
                for number in (adapter, adapter + 1)
            ]
            total = total + lax.dot_general(
                jnp.concatenate(both, axis=1),
                jnp.concatenate([held_adapter[adapter], held_adapter[adapter + 1]], axis=1),
                (((1,), (1,)), ((), ())),
                preferred_element_type=jnp.float32,
            )
        rest = PADDED_WIDTH - low
        squares_high = squares.astype(jnp.bfloat16).astype(jnp.float32)
        extra = jnp.where(
            lane(rest) == 0,
            squares_high,
            jnp.where(
                lane(rest) == 1, squares - squares_high, jnp.where(lane(rest) == 2, home, 0.0)
            ),
        )
        held_out[first : first + block, base_end : base_end + PADDED_WIDTH] = jnp.concatenate(
            [total, extra], axis=1
        ).astype(jnp.bfloat16)

    for copy in copies[2:]:
        copy.wait()

    @pl.loop(0, every_row // block)
    def _(index):
        rows = pl.ds(pl.multiple_of(index * block, block), block)
        gained = gained_ref[rows, :]
        held_out[rows, 0:query_width] = dot(gained, held_query[...]).astype(jnp.bfloat16)
        held_out[rows, query_width:key_end] = dot(gained, held_key[...]).astype(jnp.bfloat16)
        held_out[rows, key_end:base_end] = dot(gained, held_value[...]).astype(jnp.bfloat16)
        pltpu.make_async_copy(held_out.at[rows], out_ref.at[rows], left.at[index]).start()

    for index in range(every_row // block):
        rows = pl.ds(index * block, block)
        pltpu.make_async_copy(held_out.at[rows], out_ref.at[rows], left.at[index]).wait()


def project(inputs, gain, w_query, w_key, w_value, adapter_in, tasks, moves, homes, own_rows):
    steps, all_rows, width = inputs.shape
    columns = w_query.shape[1] + w_key.shape[1] + w_value.shape[1] + PADDED_WIDTH
    large = (inputs, jnp.swapaxes(adapter_in, 1, 2), w_query, w_key, w_value)
    return pl.pallas_call(
        functools.partial(project_kernel, own_rows),
        out_shape=jax.ShapeDtypeStruct((steps * all_rows, columns), jnp.bfloat16),
        in_specs=[pl.BlockSpec(memory_space=pltpu.VMEM)] * 4
        + [pl.BlockSpec(memory_space=pl.ANY)] * len(large),
        out_specs=pl.BlockSpec(memory_space=pl.ANY),
        scratch_shapes=[pltpu.VMEM(array.shape, jnp.bfloat16) for array in large]
        + [
            pltpu.VMEM((steps * all_rows, width), jnp.bfloat16),
            pltpu.VMEM((steps * all_rows, columns), jnp.bfloat16),
            pltpu.SemaphoreType.DMA((len(large),)),
            pltpu.SemaphoreType.DMA((steps * all_rows // 128,)),
        ],
        cost_estimate=pl.CostEstimate(
            flops=2 * steps * all_rows * width * 3328, bytes_accessed=3_000_000, transcendentals=0
        ),
    )(gain[None, :], tasks[None, :], moves.T, homes[None, :], *large)


def low_kernel(low, parts_ref, low_ref):
    sources, rows, columns = parts_ref.shape
    targets, _, width = low_ref.shape
    total = parts_ref[0, :, columns - width :].astype(jnp.float32)
    for source in range(1, sources):
        total = total + parts_ref[source, :, columns - width :].astype(jnp.float32)
    lane = lax.broadcasted_iota(jnp.int32, total.shape, 1)
    terms = jnp.logical_or(lane == low, lane == low + 1)
    squares = jnp.sum(jnp.where(terms, total, 0.0), axis=1, keepdims=True)
    squares_high = squares.astype(jnp.bfloat16).astype(jnp.float32)
    total = jnp.where(
        lane == low,
        squares_high,
        jnp.where(lane == low + 1, squares - squares_high, total),
    ).astype(jnp.bfloat16)
    for target in range(targets):
        low_ref[target] = total


def sum_low(parts, base_end, low, depth):
    _, rows, columns = parts.shape
    return pl.pallas_call(
        functools.partial(low_kernel, low),
        out_shape=jax.ShapeDtypeStruct((depth, rows, columns - base_end), jnp.bfloat16),
        in_specs=[pl.BlockSpec(memory_space=pltpu.VMEM)],
        out_specs=pl.BlockSpec(memory_space=pltpu.VMEM),
        compiler_params=pltpu.CompilerParams(vmem_limit_bytes=16 * 1024 * 1024),
        cost_estimate=pl.CostEstimate(
            flops=parts.size // 6, bytes_accessed=parts.size // 3, transcendentals=0
        ),
    )(parts)


def lift_kernel(
    rank,
    head_dim,
    model_width,
    groups,
    low_ref,
    line_ref,
    other_ref,
    base_ref,
    out_ref,
):
    rows, columns = out_ref.shape
    line = line_ref.shape[0]
    low = 3 * rank
    total = low_ref[0].astype(jnp.float32)
    for source in range(1, low_ref.shape[0]):
        total = total + low_ref[source].astype(jnp.float32)
    lane = lax.broadcasted_iota(jnp.int32, total.shape, 1)
    terms = jnp.logical_or(lane == low, lane == low + 1)
    squares = jnp.sum(jnp.where(terms, total, 0.0), axis=1, keepdims=True)
    inverse = lax.rsqrt(squares / model_width + epsilon)
    lowrank = (inverse * total).astype(jnp.bfloat16)
    from_lane = lax.broadcasted_iota(jnp.int32, (PADDED_WIDTH, line * rank), 0)
    to_lane = lax.broadcasted_iota(jnp.int32, (PADDED_WIDTH, line * rank), 1)
    slot_lane = lax.broadcasted_iota(jnp.int32, (rows, line * rank), 1) // rank
    home = jnp.sum(jnp.where(lane == low + 2, total, 0.0), axis=1, keepdims=True) / groups
    home = home.astype(jnp.int32)
    depth = low_ref.shape[0]
    same_half = home // depth % 2 == lax.axis_index("y_lo")
    slot = home // (2 * depth) + jnp.where(same_half, 0, line)
    slot = jnp.where(home % depth == lax.axis_index("z"), slot, -1)
    spreads = []
    for number in range(3):
        pick = jnp.where(from_lane == number * rank + to_lane % rank, 1.0, 0.0)
        tiled = dot(lowrank, pick.astype(jnp.bfloat16))
        spreads.append(
            [
                jnp.where(slot == slot_lane + half * line, tiled, 0.0).astype(jnp.bfloat16)
                for half in range(2)
            ]
        )
    key_first, value_first = columns - 2 * head_dim, columns - head_dim
    bounds = ((0, key_first), (key_first, value_first), (value_first, columns))
    for (first, last), (near, far) in zip(bounds, spreads, strict=True):
        lifted = dot(near, line_ref[:, :, first:last].reshape(line * rank, last - first))
        lifted = lifted + dot(
            far, other_ref[:, :, first:last].reshape(line * rank, last - first)
        )
        out_ref[:, first:last] = (inverse * base_ref[:, first:last] + lifted).astype(jnp.bfloat16)


def lift(low_parts, base, up_line, up_other, rank, head_dim, model_width, groups):
    return pl.pallas_call(
        functools.partial(lift_kernel, rank, head_dim, model_width, groups),
        out_shape=jax.ShapeDtypeStruct(base.shape, jnp.bfloat16),
        in_specs=[pl.BlockSpec(memory_space=pltpu.VMEM)] * 4,
        out_specs=pl.BlockSpec(memory_space=pltpu.VMEM),
        compiler_params=pltpu.CompilerParams(vmem_limit_bytes=16 * 1024 * 1024),
        cost_estimate=pl.CostEstimate(
            flops=2 * base.size * up_line.shape[0] * 2 * rank,
            bytes_accessed=2_000_000,
            transcendentals=0,
        ),
    )(low_parts, up_line, up_other, base)


def repeat_kernel(rows_ref, out_ref):
    rows = rows_ref[...]
    for target in range(out_ref.shape[0]):
        out_ref[target] = rows


def repeat(rows, count):
    return pl.pallas_call(
        repeat_kernel,
        out_shape=jax.ShapeDtypeStruct((count, *rows.shape), rows.dtype),
        in_specs=[pl.BlockSpec(memory_space=pltpu.VMEM)],
        out_specs=pl.BlockSpec(memory_space=pltpu.VMEM),
        compiler_params=pltpu.CompilerParams(vmem_limit_bytes=16 * 1024 * 1024),
        cost_estimate=pl.CostEstimate(
            flops=0, bytes_accessed=2 * count * rows.size, transcendentals=0
        ),
    )(rows)


def attend(queries, cache_keys, value_cache, fresh_keys, fresh_values, lengths, query_steps):
    scaling = 1.0 / math.sqrt(queries.shape[-1])
    old_scores = (
        jnp.einsum("rnd,rjd->rnj", queries, cache_keys, preferred_element_type=jnp.float32)
        * scaling
    )
    new_scores = (
        jnp.einsum("rnd,rjd->rnj", queries, fresh_keys, preferred_element_type=jnp.float32)
        * scaling
    )
    visible = jnp.arange(cache_keys.shape[1])[None, None, :] < lengths[:, None, None]
    old_scores = jnp.where(visible, old_scores, -1e30)
    fresh = np.arange(fresh_keys.shape[1])[None, None, :] <= query_steps[None, :, None]
    new_scores = jnp.where(fresh, new_scores, -1e30)
    highest = jnp.maximum(jnp.max(old_scores, axis=-1), jnp.max(new_scores, axis=-1))[..., None]
    old_exp = jnp.exp(old_scores - highest)
    new_exp = jnp.exp(new_scores - highest)
    denominator = jnp.sum(old_exp, axis=-1, keepdims=True) + jnp.sum(
        new_exp, axis=-1, keepdims=True
    )
    old_weights = (old_exp / denominator).astype(jnp.bfloat16)
    new_weights = (new_exp / denominator).astype(jnp.bfloat16)
    mixed = jnp.einsum(
        "rnj,rjd->rnd", old_weights, value_cache, preferred_element_type=jnp.float32
    )
    mixed = mixed + jnp.einsum(
        "rnj,rjd->rnd", new_weights, fresh_values, preferred_element_type=jnp.float32
    )
    return mixed.astype(jnp.bfloat16)


def on_device(
    inputs,
    gain,
    w_query,
    key_projection_weight,
    value_projection_weight,
    w_output,
    adapter_in,
    adapter_attn,
    adapter_out,
    pool_query,
    slot_keyvalue_matrices,
    cache_keys,
    value_cache,
    tasks,
    homes,
    moves,
    lengths,
):
    steps, all_rows, width_part = inputs.shape
    own_rows = lengths.shape[0]
    groups = all_rows // own_rows
    planes = lax.axis_size(PLANE)
    line = lax.axis_size("x")
    depth = lax.axis_size("z")
    task_count = homes.shape[0]
    rank = adapter_out.shape[1]
    head_dim = cache_keys.shape[3]
    query_width = w_query.shape[1]
    heads = query_width // head_dim
    key_end = query_width + head_dim
    base_end = key_end + head_dim
    per_group = steps * own_rows
    every_row = groups * per_group
    model_width = width_part * groups
    column_rows = depth * per_group

    partial = project(
        inputs,
        gain,
        w_query,
        key_projection_weight,
        value_projection_weight,
        adapter_in,
        tasks,
        moves,
        homes,
        own_rows,
    )
    partial, pool_query, slot_keyvalue_matrices = lax.optimization_barrier(
        (partial, pool_query, slot_keyvalue_matrices)
    )
    with jax.named_scope("sum_plane"):
        by_plane = exchange(partial.reshape(planes, column_rows, -1), PLANE)

    up = jnp.concatenate(
        [
            pool_query.reshape(rank, query_width),
            slot_keyvalue_matrices.reshape(rank, 2 * head_dim),
        ],
        axis=1,
    )
    with jax.named_scope("up_x"):
        up_line = lax.all_gather(up, "x", axis=0)
    with jax.named_scope("up_y_lo"):
        up_other = lax.ppermute(up_line, "y_lo", [(0, 1), (1, 0)])
    low_part = sum_low(by_plane, base_end, 3 * rank, depth)
    plane_sum = jnp.sum(by_plane[:, :, :base_end].astype(jnp.float32), axis=0)
    with jax.named_scope("sum_low"):
        low_parts = exchange(low_part, "z")

    raw_part = lift(
        low_parts, plane_sum, up_line, up_other, rank, head_dim, model_width, groups
    )
    with jax.named_scope("sum_z"):
        by_depth = exchange(raw_part.reshape(depth, per_group, base_end), "z")
    raw = jnp.sum(by_depth.astype(jnp.float32), axis=0)

    row_step = jnp.arange(per_group) // own_rows
    positions = jnp.tile(lengths, steps) + row_step
    queries = apply_rotary(raw[:, :query_width].reshape(per_group, heads, head_dim), positions)
    new_keys = apply_rotary(
        raw[:, query_width:key_end].reshape(per_group, 1, head_dim), positions
    )
    raw_value = raw[:, key_end:]

    def by_row(array):
        return (
            array.astype(jnp.bfloat16)
            .reshape(steps, own_rows, -1, head_dim)
            .transpose(1, 0, 2, 3)
            .reshape(own_rows, -1, head_dim)
        )

    attended = attend(
        by_row(queries),
        cache_keys.reshape(own_rows, -1, head_dim),
        value_cache.reshape(own_rows, -1, head_dim),
        by_row(new_keys),
        by_row(raw_value),
        lengths,
        np.arange(steps * heads) // heads,
    )
    attended = (
        attended.reshape(own_rows, steps, query_width)
        .transpose(1, 0, 2)
        .reshape(per_group, query_width)
    )

    with jax.named_scope("gather_z"):
        column = exchange(
            jnp.broadcast_to(attended[None], (depth, per_group, query_width)), "z"
        ).reshape(depth * per_group, query_width)
    column, tasks, moves = lax.optimization_barrier((column, tasks, moves))
    with jax.named_scope("gather_plane"):
        piece_rows = exchange(repeat(column, planes), PLANE).reshape(every_row, query_width)

    group_tasks = tasks.reshape(groups, own_rows)
    matched = moves[:, 1][None, :] == jnp.arange(groups, dtype=jnp.int32)[:, None]
    moved = jnp.any(matched, axis=1)
    chosen = jnp.sum(jnp.where(matched, moves[:, 0][None, :], 0), axis=1)
    late = jnp.where(moved[:, None], chosen[:, None], group_tasks)
    active = jnp.stack([group_tasks if s < steps // 2 else late for s in range(steps)], axis=1)
    active = active.reshape(every_row)
    marks = active[:, None] == jnp.arange(task_count, dtype=jnp.int32)[None, :]

    every_reduced = jnp.einsum(
        "rq,tqc->rtc", piece_rows, adapter_attn, preferred_element_type=jnp.float32
    )
    reduced = jnp.where(marks[:, :, None], every_reduced, 0).astype(jnp.bfloat16)
    mixed = dot(piece_rows, w_output) + dot(
        reduced.reshape(every_row, task_count * rank),
        adapter_out.reshape(task_count * rank, width_part),
    )
    mixed = mixed.astype(jnp.bfloat16)
    core = lax.axis_index("core")
    cores = lax.axis_size("core")
    half = steps // cores
    with jax.named_scope("sum_core"):
        pair = lax.all_gather(mixed, "core", axis=0)
    mine = lax.dynamic_slice_in_dim(
        pair.reshape(cores, groups, steps, own_rows, width_part), core * half, half, 2
    ).astype(jnp.float32)
    mine = jnp.sum(mine, axis=0)
    mine = mine.transpose(1, 0, 2, 3).reshape(half, all_rows, width_part)
    for pairs in ([[0, 1], [2, 3]], [[1, 2], [3, 0]]):
        with jax.named_scope("sum_y_hi"):
            both = lax.all_gather(
                mine.astype(jnp.bfloat16), "y_hi", axis=0, axis_index_groups=pairs
            )
        mine = both[0].astype(jnp.float32) + both[1].astype(jnp.float32)
    residual = lax.dynamic_slice_in_dim(inputs, core * half, half, 0)
    finished = (residual.astype(jnp.float32) + mine).astype(jnp.bfloat16)
    with jax.named_scope("gather_core"):
        return lax.all_gather(finished, "core", axis=0, tiled=True)


def solution(mesh):
    parts = Mesh(mesh.devices.reshape(4, 2, 8, 4, 2), GROUP + TENSOR)
    return jax.shard_map(
        on_device,
        mesh=parts,
        in_specs=(
            P(None, None, GROUP),
            P(GROUP),
            P(GROUP, TENSOR),
            P(GROUP, TENSOR),
            P(GROUP, TENSOR),
            P(TENSOR, GROUP),
            P(None, GROUP, None),
            P(None, TENSOR, None),
            P(None, None, GROUP),
            P(GROUP, None, TENSOR),
            P(GROUP, None, None, TENSOR),
            P(GROUP, TENSOR, None, None),
            P(GROUP, TENSOR, None, None),
            P(),
            P(),
            P(),
            P(GROUP),
        ),
        out_specs=P(None, None, GROUP),
        check_vma=False,
    )
```

```python
import functools
import math

import jax
import jax.numpy as jnp
import numpy as np
from jax import lax
from jax.experimental import pallas as pl
from jax.experimental.pallas import tpu as pltpu
from jax.sharding import Mesh
from jax.sharding import PartitionSpec as P

epsilon = 1e-05
GROUP = ("x", "y_lo", "z")
PLANE = ("x", "y_lo")
TENSOR = ("y_hi", "core")
PADDED_WIDTH = 256


def exchange(blocks, axes):
    return lax.all_to_all(blocks, axes, 0, 0, tiled=True)


def apply_rotary(vectors, token_positions):
    half_width = vectors.shape[-1] // 2
    frequency = jnp.exp(
        -jnp.log(500000.0) * jnp.arange(half_width, dtype=jnp.float32) * (2.0 / vectors.shape[-1])
    )
    angles = token_positions.astype(jnp.float32)[:, None] * frequency[None, :]
    cosine = jnp.cos(angles)[:, None, :]
    sine_part = jnp.sin(angles)[:, None, :]
    leading = vectors[..., :half_width]
    trailing = vectors[..., half_width:]
    return jnp.concatenate(
        [leading * cosine - trailing * sine_part, leading * sine_part + trailing * cosine], axis=-1
    )


def dot(left, right):
    return jnp.dot(left, right, preferred_element_type=jnp.float32)


def start_copies(pairs, arrived):
    copies = [
        pltpu.make_async_copy(source, held, arrived.at[number])
        for number, (source, held) in enumerate(pairs)
    ]
    for copy in copies:
        copy.start()
    return copies


def row_tasks(row, own_rows, per_group, tasks_ref, moves_ref):
    group = row // per_group
    tasks, moves = tasks_ref.shape[1], moves_ref.shape[1]
    lane = lax.broadcasted_iota(jnp.int32, (row.shape[0], tasks), 1)
    own = lane == group * own_rows + row % own_rows
    task = jnp.sum(jnp.where(own, tasks_ref[...], 0), axis=1, keepdims=True)
    here = moves_ref[1:2, :] == jnp.broadcast_to(group, (row.shape[0], moves))
    moved = jnp.sum(jnp.where(here, 1, 0), axis=1, keepdims=True) > 0
    chosen = jnp.sum(jnp.where(here, moves_ref[0:1, :], 0), axis=1, keepdims=True)
    late = row % per_group >= per_group // 2
    return jnp.where(jnp.logical_and(late, moved), chosen, task)


def project_kernel(
    own_rows,
    gain_ref,
    tasks_ref,
    moves_ref,
    homes_ref,
    inputs_ref,
    adapter_ref,
    query_ref,
    key_ref,
    value_ref,
    out_ref,
    held_inputs,
    held_adapter,
    held_query,
    held_key,
    held_value,
    gained_ref,
    held_out,
    arrived,
    left,
):
    steps, all_rows, width = inputs_ref.shape
    every_row = steps * all_rows
    per_group = steps * own_rows
    query_width = query_ref.shape[1]
    head_dim = key_ref.shape[1]
    adapters, low, _ = adapter_ref.shape
    key_end = query_width + head_dim
    base_end = key_end + head_dim
    block = 128
    copies = start_copies(
        (
            (inputs_ref, held_inputs),
            (adapter_ref, held_adapter),
            (query_ref, held_query),
            (key_ref, held_key),
            (value_ref, held_value),
        ),
        arrived,
    )

    def lane(width):
        return lax.broadcasted_iota(jnp.int32, (block, width), 1)

    copies[0].wait()
    gathered = held_inputs[...].reshape(every_row, width)
    squares_of = []
    for first in range(0, every_row, block):
        row = first + lax.broadcasted_iota(jnp.int32, (block, 1), 0)
        place = row % per_group // own_rows * all_rows + row // per_group * own_rows + row % own_rows
        order = jnp.where(lane(every_row) == place, 1.0, 0.0).astype(jnp.bfloat16)
        states = dot(order, gathered)
        gained_ref[first : first + block, :] = (states * gain_ref[...]).astype(jnp.bfloat16)
        squares_of.append(jnp.sum(states * states, axis=1, keepdims=True))

    copies[1].wait()
    for index, squares in enumerate(squares_of):
        first = index * block

        row = first + lax.broadcasted_iota(jnp.int32, (block, 1), 0)
        task = row_tasks(row, own_rows, per_group, tasks_ref, moves_ref)
        home = jnp.sum(
            jnp.where(lane(adapters) == task, homes_ref[...], 0), axis=1, keepdims=True
        ).astype(jnp.float32)
        gained = gained_ref[first : first + block, :]
        total = jnp.zeros((block, low), jnp.float32)
        for adapter in range(0, adapters, 2):
            both = [
                jnp.where(task == number, gained, jnp.zeros_like(gained))
                for number in (adapter, adapter + 1)
            ]
            total = total + lax.dot_general(
                jnp.concatenate(both, axis=1),
                jnp.concatenate([held_adapter[adapter], held_adapter[adapter + 1]], axis=1),
                (((1,), (1,)), ((), ())),
                preferred_element_type=jnp.float32,
            )
        rest = PADDED_WIDTH - low
        squares_high = squares.astype(jnp.bfloat16).astype(jnp.float32)
        extra = jnp.where(
            lane(rest) == 0,
            squares_high,
            jnp.where(
                lane(rest) == 1, squares - squares_high, jnp.where(lane(rest) == 2, home, 0.0)
            ),
        )
        held_out[first : first + block, base_end : base_end + PADDED_WIDTH] = jnp.concatenate(
            [total, extra], axis=1
        ).astype(jnp.bfloat16)

    for copy in copies[2:]:
        copy.wait()

    @pl.loop(0, every_row // block)
    def _(index):
        rows = pl.ds(pl.multiple_of(index * block, block), block)
        gained = gained_ref[rows, :]
        held_out[rows, 0:query_width] = dot(gained, held_query[...]).astype(jnp.bfloat16)
        held_out[rows, query_width:key_end] = dot(gained, held_key[...]).astype(jnp.bfloat16)
        held_out[rows, key_end:base_end] = dot(gained, held_value[...]).astype(jnp.bfloat16)
        pltpu.make_async_copy(held_out.at[rows], out_ref.at[rows], left.at[index]).start()

    for index in range(every_row // block):
        rows = pl.ds(index * block, block)
        pltpu.make_async_copy(held_out.at[rows], out_ref.at[rows], left.at[index]).wait()


def project(inputs, gain, w_query, w_key, w_value, adapter_in, tasks, moves, homes, own_rows):
    steps, all_rows, width = inputs.shape
    columns = w_query.shape[1] + w_key.shape[1] + w_value.shape[1] + PADDED_WIDTH
    large = (inputs, jnp.swapaxes(adapter_in, 1, 2), w_query, w_key, w_value)
    return pl.pallas_call(
        functools.partial(project_kernel, own_rows),
        out_shape=jax.ShapeDtypeStruct((steps * all_rows, columns), jnp.bfloat16),
        in_specs=[pl.BlockSpec(memory_space=pltpu.VMEM)] * 4
        + [pl.BlockSpec(memory_space=pl.ANY)] * len(large),
        out_specs=pl.BlockSpec(memory_space=pl.ANY),
        scratch_shapes=[pltpu.VMEM(array.shape, jnp.bfloat16) for array in large]
        + [
            pltpu.VMEM((steps * all_rows, width), jnp.bfloat16),
            pltpu.VMEM((steps * all_rows, columns), jnp.bfloat16),
            pltpu.SemaphoreType.DMA((len(large),)),
            pltpu.SemaphoreType.DMA((steps * all_rows // 128,)),
        ],
        cost_estimate=pl.CostEstimate(
            flops=2 * steps * all_rows * width * 3328, bytes_accessed=3_000_000, transcendentals=0
        ),
    )(gain[None, :], tasks[None, :], moves.T, homes[None, :], *large)


def low_kernel(low, parts_ref, low_ref):
    sources, rows, columns = parts_ref.shape
    targets, _, width = low_ref.shape
    total = parts_ref[0, :, columns - width :].astype(jnp.float32)
    for source in range(1, sources):
        total = total + parts_ref[source, :, columns - width :].astype(jnp.float32)
    lane = lax.broadcasted_iota(jnp.int32, total.shape, 1)
    terms = jnp.logical_or(lane == low, lane == low + 1)
    squares = jnp.sum(jnp.where(terms, total, 0.0), axis=1, keepdims=True)
    squares_high = squares.astype(jnp.bfloat16).astype(jnp.float32)
    total = jnp.where(
        lane == low,
        squares_high,
        jnp.where(lane == low + 1, squares - squares_high, total),
    ).astype(jnp.bfloat16)
    for target in range(targets):
        low_ref[target] = total


def sum_low(parts, base_end, low, depth):
    _, rows, columns = parts.shape
    return pl.pallas_call(
        functools.partial(low_kernel, low),
        out_shape=jax.ShapeDtypeStruct((depth, rows, columns - base_end), jnp.bfloat16),
        in_specs=[pl.BlockSpec(memory_space=pltpu.VMEM)],
        out_specs=pl.BlockSpec(memory_space=pltpu.VMEM),
        compiler_params=pltpu.CompilerParams(vmem_limit_bytes=16 * 1024 * 1024),
        cost_estimate=pl.CostEstimate(
            flops=parts.size // 6, bytes_accessed=parts.size // 3, transcendentals=0
        ),
    )(parts)


def lift_kernel(
    rank,
    head_dim,
    model_width,
    groups,
    low_ref,
    line_ref,
    other_ref,
    base_ref,
    out_ref,
):
    rows, columns = out_ref.shape
    line = line_ref.shape[0]
    low = 3 * rank
    total = low_ref[0].astype(jnp.float32)
    for source in range(1, low_ref.shape[0]):
        total = total + low_ref[source].astype(jnp.float32)
    lane = lax.broadcasted_iota(jnp.int32, total.shape, 1)
    terms = jnp.logical_or(lane == low, lane == low + 1)
    squares = jnp.sum(jnp.where(terms, total, 0.0), axis=1, keepdims=True)
    inverse = lax.rsqrt(squares / model_width + epsilon)
    lowrank = (inverse * total).astype(jnp.bfloat16)
    from_lane = lax.broadcasted_iota(jnp.int32, (PADDED_WIDTH, line * rank), 0)
    to_lane = lax.broadcasted_iota(jnp.int32, (PADDED_WIDTH, line * rank), 1)
    slot_lane = lax.broadcasted_iota(jnp.int32, (rows, line * rank), 1) // rank
    home = jnp.sum(jnp.where(lane == low + 2, total, 0.0), axis=1, keepdims=True) / groups
    home = home.astype(jnp.int32)
    depth = low_ref.shape[0]
    same_half = home // depth % 2 == lax.axis_index("y_lo")
    slot = home // (2 * depth) + jnp.where(same_half, 0, line)
    slot = jnp.where(home % depth == lax.axis_index("z"), slot, -1)
    spreads = []
    for number in range(3):
        pick = jnp.where(from_lane == number * rank + to_lane % rank, 1.0, 0.0)
        tiled = dot(lowrank, pick.astype(jnp.bfloat16))
        spreads.append(
            [
                jnp.where(slot == slot_lane + half * line, tiled, 0.0).astype(jnp.bfloat16)
                for half in range(2)
            ]
        )
    key_first, value_first = columns - 2 * head_dim, columns - head_dim
    bounds = ((0, key_first), (key_first, value_first), (value_first, columns))
    for (first, last), (near, far) in zip(bounds, spreads, strict=True):
        lifted = dot(near, line_ref[:, :, first:last].reshape(line * rank, last - first))
        lifted = lifted + dot(
            far, other_ref[:, :, first:last].reshape(line * rank, last - first)
        )
        out_ref[:, first:last] = (inverse * base_ref[:, first:last] + lifted).astype(jnp.bfloat16)


def lift(low_parts, base, up_line, up_other, rank, head_dim, model_width, groups):
    return pl.pallas_call(
        functools.partial(lift_kernel, rank, head_dim, model_width, groups),
        out_shape=jax.ShapeDtypeStruct(base.shape, jnp.bfloat16),
        in_specs=[pl.BlockSpec(memory_space=pltpu.VMEM)] * 4,
        out_specs=pl.BlockSpec(memory_space=pltpu.VMEM),
        compiler_params=pltpu.CompilerParams(vmem_limit_bytes=16 * 1024 * 1024),
        cost_estimate=pl.CostEstimate(
            flops=2 * base.size * up_line.shape[0] * 2 * rank,
            bytes_accessed=2_000_000,
            transcendentals=0,
        ),
    )(low_parts, up_line, up_other, base)


def output_kernel(
    own_rows,
    steps,
    tasks_ref,
    moves_ref,
    rows_ref,
    down_ref,
    weight_ref,
    up_ref,
    out_ref,
    held_weight,
    held_up,
    held_out,
    arrived,
):
    copies = start_copies(((weight_ref, held_weight), (up_ref, held_up)), arrived)
    every_row, _ = rows_ref.shape
    adapters, rank, width = down_ref.shape
    per_group = steps * own_rows
    all_rows = every_row // steps
    block = 128
    down = down_ref[...].reshape(adapters * rank, width)
    for first in range(0, every_row, block):
        row = first + lax.broadcasted_iota(jnp.int32, (block, 1), 0)
        task = row_tasks(row, own_rows, per_group, tasks_ref, moves_ref)
        rows = rows_ref[first : first + block, :]
        reduced = lax.dot_general(
            rows, down, (((1,), (1,)), ((), ())), preferred_element_type=jnp.float32
        )
        owner = lax.broadcasted_iota(jnp.int32, reduced.shape, 1) // rank
        reduced = jnp.where(owner == task, reduced, 0.0).astype(jnp.bfloat16)
        if first == 0:
            for copy in copies:
                copy.wait()
        total = dot(rows, held_weight[...]) + dot(
            reduced, held_up[...].reshape(adapters * rank, out_ref.shape[1])
        )
        held_out[first : first + block, :] = total.astype(jnp.bfloat16)
    for first in range(0, every_row, block):
        row = first + lax.broadcasted_iota(jnp.int32, (block, 1), 0)
        place = row % all_rows // own_rows * per_group + row // all_rows * own_rows + row % own_rows
        lane = lax.broadcasted_iota(jnp.int32, (block, every_row), 1)
        order = jnp.where(lane == place, 1.0, 0.0).astype(jnp.bfloat16)
        out_ref[first : first + block, :] = dot(order, held_out[...]).astype(jnp.bfloat16)


def output(rows, w_output, adapter_attn, adapter_out, tasks, moves, own_rows, steps):
    every_row, width = rows.shape
    columns = w_output.shape[1]
    return pl.pallas_call(
        functools.partial(output_kernel, own_rows, steps),
        out_shape=jax.ShapeDtypeStruct((every_row, columns), jnp.bfloat16),
        in_specs=[pl.BlockSpec(memory_space=pltpu.VMEM)] * 4
        + [pl.BlockSpec(memory_space=pl.ANY)] * 2,
        out_specs=pl.BlockSpec(memory_space=pltpu.VMEM),
        scratch_shapes=[
            pltpu.VMEM(w_output.shape, jnp.bfloat16),
            pltpu.VMEM(adapter_out.shape, jnp.bfloat16),
            pltpu.VMEM((every_row, columns), jnp.bfloat16),
            pltpu.SemaphoreType.DMA((2,)),
        ],
        compiler_params=pltpu.CompilerParams(vmem_limit_bytes=16 * 1024 * 1024),
        cost_estimate=pl.CostEstimate(
            flops=2 * every_row * width * 640, bytes_accessed=3_000_000, transcendentals=0
        ),
    )(
        tasks[None, :],
        moves.T,
        rows,
        jnp.swapaxes(adapter_attn, 1, 2),
        w_output,
        adapter_out,
    )


def attend(queries, cache_keys, value_cache, fresh_keys, fresh_values, lengths, query_steps):
    scaling = 1.0 / math.sqrt(queries.shape[-1])
    old_scores = (
        jnp.einsum("rnd,rjd->rnj", queries, cache_keys, preferred_element_type=jnp.float32)
        * scaling
    )
    new_scores = (
        jnp.einsum("rnd,rjd->rnj", queries, fresh_keys, preferred_element_type=jnp.float32)
        * scaling
    )
    visible = jnp.arange(cache_keys.shape[1])[None, None, :] < lengths[:, None, None]
    old_scores = jnp.where(visible, old_scores, -1e30)
    fresh = np.arange(fresh_keys.shape[1])[None, None, :] <= query_steps[None, :, None]
    new_scores = jnp.where(fresh, new_scores, -1e30)
    highest = jnp.maximum(jnp.max(old_scores, axis=-1), jnp.max(new_scores, axis=-1))[..., None]
    old_exp = jnp.exp(old_scores - highest)
    new_exp = jnp.exp(new_scores - highest)
    denominator = jnp.sum(old_exp, axis=-1, keepdims=True) + jnp.sum(
        new_exp, axis=-1, keepdims=True
    )
    old_weights = (old_exp / denominator).astype(jnp.bfloat16)
    new_weights = (new_exp / denominator).astype(jnp.bfloat16)
    mixed = jnp.einsum(
        "rnj,rjd->rnd", old_weights, value_cache, preferred_element_type=jnp.float32
    )
    mixed = mixed + jnp.einsum(
        "rnj,rjd->rnd", new_weights, fresh_values, preferred_element_type=jnp.float32
    )
    return mixed.astype(jnp.bfloat16)


def on_device(
    inputs,
    gain,
    w_query,
    key_projection_weight,
    value_projection_weight,
    w_output,
    adapter_in,
    adapter_attn,
    adapter_out,
    pool_query,
    slot_keyvalue_matrices,
    cache_keys,
    value_cache,
    tasks,
    homes,
    moves,
    lengths,
):
    steps, all_rows, width_part = inputs.shape
    own_rows = lengths.shape[0]
    groups = all_rows // own_rows
    planes = lax.axis_size(PLANE)
    line = lax.axis_size("x")
    depth = lax.axis_size("z")
    task_count = homes.shape[0]
    rank = adapter_out.shape[1]
    head_dim = cache_keys.shape[3]
    query_width = w_query.shape[1]
    heads = query_width // head_dim
    key_end = query_width + head_dim
    base_end = key_end + head_dim
    per_group = steps * own_rows
    every_row = groups * per_group
    model_width = width_part * groups
    column_rows = depth * per_group

    partial = project(
        inputs,
        gain,
        w_query,
        key_projection_weight,
        value_projection_weight,
        adapter_in,
        tasks,
        moves,
        homes,
        own_rows,
    )
    partial, pool_query, slot_keyvalue_matrices = lax.optimization_barrier(
        (partial, pool_query, slot_keyvalue_matrices)
    )
    with jax.named_scope("sum_plane"):
        by_plane = exchange(partial.reshape(planes, column_rows, -1), PLANE)

    up = jnp.concatenate(
        [
            pool_query.reshape(rank, query_width),
            slot_keyvalue_matrices.reshape(rank, 2 * head_dim),
        ],
        axis=1,
    )
    with jax.named_scope("up_x"):
        up_line = lax.all_gather(up, "x", axis=0)
    with jax.named_scope("up_y_lo"):
        up_other = lax.ppermute(up_line, "y_lo", [(0, 1), (1, 0)])
    low_part = sum_low(by_plane, base_end, 3 * rank, depth)
    plane_sum = jnp.sum(by_plane[:, :, :base_end].astype(jnp.float32), axis=0)
    with jax.named_scope("sum_low"):
        low_parts = exchange(low_part, "z")

    raw_part = lift(
        low_parts, plane_sum, up_line, up_other, rank, head_dim, model_width, groups
    )
    with jax.named_scope("sum_z"):
        by_depth = exchange(raw_part.reshape(depth, per_group, base_end), "z")
    raw = jnp.sum(by_depth.astype(jnp.float32), axis=0)

    row_step = jnp.arange(per_group) // own_rows
    positions = jnp.tile(lengths, steps) + row_step
    queries = apply_rotary(raw[:, :query_width].reshape(per_group, heads, head_dim), positions)
    new_keys = apply_rotary(
        raw[:, query_width:key_end].reshape(per_group, 1, head_dim), positions
    )
    raw_value = raw[:, key_end:]

    def by_row(array):
        return (
            array.astype(jnp.bfloat16)
            .reshape(steps, own_rows, -1, head_dim)
            .transpose(1, 0, 2, 3)
            .reshape(own_rows, -1, head_dim)
        )

    attended = attend(
        by_row(queries),
        cache_keys.reshape(own_rows, -1, head_dim),
        value_cache.reshape(own_rows, -1, head_dim),
        by_row(new_keys),
        by_row(raw_value),
        lengths,
        np.arange(steps * heads) // heads,
    )
    attended = (
        attended.reshape(own_rows, steps, query_width)
        .transpose(1, 0, 2)
        .reshape(per_group, query_width)
    )

    with jax.named_scope("gather_z"):
        column = exchange(
            jnp.broadcast_to(attended[None], (depth, per_group, query_width)), "z"
        ).reshape(depth * per_group, query_width)
    with jax.named_scope("gather_plane"):
        piece_rows = exchange(
            jnp.broadcast_to(column[None], (planes, depth * per_group, query_width)), PLANE
        ).reshape(every_row, query_width)

    mixed = output(
        piece_rows, w_output, adapter_attn, adapter_out, tasks, moves, own_rows, steps
    )
    with jax.named_scope("sum_core"):
        both = lax.all_gather(mixed, "core", axis=0)
    total = both[0].astype(jnp.float32) + both[1].astype(jnp.float32)
    for pairs in ([[0, 1], [2, 3]], [[1, 2], [3, 0]]):
        with jax.named_scope("sum_y_hi"):
            both = lax.all_gather(
                total.astype(jnp.bfloat16), "y_hi", axis=0, axis_index_groups=pairs
            )
        total = both[0].astype(jnp.float32) + both[1].astype(jnp.float32)
    finished = inputs.astype(jnp.float32) + total.reshape(inputs.shape)
    return finished.astype(jnp.bfloat16)


def solution(mesh):
    parts = Mesh(mesh.devices.reshape(4, 2, 8, 4, 2), GROUP + TENSOR)
    return jax.shard_map(
        on_device,
        mesh=parts,
        in_specs=(
            P(None, None, GROUP),
            P(GROUP),
            P(GROUP, TENSOR),
            P(GROUP, TENSOR),
            P(GROUP, TENSOR),
            P(TENSOR, GROUP),
            P(None, GROUP, None),
            P(None, TENSOR, None),
            P(None, None, GROUP),
            P(GROUP, None, TENSOR),
            P(GROUP, None, None, TENSOR),
            P(GROUP, TENSOR, None, None),
            P(GROUP, TENSOR, None, None),
            P(),
            P(),
            P(),
            P(GROUP),
        ),
        out_specs=P(None, None, GROUP),
        check_vma=False,
    )
```

```python
import functools
import math

import jax
import jax.numpy as jnp
import numpy as np
from jax import lax
from jax.experimental import pallas as pl
from jax.experimental.pallas import tpu as pltpu
from jax.sharding import Mesh
from jax.sharding import PartitionSpec as P

epsilon = 1e-05
GROUP = ("x", "y_lo", "z")
PLANE = ("x", "y_lo")
TENSOR = ("y_hi", "core")
PADDED_WIDTH = 256


def exchange(blocks, axes):
    return lax.all_to_all(blocks, axes, 0, 0, tiled=True)


def apply_rotary(vectors, token_positions):
    half_width = vectors.shape[-1] // 2
    frequency = jnp.exp(
        -jnp.log(500000.0) * jnp.arange(half_width, dtype=jnp.float32) * (2.0 / vectors.shape[-1])
    )
    angles = token_positions.astype(jnp.float32)[:, None] * frequency[None, :]
    cosine = jnp.cos(angles)[:, None, :]
    sine_part = jnp.sin(angles)[:, None, :]
    leading = vectors[..., :half_width]
    trailing = vectors[..., half_width:]
    return jnp.concatenate(
        [leading * cosine - trailing * sine_part, leading * sine_part + trailing * cosine], axis=-1
    )


def dot(left, right):
    return jnp.dot(left, right, preferred_element_type=jnp.float32)


def start_copies(pairs, arrived):
    copies = [
        pltpu.make_async_copy(source, held, arrived.at[number])
        for number, (source, held) in enumerate(pairs)
    ]
    for copy in copies:
        copy.start()
    return copies


def row_tasks(row, own_rows, per_group, tasks_ref, moves_ref):
    group = row // per_group
    tasks, moves = tasks_ref.shape[1], moves_ref.shape[1]
    lane = lax.broadcasted_iota(jnp.int32, (row.shape[0], tasks), 1)
    own = lane == group * own_rows + row % own_rows
    task = jnp.sum(jnp.where(own, tasks_ref[...], 0), axis=1, keepdims=True)
    here = moves_ref[1:2, :] == jnp.broadcast_to(group, (row.shape[0], moves))
    moved = jnp.sum(jnp.where(here, 1, 0), axis=1, keepdims=True) > 0
    chosen = jnp.sum(jnp.where(here, moves_ref[0:1, :], 0), axis=1, keepdims=True)
    late = row % per_group >= per_group // 2
    return jnp.where(jnp.logical_and(late, moved), chosen, task)


def project_kernel(
    own_rows,
    gain_ref,
    tasks_ref,
    moves_ref,
    homes_ref,
    inputs_ref,
    adapter_ref,
    query_ref,
    key_ref,
    value_ref,
    out_ref,
    held_inputs,
    held_adapter,
    held_query,
    held_key,
    held_value,
    gained_ref,
    held_out,
    arrived,
    left,
):
    steps, all_rows, width = inputs_ref.shape
    every_row = steps * all_rows
    per_group = steps * own_rows
    query_width = query_ref.shape[1]
    head_dim = key_ref.shape[1]
    adapters, low, _ = adapter_ref.shape
    key_end = query_width + head_dim
    base_end = key_end + head_dim
    block = 128
    copies = start_copies(
        (
            (inputs_ref, held_inputs),
            (adapter_ref, held_adapter),
            (query_ref, held_query),
            (key_ref, held_key),
            (value_ref, held_value),
        ),
        arrived,
    )

    def lane(width):
        return lax.broadcasted_iota(jnp.int32, (block, width), 1)

    copies[0].wait()
    gathered = held_inputs[...].reshape(every_row, width)
    squares_of = []
    for first in range(0, every_row, block):
        row = first + lax.broadcasted_iota(jnp.int32, (block, 1), 0)
        place = row % per_group // own_rows * all_rows + row // per_group * own_rows + row % own_rows
        order = jnp.where(lane(every_row) == place, 1.0, 0.0).astype(jnp.bfloat16)
        states = dot(order, gathered)
        gained_ref[first : first + block, :] = (states * gain_ref[...]).astype(jnp.bfloat16)
        squares_of.append(jnp.sum(states * states, axis=1, keepdims=True))

    copies[1].wait()
    for index, squares in enumerate(squares_of):
        first = index * block

        row = first + lax.broadcasted_iota(jnp.int32, (block, 1), 0)
        task = row_tasks(row, own_rows, per_group, tasks_ref, moves_ref)
        home = jnp.sum(
            jnp.where(lane(adapters) == task, homes_ref[...], 0), axis=1, keepdims=True
        ).astype(jnp.float32)
        gained = gained_ref[first : first + block, :]
        total = jnp.zeros((block, low), jnp.float32)
        for adapter in range(0, adapters, 2):
            both = [
                jnp.where(task == number, gained, jnp.zeros_like(gained))
                for number in (adapter, adapter + 1)
            ]
            total = total + lax.dot_general(
                jnp.concatenate(both, axis=1),
                jnp.concatenate([held_adapter[adapter], held_adapter[adapter + 1]], axis=1),
                (((1,), (1,)), ((), ())),
                preferred_element_type=jnp.float32,
            )
        rest = PADDED_WIDTH - low
        squares_high = squares.astype(jnp.bfloat16).astype(jnp.float32)
        extra = jnp.where(
            lane(rest) == 0,
            squares_high,
            jnp.where(
                lane(rest) == 1, squares - squares_high, jnp.where(lane(rest) == 2, home, 0.0)
            ),
        )
        held_out[first : first + block, base_end : base_end + PADDED_WIDTH] = jnp.concatenate(
            [total, extra], axis=1
        ).astype(jnp.bfloat16)

    for copy in copies[2:]:
        copy.wait()

    @pl.loop(0, every_row // block)
    def _(index):
        rows = pl.ds(pl.multiple_of(index * block, block), block)
        gained = gained_ref[rows, :]
        held_out[rows, 0:query_width] = dot(gained, held_query[...]).astype(jnp.bfloat16)
        held_out[rows, query_width:key_end] = dot(gained, held_key[...]).astype(jnp.bfloat16)
        held_out[rows, key_end:base_end] = dot(gained, held_value[...]).astype(jnp.bfloat16)
        pltpu.make_async_copy(held_out.at[rows], out_ref.at[rows], left.at[index]).start()

    for index in range(every_row // block):
        rows = pl.ds(index * block, block)
        pltpu.make_async_copy(held_out.at[rows], out_ref.at[rows], left.at[index]).wait()


def project(inputs, gain, w_query, w_key, w_value, adapter_in, tasks, moves, homes, own_rows):
    steps, all_rows, width = inputs.shape
    columns = w_query.shape[1] + w_key.shape[1] + w_value.shape[1] + PADDED_WIDTH
    large = (inputs, jnp.swapaxes(adapter_in, 1, 2), w_query, w_key, w_value)
    return pl.pallas_call(
        functools.partial(project_kernel, own_rows),
        out_shape=jax.ShapeDtypeStruct((steps * all_rows, columns), jnp.bfloat16),
        in_specs=[pl.BlockSpec(memory_space=pltpu.VMEM)] * 4
        + [pl.BlockSpec(memory_space=pl.ANY)] * len(large),
        out_specs=pl.BlockSpec(memory_space=pl.ANY),
        scratch_shapes=[pltpu.VMEM(array.shape, jnp.bfloat16) for array in large]
        + [
            pltpu.VMEM((steps * all_rows, width), jnp.bfloat16),
            pltpu.VMEM((steps * all_rows, columns), jnp.bfloat16),
            pltpu.SemaphoreType.DMA((len(large),)),
            pltpu.SemaphoreType.DMA((steps * all_rows // 128,)),
        ],
        cost_estimate=pl.CostEstimate(
            flops=2 * steps * all_rows * width * 3328, bytes_accessed=3_000_000, transcendentals=0
        ),
    )(gain[None, :], tasks[None, :], moves.T, homes[None, :], *large)


def low_kernel(low, parts_ref, low_ref):
    sources, rows, columns = parts_ref.shape
    targets, _, width = low_ref.shape
    total = parts_ref[0, :, columns - width :].astype(jnp.float32)
    for source in range(1, sources):
        total = total + parts_ref[source, :, columns - width :].astype(jnp.float32)
    lane = lax.broadcasted_iota(jnp.int32, total.shape, 1)
    terms = jnp.logical_or(lane == low, lane == low + 1)
    squares = jnp.sum(jnp.where(terms, total, 0.0), axis=1, keepdims=True)
    squares_high = squares.astype(jnp.bfloat16).astype(jnp.float32)
    total = jnp.where(
        lane == low,
        squares_high,
        jnp.where(lane == low + 1, squares - squares_high, total),
    ).astype(jnp.bfloat16)
    for target in range(targets):
        low_ref[target] = total


def sum_low(parts, base_end, low, depth):
    _, rows, columns = parts.shape
    return pl.pallas_call(
        functools.partial(low_kernel, low),
        out_shape=jax.ShapeDtypeStruct((depth, rows, columns - base_end), jnp.bfloat16),
        in_specs=[pl.BlockSpec(memory_space=pltpu.VMEM)],
        out_specs=pl.BlockSpec(memory_space=pltpu.VMEM),
        compiler_params=pltpu.CompilerParams(vmem_limit_bytes=16 * 1024 * 1024),
        cost_estimate=pl.CostEstimate(
            flops=parts.size // 6, bytes_accessed=parts.size // 3, transcendentals=0
        ),
    )(parts)


def lift_kernel(
    rank,
    head_dim,
    model_width,
    groups,
    low_ref,
    line_ref,
    other_ref,
    base_ref,
    out_ref,
):
    rows, columns = out_ref.shape
    line = line_ref.shape[0]
    low = 3 * rank
    total = low_ref[0].astype(jnp.float32)
    for source in range(1, low_ref.shape[0]):
        total = total + low_ref[source].astype(jnp.float32)
    lane = lax.broadcasted_iota(jnp.int32, total.shape, 1)
    terms = jnp.logical_or(lane == low, lane == low + 1)
    squares = jnp.sum(jnp.where(terms, total, 0.0), axis=1, keepdims=True)
    inverse = lax.rsqrt(squares / model_width + epsilon)
    lowrank = (inverse * total).astype(jnp.bfloat16)
    from_lane = lax.broadcasted_iota(jnp.int32, (PADDED_WIDTH, line * rank), 0)
    to_lane = lax.broadcasted_iota(jnp.int32, (PADDED_WIDTH, line * rank), 1)
    slot_lane = lax.broadcasted_iota(jnp.int32, (rows, line * rank), 1) // rank
    home = jnp.sum(jnp.where(lane == low + 2, total, 0.0), axis=1, keepdims=True) / groups
    home = home.astype(jnp.int32)
    depth = low_ref.shape[0]
    same_half = home // depth % 2 == lax.axis_index("y_lo")
    slot = home // (2 * depth) + jnp.where(same_half, 0, line)
    slot = jnp.where(home % depth == lax.axis_index("z"), slot, -1)
    spreads = []
    for number in range(3):
        pick = jnp.where(from_lane == number * rank + to_lane % rank, 1.0, 0.0)
        tiled = dot(lowrank, pick.astype(jnp.bfloat16))
        spreads.append(
            [
                jnp.where(slot == slot_lane + half * line, tiled, 0.0).astype(jnp.bfloat16)
                for half in range(2)
            ]
        )
    key_first, value_first = columns - 2 * head_dim, columns - head_dim
    bounds = ((0, key_first), (key_first, value_first), (value_first, columns))
    for (first, last), (near, far) in zip(bounds, spreads, strict=True):
        lifted = dot(near, line_ref[:, :, first:last].reshape(line * rank, last - first))
        lifted = lifted + dot(
            far, other_ref[:, :, first:last].reshape(line * rank, last - first)
        )
        out_ref[:, first:last] = (inverse * base_ref[:, first:last] + lifted).astype(jnp.bfloat16)


def lift(low_parts, base, up_line, up_other, rank, head_dim, model_width, groups):
    return pl.pallas_call(
        functools.partial(lift_kernel, rank, head_dim, model_width, groups),
        out_shape=jax.ShapeDtypeStruct(base.shape, jnp.bfloat16),
        in_specs=[pl.BlockSpec(memory_space=pltpu.VMEM)] * 4,
        out_specs=pl.BlockSpec(memory_space=pltpu.VMEM),
        compiler_params=pltpu.CompilerParams(vmem_limit_bytes=16 * 1024 * 1024),
        cost_estimate=pl.CostEstimate(
            flops=2 * base.size * up_line.shape[0] * 2 * rank,
            bytes_accessed=2_000_000,
            transcendentals=0,
        ),
    )(low_parts, up_line, up_other, base)


def output_kernel(
    own_rows,
    steps,
    tasks_ref,
    moves_ref,
    rows_ref,
    down_ref,
    weight_ref,
    up_ref,
    out_ref,
    held_weight,
    held_up,
    held_out,
    arrived,
):
    copies = start_copies(((weight_ref, held_weight), (up_ref, held_up)), arrived)
    every_row, _ = rows_ref.shape
    adapters, rank, width = down_ref.shape
    per_group = steps * own_rows
    all_rows = every_row // steps
    block = 256
    down = down_ref[...].reshape(adapters * rank, width)
    for first in range(0, every_row, block):
        row = first + lax.broadcasted_iota(jnp.int32, (block, 1), 0)
        task = row_tasks(row, own_rows, per_group, tasks_ref, moves_ref)
        rows = rows_ref[first : first + block, :]
        reduced = lax.dot_general(
            rows, down, (((1,), (1,)), ((), ())), preferred_element_type=jnp.float32
        )
        owner = lax.broadcasted_iota(jnp.int32, reduced.shape, 1) // rank
        reduced = jnp.where(owner == task, reduced, 0.0).astype(jnp.bfloat16)
        if first == 0:
            for copy in copies:
                copy.wait()
        total = dot(rows, held_weight[...]) + dot(
            reduced, held_up[...].reshape(adapters * rank, out_ref.shape[1])
        )
        held_out[first : first + block, :] = total.astype(jnp.bfloat16)
    for first in range(0, every_row, block):
        row = first + lax.broadcasted_iota(jnp.int32, (block, 1), 0)
        place = row % all_rows // own_rows * per_group + row // all_rows * own_rows + row % own_rows
        lane = lax.broadcasted_iota(jnp.int32, (block, every_row), 1)
        order = jnp.where(lane == place, 1.0, 0.0).astype(jnp.bfloat16)
        out_ref[first : first + block, :] = dot(order, held_out[...]).astype(jnp.bfloat16)


def output(rows, w_output, adapter_attn, adapter_out, tasks, moves, own_rows, steps):
    every_row, width = rows.shape
    columns = w_output.shape[1]
    return pl.pallas_call(
        functools.partial(output_kernel, own_rows, steps),
        out_shape=jax.ShapeDtypeStruct((every_row, columns), jnp.bfloat16),
        in_specs=[pl.BlockSpec(memory_space=pltpu.VMEM)] * 4
        + [pl.BlockSpec(memory_space=pl.ANY)] * 2,
        out_specs=pl.BlockSpec(memory_space=pltpu.VMEM),
        scratch_shapes=[
            pltpu.VMEM(w_output.shape, jnp.bfloat16),
            pltpu.VMEM(adapter_out.shape, jnp.bfloat16),
            pltpu.VMEM((every_row, columns), jnp.bfloat16),
            pltpu.SemaphoreType.DMA((2,)),
        ],
        compiler_params=pltpu.CompilerParams(vmem_limit_bytes=16 * 1024 * 1024),
        cost_estimate=pl.CostEstimate(
            flops=2 * every_row * width * 640, bytes_accessed=3_000_000, transcendentals=0
        ),
    )(
        tasks[None, :],
        moves.T,
        rows,
        jnp.swapaxes(adapter_attn, 1, 2),
        w_output,
        adapter_out,
    )


def attend(queries, cache_keys, value_cache, fresh_keys, fresh_values, lengths, query_steps):
    scaling = 1.0 / math.sqrt(queries.shape[-1])
    old_scores = (
        jnp.einsum("rnd,rjd->rnj", queries, cache_keys, preferred_element_type=jnp.float32)
        * scaling
    )
    new_scores = (
        jnp.einsum("rnd,rjd->rnj", queries, fresh_keys, preferred_element_type=jnp.float32)
        * scaling
    )
    visible = jnp.arange(cache_keys.shape[1])[None, None, :] < lengths[:, None, None]
    old_scores = jnp.where(visible, old_scores, -1e30)
    fresh = np.arange(fresh_keys.shape[1])[None, None, :] <= query_steps[None, :, None]
    new_scores = jnp.where(fresh, new_scores, -1e30)
    highest = jnp.maximum(jnp.max(old_scores, axis=-1), jnp.max(new_scores, axis=-1))[..., None]
    old_exp = jnp.exp(old_scores - highest)
    new_exp = jnp.exp(new_scores - highest)
    denominator = jnp.sum(old_exp, axis=-1, keepdims=True) + jnp.sum(
        new_exp, axis=-1, keepdims=True
    )
    old_weights = (old_exp / denominator).astype(jnp.bfloat16)
    new_weights = (new_exp / denominator).astype(jnp.bfloat16)
    mixed = jnp.einsum(
        "rnj,rjd->rnd", old_weights, value_cache, preferred_element_type=jnp.float32
    )
    mixed = mixed + jnp.einsum(
        "rnj,rjd->rnd", new_weights, fresh_values, preferred_element_type=jnp.float32
    )
    return mixed.astype(jnp.bfloat16)


def on_device(
    inputs,
    gain,
    w_query,
    key_projection_weight,
    value_projection_weight,
    w_output,
    adapter_in,
    adapter_attn,
    adapter_out,
    pool_query,
    slot_keyvalue_matrices,
    cache_keys,
    value_cache,
    tasks,
    homes,
    moves,
    lengths,
):
    steps, all_rows, width_part = inputs.shape
    own_rows = lengths.shape[0]
    groups = all_rows // own_rows
    planes = lax.axis_size(PLANE)
    line = lax.axis_size("x")
    depth = lax.axis_size("z")
    task_count = homes.shape[0]
    rank = adapter_out.shape[1]
    head_dim = cache_keys.shape[3]
    query_width = w_query.shape[1]
    heads = query_width // head_dim
    key_end = query_width + head_dim
    base_end = key_end + head_dim
    per_group = steps * own_rows
    every_row = groups * per_group
    model_width = width_part * groups
    column_rows = depth * per_group

    partial = project(
        inputs,
        gain,
        w_query,
        key_projection_weight,
        value_projection_weight,
        adapter_in,
        tasks,
        moves,
        homes,
        own_rows,
    )
    partial, pool_query, slot_keyvalue_matrices = lax.optimization_barrier(
        (partial, pool_query, slot_keyvalue_matrices)
    )
    with jax.named_scope("sum_plane"):
        by_plane = exchange(partial.reshape(planes, column_rows, -1), PLANE)

    up = jnp.concatenate(
        [
            pool_query.reshape(rank, query_width),
            slot_keyvalue_matrices.reshape(rank, 2 * head_dim),
        ],
        axis=1,
    )
    with jax.named_scope("up_x"):
        up_line = lax.all_gather(up, "x", axis=0)
    with jax.named_scope("up_y_lo"):
        up_other = lax.ppermute(up_line, "y_lo", [(0, 1), (1, 0)])
    low_part = sum_low(by_plane, base_end, 3 * rank, depth)
    plane_sum = jnp.sum(by_plane[:, :, :base_end].astype(jnp.float32), axis=0)
    with jax.named_scope("sum_low"):
        low_parts = exchange(low_part, "z")

    raw_part = lift(
        low_parts, plane_sum, up_line, up_other, rank, head_dim, model_width, groups
    )
    raw_part, first_core = lax.optimization_barrier((raw_part, lax.axis_index("core") == 0))
    with jax.named_scope("sum_z"):
        by_depth = exchange(raw_part.reshape(depth, per_group, base_end), "z")
    raw = jnp.sum(by_depth.astype(jnp.float32), axis=0)

    row_step = jnp.arange(per_group) // own_rows
    positions = jnp.tile(lengths, steps) + row_step
    queries = apply_rotary(raw[:, :query_width].reshape(per_group, heads, head_dim), positions)
    new_keys = apply_rotary(
        raw[:, query_width:key_end].reshape(per_group, 1, head_dim), positions
    )
    raw_value = raw[:, key_end:]

    def by_row(array):
        return (
            array.astype(jnp.bfloat16)
            .reshape(steps, own_rows, -1, head_dim)
            .transpose(1, 0, 2, 3)
            .reshape(own_rows, -1, head_dim)
        )

    attended = attend(
        by_row(queries),
        cache_keys.reshape(own_rows, -1, head_dim),
        value_cache.reshape(own_rows, -1, head_dim),
        by_row(new_keys),
        by_row(raw_value),
        lengths,
        np.arange(steps * heads) // heads,
    )
    attended = (
        attended.reshape(own_rows, steps, query_width)
        .transpose(1, 0, 2)
        .reshape(per_group, query_width)
    )

    with jax.named_scope("gather_z"):
        column = exchange(
            jnp.broadcast_to(attended[None], (depth, per_group, query_width)), "z"
        ).reshape(depth * per_group, query_width)
    with jax.named_scope("gather_plane"):
        piece_rows = exchange(
            jnp.broadcast_to(column[None], (planes, depth * per_group, query_width)), PLANE
        ).reshape(every_row, query_width)

    mixed = output(
        piece_rows, w_output, adapter_attn, adapter_out, tasks, moves, own_rows, steps
    )
    with jax.named_scope("sum_core"):
        both = lax.all_gather(mixed, "core", axis=0)
    half = every_row // 2
    both = jnp.where(first_core, both[:, :half], both[:, half:])
    total = both[0].astype(jnp.float32) + both[1].astype(jnp.float32)
    for pairs in ([[0, 1], [2, 3]], [[1, 2], [3, 0]]):
        with jax.named_scope("sum_y_hi"):
            both = lax.all_gather(
                total.astype(jnp.bfloat16), "y_hi", axis=0, axis_index_groups=pairs
            )
        total = both[0].astype(jnp.float32) + both[1].astype(jnp.float32)
    total, residual = lax.optimization_barrier((total, inputs.reshape(every_row, width_part)))
    residual = jnp.where(first_core, residual[:half], residual[half:])
    finished = (residual.astype(jnp.float32) + total).astype(jnp.bfloat16)
    with jax.named_scope("gather_core"):
        finished = lax.all_gather(finished, "core", axis=0, tiled=True)
    return finished.reshape(inputs.shape)


def solution(mesh):
    parts = Mesh(mesh.devices.reshape(4, 2, 8, 4, 2), GROUP + TENSOR)
    return jax.shard_map(
        on_device,
        mesh=parts,
        in_specs=(
            P(None, None, GROUP),
            P(GROUP),
            P(GROUP, TENSOR),
            P(GROUP, TENSOR),
            P(GROUP, TENSOR),
            P(TENSOR, GROUP),
            P(None, GROUP, None),
            P(None, TENSOR, None),
            P(None, None, GROUP),
            P(GROUP, None, TENSOR),
            P(GROUP, None, None, TENSOR),
            P(GROUP, TENSOR, None, None),
            P(GROUP, TENSOR, None, None),
            P(),
            P(),
            P(),
            P(GROUP),
        ),
        out_specs=P(None, None, GROUP),
        check_vma=False,
    )
```

```python
import functools
import math

import jax
import jax.numpy as jnp
import numpy as np
from jax import lax
from jax.experimental import pallas as pl
from jax.experimental.pallas import tpu as pltpu
from jax.sharding import Mesh
from jax.sharding import PartitionSpec as P

epsilon = 1e-05
GROUP = ("x", "y_lo", "z")
PLANE = ("x", "y_lo")
TENSOR = ("y_hi", "core")
PADDED_WIDTH = 256


def exchange(blocks, axes):
    return lax.all_to_all(blocks, axes, 0, 0, tiled=True)


def apply_rotary(vectors, token_positions):
    half_width = vectors.shape[-1] // 2
    frequency = jnp.exp(
        -jnp.log(500000.0) * jnp.arange(half_width, dtype=jnp.float32) * (2.0 / vectors.shape[-1])
    )
    angles = token_positions.astype(jnp.float32)[:, None] * frequency[None, :]
    cosine = jnp.cos(angles)[:, None, :]
    sine_part = jnp.sin(angles)[:, None, :]
    leading = vectors[..., :half_width]
    trailing = vectors[..., half_width:]
    return jnp.concatenate(
        [leading * cosine - trailing * sine_part, leading * sine_part + trailing * cosine], axis=-1
    )


def dot(left, right):
    return jnp.dot(left, right, preferred_element_type=jnp.float32)


def start_copies(pairs, arrived):
    copies = [
        pltpu.make_async_copy(source, held, arrived.at[number])
        for number, (source, held) in enumerate(pairs)
    ]
    for copy in copies:
        copy.start()
    return copies


def row_tasks(row, own_rows, per_group, tasks_ref, moves_ref):
    group = row // per_group
    tasks, moves = tasks_ref.shape[1], moves_ref.shape[1]
    lane = lax.broadcasted_iota(jnp.int32, (row.shape[0], tasks), 1)
    own = lane == group * own_rows + row % own_rows
    task = jnp.sum(jnp.where(own, tasks_ref[...], 0), axis=1, keepdims=True)
    here = moves_ref[1:2, :] == jnp.broadcast_to(group, (row.shape[0], moves))
    moved = jnp.sum(jnp.where(here, 1, 0), axis=1, keepdims=True) > 0
    chosen = jnp.sum(jnp.where(here, moves_ref[0:1, :], 0), axis=1, keepdims=True)
    late = row % per_group >= per_group // 2
    return jnp.where(jnp.logical_and(late, moved), chosen, task)


def project_kernel(
    own_rows,
    gain_ref,
    tasks_ref,
    moves_ref,
    homes_ref,
    inputs_ref,
    adapter_ref,
    query_ref,
    key_ref,
    value_ref,
    out_ref,
    held_inputs,
    held_adapter,
    held_query,
    held_key,
    held_value,
    gained_ref,
    held_out,
    arrived,
    left,
):
    steps, all_rows, width = inputs_ref.shape
    every_row = steps * all_rows
    per_group = steps * own_rows
    query_width = query_ref.shape[1]
    head_dim = key_ref.shape[1]
    adapters, low, _ = adapter_ref.shape
    key_end = query_width + head_dim
    base_end = key_end + head_dim
    block = 256
    copies = start_copies(
        (
            (inputs_ref, held_inputs),
            (adapter_ref, held_adapter),
            (query_ref, held_query),
            (key_ref, held_key),
            (value_ref, held_value),
        ),
        arrived,
    )

    def lane(width):
        return lax.broadcasted_iota(jnp.int32, (block, width), 1)

    copies[0].wait()
    gathered = held_inputs[...].reshape(every_row, width)
    squares_of = []
    for first in range(0, every_row, block):
        row = first + lax.broadcasted_iota(jnp.int32, (block, 1), 0)
        place = row % per_group // own_rows * all_rows + row // per_group * own_rows + row % own_rows
        order = jnp.where(lane(every_row) == place, 1.0, 0.0).astype(jnp.bfloat16)
        states = dot(order, gathered)
        gained_ref[first : first + block, :] = (states * gain_ref[...]).astype(jnp.bfloat16)
        squares_of.append(jnp.sum(states * states, axis=1, keepdims=True))

    copies[1].wait()
    for index, squares in enumerate(squares_of):
        first = index * block

        row = first + lax.broadcasted_iota(jnp.int32, (block, 1), 0)
        task = row_tasks(row, own_rows, per_group, tasks_ref, moves_ref)
        home = jnp.sum(
            jnp.where(lane(adapters) == task, homes_ref[...], 0), axis=1, keepdims=True
        ).astype(jnp.float32)
        gained = gained_ref[first : first + block, :]
        total = jnp.zeros((block, low), jnp.float32)
        for adapter in range(0, adapters, 2):
            both = [
                jnp.where(task == number, gained, jnp.zeros_like(gained))
                for number in (adapter, adapter + 1)
            ]
            total = total + lax.dot_general(
                jnp.concatenate(both, axis=1),
                jnp.concatenate([held_adapter[adapter], held_adapter[adapter + 1]], axis=1),
                (((1,), (1,)), ((), ())),
                preferred_element_type=jnp.float32,
            )
        rest = PADDED_WIDTH - low
        squares_high = squares.astype(jnp.bfloat16).astype(jnp.float32)
        extra = jnp.where(
            lane(rest) == 0,
            squares_high,
            jnp.where(
                lane(rest) == 1, squares - squares_high, jnp.where(lane(rest) == 2, home, 0.0)
            ),
        )
        held_out[first : first + block, base_end : base_end + PADDED_WIDTH] = jnp.concatenate(
            [total, extra], axis=1
        ).astype(jnp.bfloat16)

    for copy in copies[2:]:
        copy.wait()

    @pl.loop(0, every_row // block)
    def _(index):
        rows = pl.ds(pl.multiple_of(index * block, block), block)
        gained = gained_ref[rows, :]
        held_out[rows, 0:query_width] = dot(gained, held_query[...]).astype(jnp.bfloat16)
        held_out[rows, query_width:key_end] = dot(gained, held_key[...]).astype(jnp.bfloat16)
        held_out[rows, key_end:base_end] = dot(gained, held_value[...]).astype(jnp.bfloat16)
        pltpu.make_async_copy(held_out.at[rows], out_ref.at[rows], left.at[index]).start()

    for index in range(every_row // block):
        rows = pl.ds(index * block, block)
        pltpu.make_async_copy(held_out.at[rows], out_ref.at[rows], left.at[index]).wait()


def project(inputs, gain, w_query, w_key, w_value, adapter_in, tasks, moves, homes, own_rows):
    steps, all_rows, width = inputs.shape
    columns = w_query.shape[1] + w_key.shape[1] + w_value.shape[1] + PADDED_WIDTH
    large = (inputs, jnp.swapaxes(adapter_in, 1, 2), w_query, w_key, w_value)
    return pl.pallas_call(
        functools.partial(project_kernel, own_rows),
        out_shape=jax.ShapeDtypeStruct((steps * all_rows, columns), jnp.bfloat16),
        in_specs=[pl.BlockSpec(memory_space=pltpu.VMEM)] * 4
        + [pl.BlockSpec(memory_space=pl.ANY)] * len(large),
        out_specs=pl.BlockSpec(memory_space=pl.ANY),
        scratch_shapes=[pltpu.VMEM(array.shape, jnp.bfloat16) for array in large]
        + [
            pltpu.VMEM((steps * all_rows, width), jnp.bfloat16),
            pltpu.VMEM((steps * all_rows, columns), jnp.bfloat16),
            pltpu.SemaphoreType.DMA((len(large),)),
            pltpu.SemaphoreType.DMA((steps * all_rows // 256,)),
        ],
        cost_estimate=pl.CostEstimate(
            flops=2 * steps * all_rows * width * 3328, bytes_accessed=3_000_000, transcendentals=0
        ),
    )(gain[None, :], tasks[None, :], moves.T, homes[None, :], *large)


def low_kernel(low, parts_ref, low_ref):
    sources, rows, columns = parts_ref.shape
    targets, _, width = low_ref.shape
    total = parts_ref[0, :, columns - width :].astype(jnp.float32)
    for source in range(1, sources):
        total = total + parts_ref[source, :, columns - width :].astype(jnp.float32)
    lane = lax.broadcasted_iota(jnp.int32, total.shape, 1)
    terms = jnp.logical_or(lane == low, lane == low + 1)
    squares = jnp.sum(jnp.where(terms, total, 0.0), axis=1, keepdims=True)
    squares_high = squares.astype(jnp.bfloat16).astype(jnp.float32)
    total = jnp.where(
        lane == low,
        squares_high,
        jnp.where(lane == low + 1, squares - squares_high, total),
    ).astype(jnp.bfloat16)
    for target in range(targets):
        low_ref[target] = total


def sum_low(parts, base_end, low, depth):
    _, rows, columns = parts.shape
    return pl.pallas_call(
        functools.partial(low_kernel, low),
        out_shape=jax.ShapeDtypeStruct((depth, rows, columns - base_end), jnp.bfloat16),
        in_specs=[pl.BlockSpec(memory_space=pltpu.VMEM)],
        out_specs=pl.BlockSpec(memory_space=pltpu.VMEM),
        compiler_params=pltpu.CompilerParams(vmem_limit_bytes=16 * 1024 * 1024),
        cost_estimate=pl.CostEstimate(
            flops=parts.size // 6, bytes_accessed=parts.size // 3, transcendentals=0
        ),
    )(parts)


def lift_kernel(
    rank,
    head_dim,
    model_width,
    groups,
    low_ref,
    line_ref,
    other_ref,
    base_ref,
    out_ref,
):
    rows, columns = out_ref.shape
    line = line_ref.shape[0]
    low = 3 * rank
    total = low_ref[0].astype(jnp.float32)
    for source in range(1, low_ref.shape[0]):
        total = total + low_ref[source].astype(jnp.float32)
    lane = lax.broadcasted_iota(jnp.int32, total.shape, 1)
    terms = jnp.logical_or(lane == low, lane == low + 1)
    squares = jnp.sum(jnp.where(terms, total, 0.0), axis=1, keepdims=True)
    inverse = lax.rsqrt(squares / model_width + epsilon)
    lowrank = (inverse * total).astype(jnp.bfloat16)
    from_lane = lax.broadcasted_iota(jnp.int32, (PADDED_WIDTH, line * rank), 0)
    to_lane = lax.broadcasted_iota(jnp.int32, (PADDED_WIDTH, line * rank), 1)
    slot_lane = lax.broadcasted_iota(jnp.int32, (rows, line * rank), 1) // rank
    home = jnp.sum(jnp.where(lane == low + 2, total, 0.0), axis=1, keepdims=True) / groups
    home = home.astype(jnp.int32)
    depth = low_ref.shape[0]
    same_half = home // depth % 2 == lax.axis_index("y_lo")
    slot = home // (2 * depth) + jnp.where(same_half, 0, line)
    slot = jnp.where(home % depth == lax.axis_index("z"), slot, -1)
    spreads = []
    for number in range(3):
        pick = jnp.where(from_lane == number * rank + to_lane % rank, 1.0, 0.0)
        tiled = dot(lowrank, pick.astype(jnp.bfloat16))
        spreads.append(
            [
                jnp.where(slot == slot_lane + half * line, tiled, 0.0).astype(jnp.bfloat16)
                for half in range(2)
            ]
        )
    key_first, value_first = columns - 2 * head_dim, columns - head_dim
    bounds = ((0, key_first), (key_first, value_first), (value_first, columns))
    for (first, last), (near, far) in zip(bounds, spreads, strict=True):
        lifted = dot(near, line_ref[:, :, first:last].reshape(line * rank, last - first))
        lifted = lifted + dot(
            far, other_ref[:, :, first:last].reshape(line * rank, last - first)
        )
        out_ref[:, first:last] = (inverse * base_ref[:, first:last] + lifted).astype(jnp.bfloat16)


def lift(low_parts, base, up_line, up_other, rank, head_dim, model_width, groups):
    return pl.pallas_call(
        functools.partial(lift_kernel, rank, head_dim, model_width, groups),
        out_shape=jax.ShapeDtypeStruct(base.shape, jnp.bfloat16),
        in_specs=[pl.BlockSpec(memory_space=pltpu.VMEM)] * 4,
        out_specs=pl.BlockSpec(memory_space=pltpu.VMEM),
        compiler_params=pltpu.CompilerParams(vmem_limit_bytes=16 * 1024 * 1024),
        cost_estimate=pl.CostEstimate(
            flops=2 * base.size * up_line.shape[0] * 2 * rank,
            bytes_accessed=2_000_000,
            transcendentals=0,
        ),
    )(low_parts, up_line, up_other, base)


def output_kernel(
    own_rows,
    steps,
    tasks_ref,
    moves_ref,
    rows_ref,
    down_ref,
    weight_ref,
    up_ref,
    out_ref,
    held_weight,
    held_up,
    held_out,
    arrived,
):
    copies = start_copies(((weight_ref, held_weight), (up_ref, held_up)), arrived)
    every_row, _ = rows_ref.shape
    adapters, rank, width = down_ref.shape
    per_group = steps * own_rows
    all_rows = every_row // steps
    block = 256
    down = down_ref[...].reshape(adapters * rank, width)
    for first in range(0, every_row, block):
        row = first + lax.broadcasted_iota(jnp.int32, (block, 1), 0)
        task = row_tasks(row, own_rows, per_group, tasks_ref, moves_ref)
        rows = rows_ref[first : first + block, :]
        reduced = lax.dot_general(
            rows, down, (((1,), (1,)), ((), ())), preferred_element_type=jnp.float32
        )
        owner = lax.broadcasted_iota(jnp.int32, reduced.shape, 1) // rank
        reduced = jnp.where(owner == task, reduced, 0.0).astype(jnp.bfloat16)
        if first == 0:
            for copy in copies:
                copy.wait()
        total = dot(rows, held_weight[...]) + dot(
            reduced, held_up[...].reshape(adapters * rank, out_ref.shape[1])
        )
        held_out[first : first + block, :] = total.astype(jnp.bfloat16)
    for first in range(0, every_row, block):
        row = first + lax.broadcasted_iota(jnp.int32, (block, 1), 0)
        place = row % all_rows // own_rows * per_group + row // all_rows * own_rows + row % own_rows
        lane = lax.broadcasted_iota(jnp.int32, (block, every_row), 1)
        order = jnp.where(lane == place, 1.0, 0.0).astype(jnp.bfloat16)
        out_ref[first : first + block, :] = dot(order, held_out[...]).astype(jnp.bfloat16)


def output(rows, w_output, adapter_attn, adapter_out, tasks, moves, own_rows, steps):
    every_row, width = rows.shape
    columns = w_output.shape[1]
    return pl.pallas_call(
        functools.partial(output_kernel, own_rows, steps),
        out_shape=jax.ShapeDtypeStruct((every_row, columns), jnp.bfloat16),
        in_specs=[pl.BlockSpec(memory_space=pltpu.VMEM)] * 4
        + [pl.BlockSpec(memory_space=pl.ANY)] * 2,
        out_specs=pl.BlockSpec(memory_space=pltpu.VMEM),
        scratch_shapes=[
            pltpu.VMEM(w_output.shape, jnp.bfloat16),
            pltpu.VMEM(adapter_out.shape, jnp.bfloat16),
            pltpu.VMEM((every_row, columns), jnp.bfloat16),
            pltpu.SemaphoreType.DMA((2,)),
        ],
        compiler_params=pltpu.CompilerParams(vmem_limit_bytes=16 * 1024 * 1024),
        cost_estimate=pl.CostEstimate(
            flops=2 * every_row * width * 640, bytes_accessed=3_000_000, transcendentals=0
        ),
    )(
        tasks[None, :],
        moves.T,
        rows,
        jnp.swapaxes(adapter_attn, 1, 2),
        w_output,
        adapter_out,
    )


def attend(queries, cache_keys, value_cache, fresh_keys, fresh_values, lengths, query_steps):
    scaling = 1.0 / math.sqrt(queries.shape[-1])
    old_scores = (
        jnp.einsum("rnd,rjd->rnj", queries, cache_keys, preferred_element_type=jnp.float32)
        * scaling
    )
    new_scores = (
        jnp.einsum("rnd,rjd->rnj", queries, fresh_keys, preferred_element_type=jnp.float32)
        * scaling
    )
    visible = jnp.arange(cache_keys.shape[1])[None, None, :] < lengths[:, None, None]
    old_scores = jnp.where(visible, old_scores, -1e30)
    fresh = np.arange(fresh_keys.shape[1])[None, None, :] <= query_steps[None, :, None]
    new_scores = jnp.where(fresh, new_scores, -1e30)
    highest = jnp.maximum(jnp.max(old_scores, axis=-1), jnp.max(new_scores, axis=-1))[..., None]
    old_exp = jnp.exp(old_scores - highest)
    new_exp = jnp.exp(new_scores - highest)
    denominator = jnp.sum(old_exp, axis=-1, keepdims=True) + jnp.sum(
        new_exp, axis=-1, keepdims=True
    )
    old_weights = (old_exp / denominator).astype(jnp.bfloat16)
    new_weights = (new_exp / denominator).astype(jnp.bfloat16)
    mixed = jnp.einsum(
        "rnj,rjd->rnd", old_weights, value_cache, preferred_element_type=jnp.float32
    )
    mixed = mixed + jnp.einsum(
        "rnj,rjd->rnd", new_weights, fresh_values, preferred_element_type=jnp.float32
    )
    return mixed.astype(jnp.bfloat16)


def on_device(
    inputs,
    gain,
    w_query,
    key_projection_weight,
    value_projection_weight,
    w_output,
    adapter_in,
    adapter_attn,
    adapter_out,
    pool_query,
    slot_keyvalue_matrices,
    cache_keys,
    value_cache,
    tasks,
    homes,
    moves,
    lengths,
):
    steps, all_rows, width_part = inputs.shape
    own_rows = lengths.shape[0]
    groups = all_rows // own_rows
    planes = lax.axis_size(PLANE)
    line = lax.axis_size("x")
    depth = lax.axis_size("z")
    task_count = homes.shape[0]
    rank = adapter_out.shape[1]
    head_dim = cache_keys.shape[3]
    query_width = w_query.shape[1]
    heads = query_width // head_dim
    key_end = query_width + head_dim
    base_end = key_end + head_dim
    per_group = steps * own_rows
    every_row = groups * per_group
    model_width = width_part * groups
    column_rows = depth * per_group

    partial = project(
        inputs,
        gain,
        w_query,
        key_projection_weight,
        value_projection_weight,
        adapter_in,
        tasks,
        moves,
        homes,
        own_rows,
    )
    partial, pool_query, slot_keyvalue_matrices = lax.optimization_barrier(
        (partial, pool_query, slot_keyvalue_matrices)
    )
    with jax.named_scope("sum_plane"):
        by_plane = exchange(partial.reshape(planes, column_rows, -1), PLANE)

    up = jnp.concatenate(
        [
            pool_query.reshape(rank, query_width),
            slot_keyvalue_matrices.reshape(rank, 2 * head_dim),
        ],
        axis=1,
    )
    with jax.named_scope("up_x"):
        up_line = lax.all_gather(up, "x", axis=0)
    with jax.named_scope("up_y_lo"):
        up_other = lax.ppermute(up_line, "y_lo", [(0, 1), (1, 0)])
    low_part = sum_low(by_plane, base_end, 3 * rank, depth)
    plane_sum = jnp.sum(by_plane[:, :, :base_end].astype(jnp.float32), axis=0)
    with jax.named_scope("sum_low"):
        low_parts = exchange(low_part, "z")

    raw_part = lift(
        low_parts, plane_sum, up_line, up_other, rank, head_dim, model_width, groups
    )
    raw_part, first_core = lax.optimization_barrier((raw_part, lax.axis_index("core") == 0))
    with jax.named_scope("sum_z"):
        by_depth = exchange(raw_part.reshape(depth, per_group, base_end), "z")
    raw = jnp.sum(by_depth.astype(jnp.float32), axis=0)

    row_step = jnp.arange(per_group) // own_rows
    positions = jnp.tile(lengths, steps) + row_step
    queries = apply_rotary(raw[:, :query_width].reshape(per_group, heads, head_dim), positions)
    new_keys = apply_rotary(
        raw[:, query_width:key_end].reshape(per_group, 1, head_dim), positions
    )
    raw_value = raw[:, key_end:]

    def by_row(array):
        return (
            array.astype(jnp.bfloat16)
            .reshape(steps, own_rows, -1, head_dim)
            .transpose(1, 0, 2, 3)
            .reshape(own_rows, -1, head_dim)
        )

    attended = attend(
        by_row(queries),
        cache_keys.reshape(own_rows, -1, head_dim),
        value_cache.reshape(own_rows, -1, head_dim),
        by_row(new_keys),
        by_row(raw_value),
        lengths,
        np.arange(steps * heads) // heads,
    )
    attended = (
        attended.reshape(own_rows, steps, query_width)
        .transpose(1, 0, 2)
        .reshape(per_group, query_width)
    )

    with jax.named_scope("gather_z"):
        column = exchange(
            jnp.broadcast_to(attended[None], (depth, per_group, query_width)), "z"
        ).reshape(depth * per_group, query_width)
    with jax.named_scope("gather_plane"):
        piece_rows = exchange(
            jnp.broadcast_to(column[None], (planes, depth * per_group, query_width)), PLANE
        ).reshape(every_row, query_width)

    mixed = output(
        piece_rows, w_output, adapter_attn, adapter_out, tasks, moves, own_rows, steps
    )
    with jax.named_scope("sum_core"):
        both = lax.all_gather(mixed, "core", axis=0)
    half = every_row // 2
    both = jnp.where(first_core, both[:, :half], both[:, half:])
    total = both[0].astype(jnp.float32) + both[1].astype(jnp.float32)
    for pairs in ([[0, 1], [2, 3]], [[1, 2], [3, 0]]):
        with jax.named_scope("sum_y_hi"):
            both = lax.all_gather(
                total.astype(jnp.bfloat16), "y_hi", axis=0, axis_index_groups=pairs
            )
        total = both[0].astype(jnp.float32) + both[1].astype(jnp.float32)
    total, residual = lax.optimization_barrier((total, inputs.reshape(every_row, width_part)))
    residual = jnp.where(first_core, residual[:half], residual[half:])
    finished = (residual.astype(jnp.float32) + total).astype(jnp.bfloat16)
    with jax.named_scope("gather_core"):
        finished = lax.all_gather(finished, "core", axis=0, tiled=True)
    return finished.reshape(inputs.shape)


def solution(mesh):
    parts = Mesh(mesh.devices.reshape(4, 2, 8, 4, 2), GROUP + TENSOR)
    return jax.shard_map(
        on_device,
        mesh=parts,
        in_specs=(
            P(None, None, GROUP),
            P(GROUP),
            P(GROUP, TENSOR),
            P(GROUP, TENSOR),
            P(GROUP, TENSOR),
            P(TENSOR, GROUP),
            P(None, GROUP, None),
            P(None, TENSOR, None),
            P(None, None, GROUP),
            P(GROUP, None, TENSOR),
            P(GROUP, None, None, TENSOR),
            P(GROUP, TENSOR, None, None),
            P(GROUP, TENSOR, None, None),
            P(),
            P(),
            P(),
            P(GROUP),
        ),
        out_specs=P(None, None, GROUP),
        check_vma=False,
    )
```

```python
import functools
import math

import jax
import jax.numpy as jnp
import numpy as np
from jax import lax
from jax.experimental import pallas as pl
from jax.experimental.pallas import tpu as pltpu
from jax.sharding import Mesh
from jax.sharding import PartitionSpec as P

epsilon = 1e-05
GROUP = ("x", "y_lo", "z")
PLANE = ("x", "y_lo")
TENSOR = ("y_hi", "core")
PADDED_WIDTH = 256


def exchange(blocks, axes):
    return lax.all_to_all(blocks, axes, 0, 0, tiled=True)


def rotary_tables(token_positions, width):
    half_width = width // 2
    frequency = jnp.exp(
        -jnp.log(500000.0) * jnp.arange(half_width, dtype=jnp.float32) * (2.0 / width)
    )
    angles = token_positions.astype(jnp.float32)[:, None] * frequency[None, :]
    return jnp.cos(angles), jnp.sin(angles)


def apply_rotary(vectors, cosine, sine_part):
    half_width = vectors.shape[-1] // 2
    cosine, sine_part = cosine[:, None, :], sine_part[:, None, :]
    leading = vectors[..., :half_width]
    trailing = vectors[..., half_width:]
    return jnp.concatenate(
        [leading * cosine - trailing * sine_part, leading * sine_part + trailing * cosine], axis=-1
    )


def dot(left, right):
    return jnp.dot(left, right, preferred_element_type=jnp.float32)


def start_copies(pairs, arrived):
    copies = [
        pltpu.make_async_copy(source, held, arrived.at[number])
        for number, (source, held) in enumerate(pairs)
    ]
    for copy in copies:
        copy.start()
    return copies


def row_tasks(row, own_rows, per_group, tasks_ref, moves_ref):
    group = row // per_group
    tasks, moves = tasks_ref.shape[1], moves_ref.shape[1]
    lane = lax.broadcasted_iota(jnp.int32, (row.shape[0], tasks), 1)
    own = lane == group * own_rows + row % own_rows
    task = jnp.sum(jnp.where(own, tasks_ref[...], 0), axis=1, keepdims=True)
    here = moves_ref[1:2, :] == jnp.broadcast_to(group, (row.shape[0], moves))
    moved = jnp.sum(jnp.where(here, 1, 0), axis=1, keepdims=True) > 0
    chosen = jnp.sum(jnp.where(here, moves_ref[0:1, :], 0), axis=1, keepdims=True)
    late = row % per_group >= per_group // 2
    return jnp.where(jnp.logical_and(late, moved), chosen, task)


def project_kernel(
    own_rows,
    gain_ref,
    tasks_ref,
    moves_ref,
    homes_ref,
    inputs_ref,
    adapter_ref,
    query_ref,
    key_ref,
    value_ref,
    out_ref,
    held_inputs,
    held_adapter,
    held_query,
    held_key,
    held_value,
    gained_ref,
    held_out,
    arrived,
    left,
):
    steps, all_rows, width = inputs_ref.shape
    every_row = steps * all_rows
    per_group = steps * own_rows
    query_width = query_ref.shape[1]
    head_dim = key_ref.shape[1]
    adapters, low, _ = adapter_ref.shape
    key_end = query_width + head_dim
    base_end = key_end + head_dim
    block = 256
    copies = start_copies(
        (
            (inputs_ref, held_inputs),
            (adapter_ref, held_adapter),
            (query_ref, held_query),
            (key_ref, held_key),
            (value_ref, held_value),
        ),
        arrived,
    )

    def lane(width):
        return lax.broadcasted_iota(jnp.int32, (block, width), 1)

    copies[0].wait()
    gathered = held_inputs[...].reshape(every_row, width)
    squares_of = []
    for first in range(0, every_row, block):
        row = first + lax.broadcasted_iota(jnp.int32, (block, 1), 0)
        place = row % per_group // own_rows * all_rows + row // per_group * own_rows + row % own_rows
        order = jnp.where(lane(every_row) == place, 1.0, 0.0).astype(jnp.bfloat16)
        states = dot(order, gathered)
        gained_ref[first : first + block, :] = (states * gain_ref[...]).astype(jnp.bfloat16)
        squares_of.append(jnp.sum(states * states, axis=1, keepdims=True))

    copies[1].wait()
    for index, squares in enumerate(squares_of):
        first = index * block

        row = first + lax.broadcasted_iota(jnp.int32, (block, 1), 0)
        task = row_tasks(row, own_rows, per_group, tasks_ref, moves_ref)
        home = jnp.sum(
            jnp.where(lane(adapters) == task, homes_ref[...], 0), axis=1, keepdims=True
        ).astype(jnp.float32)
        gained = gained_ref[first : first + block, :]
        total = jnp.zeros((block, low), jnp.float32)
        for adapter in range(0, adapters, 2):
            both = [
                jnp.where(task == number, gained, jnp.zeros_like(gained))
                for number in (adapter, adapter + 1)
            ]
            total = total + lax.dot_general(
                jnp.concatenate(both, axis=1),
                jnp.concatenate([held_adapter[adapter], held_adapter[adapter + 1]], axis=1),
                (((1,), (1,)), ((), ())),
                preferred_element_type=jnp.float32,
            )
        rest = PADDED_WIDTH - low
        squares_high = squares.astype(jnp.bfloat16).astype(jnp.float32)
        extra = jnp.where(
            lane(rest) == 0,
            squares_high,
            jnp.where(
                lane(rest) == 1, squares - squares_high, jnp.where(lane(rest) == 2, home, 0.0)
            ),
        )
        held_out[first : first + block, base_end : base_end + PADDED_WIDTH] = jnp.concatenate(
            [total, extra], axis=1
        ).astype(jnp.bfloat16)

    for copy in copies[2:]:
        copy.wait()

    @pl.loop(0, every_row // block)
    def _(index):
        rows = pl.ds(pl.multiple_of(index * block, block), block)
        gained = gained_ref[rows, :]
        held_out[rows, 0:query_width] = dot(gained, held_query[...]).astype(jnp.bfloat16)
        held_out[rows, query_width:key_end] = dot(gained, held_key[...]).astype(jnp.bfloat16)
        held_out[rows, key_end:base_end] = dot(gained, held_value[...]).astype(jnp.bfloat16)
        pltpu.make_async_copy(held_out.at[rows], out_ref.at[rows], left.at[index]).start()

    for index in range(every_row // block):
        rows = pl.ds(index * block, block)
        pltpu.make_async_copy(held_out.at[rows], out_ref.at[rows], left.at[index]).wait()


def project(inputs, gain, w_query, w_key, w_value, adapter_in, tasks, moves, homes, own_rows):
    steps, all_rows, width = inputs.shape
    columns = w_query.shape[1] + w_key.shape[1] + w_value.shape[1] + PADDED_WIDTH
    large = (inputs, jnp.swapaxes(adapter_in, 1, 2), w_query, w_key, w_value)
    return pl.pallas_call(
        functools.partial(project_kernel, own_rows),
        out_shape=jax.ShapeDtypeStruct((steps * all_rows, columns), jnp.bfloat16),
        in_specs=[pl.BlockSpec(memory_space=pltpu.VMEM)] * 4
        + [pl.BlockSpec(memory_space=pl.ANY)] * len(large),
        out_specs=pl.BlockSpec(memory_space=pl.ANY),
        scratch_shapes=[pltpu.VMEM(array.shape, jnp.bfloat16) for array in large]
        + [
            pltpu.VMEM((steps * all_rows, width), jnp.bfloat16),
            pltpu.VMEM((steps * all_rows, columns), jnp.bfloat16),
            pltpu.SemaphoreType.DMA((len(large),)),
            pltpu.SemaphoreType.DMA((steps * all_rows // 256,)),
        ],
        cost_estimate=pl.CostEstimate(
            flops=2 * steps * all_rows * width * 3328, bytes_accessed=3_000_000, transcendentals=0
        ),
    )(gain[None, :], tasks[None, :], moves.T, homes[None, :], *large)


def low_kernel(low, parts_ref, low_ref):
    sources, rows, columns = parts_ref.shape
    targets, _, width = low_ref.shape
    total = parts_ref[0, :, columns - width :].astype(jnp.float32)
    for source in range(1, sources):
        total = total + parts_ref[source, :, columns - width :].astype(jnp.float32)
    lane = lax.broadcasted_iota(jnp.int32, total.shape, 1)
    terms = jnp.logical_or(lane == low, lane == low + 1)
    squares = jnp.sum(jnp.where(terms, total, 0.0), axis=1, keepdims=True)
    squares_high = squares.astype(jnp.bfloat16).astype(jnp.float32)
    total = jnp.where(
        lane == low,
        squares_high,
        jnp.where(lane == low + 1, squares - squares_high, total),
    ).astype(jnp.bfloat16)
    for target in range(targets):
        low_ref[target] = total


def sum_low(parts, base_end, low, depth):
    _, rows, columns = parts.shape
    return pl.pallas_call(
        functools.partial(low_kernel, low),
        out_shape=jax.ShapeDtypeStruct((depth, rows, columns - base_end), jnp.bfloat16),
        in_specs=[pl.BlockSpec(memory_space=pltpu.VMEM)],
        out_specs=pl.BlockSpec(memory_space=pltpu.VMEM),
        compiler_params=pltpu.CompilerParams(vmem_limit_bytes=16 * 1024 * 1024),
        cost_estimate=pl.CostEstimate(
            flops=parts.size // 6, bytes_accessed=parts.size // 3, transcendentals=0
        ),
    )(parts)


def lift_kernel(
    rank,
    head_dim,
    model_width,
    groups,
    low_ref,
    line_ref,
    other_ref,
    base_ref,
    out_ref,
):
    rows, columns = out_ref.shape
    line = line_ref.shape[0]
    low = 3 * rank
    total = low_ref[0].astype(jnp.float32)
    for source in range(1, low_ref.shape[0]):
        total = total + low_ref[source].astype(jnp.float32)
    lane = lax.broadcasted_iota(jnp.int32, total.shape, 1)
    terms = jnp.logical_or(lane == low, lane == low + 1)
    squares = jnp.sum(jnp.where(terms, total, 0.0), axis=1, keepdims=True)
    inverse = lax.rsqrt(squares / model_width + epsilon)
    lowrank = (inverse * total).astype(jnp.bfloat16)
    from_lane = lax.broadcasted_iota(jnp.int32, (PADDED_WIDTH, line * rank), 0)
    to_lane = lax.broadcasted_iota(jnp.int32, (PADDED_WIDTH, line * rank), 1)
    slot_lane = lax.broadcasted_iota(jnp.int32, (rows, line * rank), 1) // rank
    home = jnp.sum(jnp.where(lane == low + 2, total, 0.0), axis=1, keepdims=True) / groups
    home = home.astype(jnp.int32)
    depth = low_ref.shape[0]
    same_half = home // depth % 2 == lax.axis_index("y_lo")
    slot = home // (2 * depth) + jnp.where(same_half, 0, line)
    slot = jnp.where(home % depth == lax.axis_index("z"), slot, -1)
    spreads = []
    for number in range(3):
        pick = jnp.where(from_lane == number * rank + to_lane % rank, 1.0, 0.0)
        tiled = dot(lowrank, pick.astype(jnp.bfloat16))
        spreads.append(
            [
                jnp.where(slot == slot_lane + half * line, tiled, 0.0).astype(jnp.bfloat16)
                for half in range(2)
            ]
        )
    key_first, value_first = columns - 2 * head_dim, columns - head_dim
    bounds = ((0, key_first), (key_first, value_first), (value_first, columns))
    for (first, last), (near, far) in zip(bounds, spreads, strict=True):
        lifted = dot(near, line_ref[:, :, first:last].reshape(line * rank, last - first))
        lifted = lifted + dot(
            far, other_ref[:, :, first:last].reshape(line * rank, last - first)
        )
        out_ref[:, first:last] = (inverse * base_ref[:, first:last] + lifted).astype(jnp.bfloat16)


def lift(low_parts, base, up_line, up_other, rank, head_dim, model_width, groups):
    return pl.pallas_call(
        functools.partial(lift_kernel, rank, head_dim, model_width, groups),
        out_shape=jax.ShapeDtypeStruct(base.shape, jnp.bfloat16),
        in_specs=[pl.BlockSpec(memory_space=pltpu.VMEM)] * 4,
        out_specs=pl.BlockSpec(memory_space=pltpu.VMEM),
        compiler_params=pltpu.CompilerParams(vmem_limit_bytes=16 * 1024 * 1024),
        cost_estimate=pl.CostEstimate(
            flops=2 * base.size * up_line.shape[0] * 2 * rank,
            bytes_accessed=2_000_000,
            transcendentals=0,
        ),
    )(low_parts, up_line, up_other, base)


def output_kernel(
    own_rows,
    steps,
    tasks_ref,
    moves_ref,
    rows_ref,
    down_ref,
    weight_ref,
    up_ref,
    out_ref,
    held_weight,
    held_up,
    held_out,
    arrived,
):
    copies = start_copies(((weight_ref, held_weight), (up_ref, held_up)), arrived)
    every_row, _ = rows_ref.shape
    adapters, rank, width = down_ref.shape
    per_group = steps * own_rows
    all_rows = every_row // steps
    block = 256
    down = down_ref[...].reshape(adapters * rank, width)
    for first in range(0, every_row, block):
        row = first + lax.broadcasted_iota(jnp.int32, (block, 1), 0)
        task = row_tasks(row, own_rows, per_group, tasks_ref, moves_ref)
        rows = rows_ref[first : first + block, :]
        reduced = lax.dot_general(
            rows, down, (((1,), (1,)), ((), ())), preferred_element_type=jnp.float32
        )
        owner = lax.broadcasted_iota(jnp.int32, reduced.shape, 1) // rank
        reduced = jnp.where(owner == task, reduced, 0.0).astype(jnp.bfloat16)
        if first == 0:
            for copy in copies:
                copy.wait()
        total = dot(rows, held_weight[...]) + dot(
            reduced, held_up[...].reshape(adapters * rank, out_ref.shape[1])
        )
        held_out[first : first + block, :] = total.astype(jnp.bfloat16)
    for first in range(0, every_row, block):
        row = first + lax.broadcasted_iota(jnp.int32, (block, 1), 0)
        place = row % all_rows // own_rows * per_group + row // all_rows * own_rows + row % own_rows
        lane = lax.broadcasted_iota(jnp.int32, (block, every_row), 1)
        order = jnp.where(lane == place, 1.0, 0.0).astype(jnp.bfloat16)
        out_ref[first : first + block, :] = dot(order, held_out[...]).astype(jnp.bfloat16)


def output(rows, w_output, adapter_attn, adapter_out, tasks, moves, own_rows, steps):
    every_row, width = rows.shape
    columns = w_output.shape[1]
    return pl.pallas_call(
        functools.partial(output_kernel, own_rows, steps),
        out_shape=jax.ShapeDtypeStruct((every_row, columns), jnp.bfloat16),
        in_specs=[pl.BlockSpec(memory_space=pltpu.VMEM)] * 4
        + [pl.BlockSpec(memory_space=pl.ANY)] * 2,
        out_specs=pl.BlockSpec(memory_space=pltpu.VMEM),
        scratch_shapes=[
            pltpu.VMEM(w_output.shape, jnp.bfloat16),
            pltpu.VMEM(adapter_out.shape, jnp.bfloat16),
            pltpu.VMEM((every_row, columns), jnp.bfloat16),
            pltpu.SemaphoreType.DMA((2,)),
        ],
        compiler_params=pltpu.CompilerParams(vmem_limit_bytes=16 * 1024 * 1024),
        cost_estimate=pl.CostEstimate(
            flops=2 * every_row * width * 640, bytes_accessed=3_000_000, transcendentals=0
        ),
    )(
        tasks[None, :],
        moves.T,
        rows,
        jnp.swapaxes(adapter_attn, 1, 2),
        w_output,
        adapter_out,
    )


def attend(queries, cache_keys, value_cache, fresh_keys, fresh_values, visible, query_steps):
    scaling = 1.0 / math.sqrt(queries.shape[-1])
    old_scores = (
        jnp.einsum("rnd,rjd->rnj", queries, cache_keys, preferred_element_type=jnp.float32)
        * scaling
    )
    new_scores = (
        jnp.einsum("rnd,rjd->rnj", queries, fresh_keys, preferred_element_type=jnp.float32)
        * scaling
    )
    old_scores = jnp.where(visible[:, None, :], old_scores, -1e30)
    fresh = np.arange(fresh_keys.shape[1])[None, None, :] <= query_steps[None, :, None]
    new_scores = jnp.where(fresh, new_scores, -1e30)
    highest = jnp.maximum(jnp.max(old_scores, axis=-1), jnp.max(new_scores, axis=-1))[..., None]
    old_exp = jnp.exp(old_scores - highest)
    new_exp = jnp.exp(new_scores - highest)
    denominator = jnp.sum(old_exp, axis=-1, keepdims=True) + jnp.sum(
        new_exp, axis=-1, keepdims=True
    )
    old_weights = (old_exp / denominator).astype(jnp.bfloat16)
    new_weights = (new_exp / denominator).astype(jnp.bfloat16)
    mixed = jnp.einsum(
        "rnj,rjd->rnd", old_weights, value_cache, preferred_element_type=jnp.float32
    )
    mixed = mixed + jnp.einsum(
        "rnj,rjd->rnd", new_weights, fresh_values, preferred_element_type=jnp.float32
    )
    return mixed.astype(jnp.bfloat16)


def on_device(
    inputs,
    gain,
    w_query,
    key_projection_weight,
    value_projection_weight,
    w_output,
    adapter_in,
    adapter_attn,
    adapter_out,
    pool_query,
    slot_keyvalue_matrices,
    cache_keys,
    value_cache,
    tasks,
    homes,
    moves,
    lengths,
):
    steps, all_rows, width_part = inputs.shape
    own_rows = lengths.shape[0]
    groups = all_rows // own_rows
    planes = lax.axis_size(PLANE)
    line = lax.axis_size("x")
    depth = lax.axis_size("z")
    task_count = homes.shape[0]
    rank = adapter_out.shape[1]
    head_dim = cache_keys.shape[3]
    query_width = w_query.shape[1]
    heads = query_width // head_dim
    key_end = query_width + head_dim
    base_end = key_end + head_dim
    per_group = steps * own_rows
    every_row = groups * per_group
    model_width = width_part * groups
    column_rows = depth * per_group

    partial = project(
        inputs,
        gain,
        w_query,
        key_projection_weight,
        value_projection_weight,
        adapter_in,
        tasks,
        moves,
        homes,
        own_rows,
    )
    partial, pool_query, slot_keyvalue_matrices = lax.optimization_barrier(
        (partial, pool_query, slot_keyvalue_matrices)
    )
    with jax.named_scope("sum_plane"):
        by_plane = exchange(partial.reshape(planes, column_rows, -1), PLANE)

    up = jnp.concatenate(
        [
            pool_query.reshape(rank, query_width),
            slot_keyvalue_matrices.reshape(rank, 2 * head_dim),
        ],
        axis=1,
    )
    with jax.named_scope("up_x"):
        up_line = lax.all_gather(up, "x", axis=0)
    with jax.named_scope("up_y_lo"):
        up_other = lax.ppermute(up_line, "y_lo", [(0, 1), (1, 0)])
    by_plane, lengths = lax.optimization_barrier((by_plane, lengths))
    low_part = sum_low(by_plane, base_end, 3 * rank, depth)
    plane_sum = jnp.sum(by_plane[:, :, :base_end].astype(jnp.float32), axis=0)
    with jax.named_scope("sum_low"):
        low_parts = exchange(low_part, "z")

    raw_part = lift(
        low_parts, plane_sum, up_line, up_other, rank, head_dim, model_width, groups
    )
    positions = jnp.tile(lengths, steps) + jnp.arange(per_group) // own_rows
    cosine, sine_part = rotary_tables(positions, head_dim)
    visible = jnp.arange(cache_keys.shape[2])[None, :] < lengths[:, None]
    raw_part, cosine, sine_part, visible, first_core = lax.optimization_barrier(
        (raw_part, cosine, sine_part, visible, lax.axis_index("core") == 0)
    )
    with jax.named_scope("sum_z"):
        by_depth = exchange(raw_part.reshape(depth, per_group, base_end), "z")
    raw = jnp.sum(by_depth.astype(jnp.float32), axis=0)

    queries = apply_rotary(
        raw[:, :query_width].reshape(per_group, heads, head_dim), cosine, sine_part
    )
    new_keys = apply_rotary(
        raw[:, query_width:key_end].reshape(per_group, 1, head_dim), cosine, sine_part
    )
    raw_value = raw[:, key_end:]

    def by_row(array):
        return (
            array.astype(jnp.bfloat16)
            .reshape(steps, own_rows, -1, head_dim)
            .transpose(1, 0, 2, 3)
            .reshape(own_rows, -1, head_dim)
        )

    attended = attend(
        by_row(queries),
        cache_keys.reshape(own_rows, -1, head_dim),
        value_cache.reshape(own_rows, -1, head_dim),
        by_row(new_keys),
        by_row(raw_value),
        visible,
        np.arange(steps * heads) // heads,
    )
    attended = (
        attended.reshape(own_rows, steps, query_width)
        .transpose(1, 0, 2)
        .reshape(per_group, query_width)
    )

    with jax.named_scope("gather_z"):
        column = exchange(
            jnp.broadcast_to(attended[None], (depth, per_group, query_width)), "z"
        ).reshape(depth * per_group, query_width)
    with jax.named_scope("gather_plane"):
        piece_rows = exchange(
            jnp.broadcast_to(column[None], (planes, depth * per_group, query_width)), PLANE
        ).reshape(every_row, query_width)

    mixed = output(
        piece_rows, w_output, adapter_attn, adapter_out, tasks, moves, own_rows, steps
    )
    with jax.named_scope("sum_core"):
        both = lax.all_gather(mixed, "core", axis=0)
    half = every_row // 2
    both = jnp.where(first_core, both[:, :half], both[:, half:])
    total = both[0].astype(jnp.float32) + both[1].astype(jnp.float32)
    for pairs in ([[0, 1], [2, 3]], [[1, 2], [3, 0]]):
        with jax.named_scope("sum_y_hi"):
            both = lax.all_gather(
                total.astype(jnp.bfloat16), "y_hi", axis=0, axis_index_groups=pairs
            )
        total = both[0].astype(jnp.float32) + both[1].astype(jnp.float32)
    total, residual = lax.optimization_barrier((total, inputs.reshape(every_row, width_part)))
    residual = jnp.where(first_core, residual[:half], residual[half:])
    finished = (residual.astype(jnp.float32) + total).astype(jnp.bfloat16)
    with jax.named_scope("gather_core"):
        finished = lax.all_gather(finished, "core", axis=0, tiled=True)
    return finished.reshape(inputs.shape)


def solution(mesh):
    parts = Mesh(mesh.devices.reshape(4, 2, 8, 4, 2), GROUP + TENSOR)
    return jax.shard_map(
        on_device,
        mesh=parts,
        in_specs=(
            P(None, None, GROUP),
            P(GROUP),
            P(GROUP, TENSOR),
            P(GROUP, TENSOR),
            P(GROUP, TENSOR),
            P(TENSOR, GROUP),
            P(None, GROUP, None),
            P(None, TENSOR, None),
            P(None, None, GROUP),
            P(GROUP, None, TENSOR),
            P(GROUP, None, None, TENSOR),
            P(GROUP, TENSOR, None, None),
            P(GROUP, TENSOR, None, None),
            P(),
            P(),
            P(),
            P(GROUP),
        ),
        out_specs=P(None, None, GROUP),
        check_vma=False,
    )
```
